32 devices in a mesh: rep: 8 (over z, core), shard: 4 (over y, x).
Axes of the slice: x: 2, y: 2, z: 4, core: 2. Of those that a mesh axis runs over, the one named last changes fastest.
Arguments:
- hidden_in: bfloat16 [32768, 1024], P(('rep', 'shard')), may hold values from -6 to 6
- cotangent: bfloat16 [32768, 1024], P(('rep', 'shard')), may hold values from -6 to 6
- lengths: int32 [32], P(('rep', 'shard')), may hold values from 64 to 1024, as said below
- weights: bfloat16 [1024, 12288], P('shard'), may hold values from -3 to 3
- moment_m: float32 [1024, 12288], P('shard'), may hold values from -60 to 60
- moment_v: float32 [1024, 12288], P('shard'), may hold values from 30 to 10000
- vectors: float32 [7168], replicated, may hold values from -2 to 2
- vector_m: float32 [7168], replicated, may hold values from -30 to 30
- vector_v: float32 [7168], replicated, may hold values from 10 to 10000
Outputs:
- hidden_out: bfloat16 [32768, 1024], P(('rep', 'shard'))
- grad_in: bfloat16 [32768, 1024], P(('rep', 'shard'))
- weight_grad: float32 [1024, 12288], P('shard')
- new_m: float32 [1024, 12288], P('shard')
- new_v: float32 [1024, 12288], P('shard')
- weight_update: float32 [1024, 12288], P('shard')
- vector_grad: float32 [7168], replicated
- vector_new_m: float32 [7168], replicated
- vector_new_v: float32 [7168], replicated
- vector_update: float32 [7168], replicated
The draws below stay inside these ranges and needn't reach their ends.
Inputs may be any that keep to these rules, and one draw needn't show every extreme that they name: `lengths`: some sequence slot is full, of length 1024.
All inputs are finite; a program needn't handle non-finite values.
Results may differ from the reference program's by a relative error of at most 0.018.
Values may be sent and summed in bfloat16 or wider, within the bound.
No kernel may reach another device: no remote copies, remote signals or barrier semaphores. Data moves between devices by JAX's collectives and lax.ppermute only.
A program may use at most 512 MiB of HBM per device.

```python
import math
import jax
import jax.numpy as jnp
from jax import lax

D = 1024
HEADS = 16
HEAD_DIM = 64
ROT = 32
FF = 4096
SEQ_LEN = 1024
STEP = 10
SEQS = 32
TOKENS = 32768
WCOLS = 12288
VECS = 7168


def draw_lengths(key, part):
    key_a, key_b = jax.random.split(key)
    shortest = max(1, SEQ_LEN // 16)
    drawn = jax.random.randint(key_a, (SEQS,), shortest, SEQ_LEN + 1)
    position = jax.random.randint(key_b, (), 0, SEQS)
    return drawn.at[position].set(SEQ_LEN).astype(jnp.int32)


def draw_weights(key, part):
    normal_z = jnp.clip(jax.random.normal(key, (D, WCOLS), jnp.float32), -6.0, 6.0)
    columns = jnp.arange(WCOLS)
    factor = jnp.where(columns < 3 * D, D ** (-0.5), jnp.where(columns < 4 * D, 4.0 * D ** (-0.5), jnp.where(columns < 4 * D + FF, D ** (-0.5), FF ** (-0.5))))
    return (normal_z * factor[None, :]).astype(jnp.bfloat16)


def draw_vectors(key, part):
    normal_z = jnp.clip(jax.random.normal(key, (VECS,), jnp.float32), -4.0, 4.0)
    columns = jnp.arange(VECS)
    return jnp.where(columns < D, 1.0 + 0.2 * normal_z, 0.5 * normal_z)


def block_scale(own_key, extent, shards, smallest, top_value):
    level = 1.0
    for axis_at, parts in shards:
        steps = jax.random.uniform(jax.random.fold_in(jax.random.fold_in(own_key, 6), axis_at), (parts,), jnp.float32, smallest / len(shards), top_value / len(shards))
        level = level * jnp.repeat(jnp.exp(steps), extent[axis_at] // parts).reshape((-1,) + (1,) * (len(extent) - 1 - axis_at))
    return level


def normal_values(stream_key, dims, scale, bound, shards=(), kind=jnp.bfloat16):
    result = jax.random.normal(stream_key, dims, jnp.float32) * scale
    if len(shards) > 0:
        result = block_scale(stream_key, dims, shards, -0.22, 0.18) * result
    return jnp.clip(result, min=-bound, max=bound).astype(kind)


def setup_inputs(seed: int = 0) -> dict:
    keys = jax.random.split(jax.random.key(seed), 10)
    hidden_in = normal_values(keys[0], (TOKENS, D), 1.0, 6.0, ((0, 32),))
    cotangent = normal_values(keys[1], (TOKENS, D), 1.0, 6.0, ((0, 32),))
    lengths = draw_lengths(jax.random.fold_in(keys[9], 71), 0)
    weights = draw_weights(jax.random.fold_in(keys[9], 71), 0)
    moment_m = normal_values(keys[4], (D, WCOLS), 10.0, 60.0, ((0, 4),), jnp.float32)
    moment_v = jnp.clip(jnp.exp(math.log(10000.0) - 5.809143 * jax.random.uniform(keys[5], (D, WCOLS), jnp.float32) ** block_scale(keys[5], (D, WCOLS), ((0, 4),), -0.2, 0.2)), 30.0, 10000.0)
    vectors = draw_vectors(jax.random.fold_in(keys[9], 71), 0)
    vector_m = normal_values(keys[7], (VECS,), 5.0, 30.0, (), jnp.float32)
    vector_v = jnp.clip(jnp.exp(jax.random.uniform(keys[8], (VECS,), jnp.float32, math.log(10.0), math.log(10000.0))), 10.0, 10000.0)
    return {"hidden_in": hidden_in, "cotangent": cotangent, "lengths": lengths, "weights": weights, "moment_m": moment_m, "moment_v": moment_v, "vectors": vectors, "vector_m": vector_m, "vector_v": vector_v}


@jax.custom_vjp
def reduced_precision(v):
    return lax.optimization_barrier(v.astype(jnp.bfloat16)).astype(jnp.float32)

@jax.custom_vjp
def low_back(v):
    return v

def low_keep(v):
    return (reduced_precision(v), None)

def low_pass(kept, grad):
    return (grad,)

def back_keep(v):
    return (v, None)

def back_low(kept, grad):
    return (reduced_precision(grad),)
reduced_precision.defvjp(low_keep, low_pass)
low_back.defvjp(back_keep, back_low)
beta_one = 0.9
beta_two = 0.95
learn_rate = 0.02
decay_rate = 0.1
adam_eps = 1e-08
norm_epsilon = 1e-05

def rotary_tables(seq_len):
    inv_freq = jnp.power(jnp.float32(10000.0), -jnp.arange(0, ROT, 2, dtype=jnp.float32) / ROT)
    angles = jnp.arange(seq_len, dtype=jnp.float32)[:, None] * inv_freq[None, :]
    return (jnp.cos(angles), jnp.sin(angles))

def rotate(tensor, cos_table, sin_table):
    half_rot = ROT // 2
    cos_part = cos_table[:, None, :]
    sin_part = sin_table[:, None, :]
    first_half = tensor[..., :half_rot]
    second_half = tensor[..., half_rot:ROT]
    return jnp.concatenate([first_half * cos_part - second_half * sin_part, second_half * cos_part + first_half * sin_part, tensor[..., ROT:]], -1)

def layer(resid, weight_mat, vector_f32, length):
    high = lax.Precision.HIGHEST
    norm_scale_factor = vector_f32[:D]
    norm_offset = vector_f32[D:2 * D]
    out_bias = vector_f32[2 * D:3 * D]
    in_bias = vector_f32[3 * D:]
    row_mean = lax.optimization_barrier(jnp.mean(resid, -1, keepdims=True))
    centered_rows = resid - row_mean
    row_variance = lax.optimization_barrier(jnp.mean(centered_rows * centered_rows, -1, keepdims=True))
    standardized_input = centered_rows * lax.rsqrt(row_variance + norm_epsilon)
    normalized_input = reduced_precision(standardized_input * norm_scale_factor + norm_offset)
    projected = low_back(jnp.dot(normalized_input, weight_mat[:, :3 * D], precision=high))
    projected = projected.reshape(SEQ_LEN, 3, HEADS, HEAD_DIM)
    cos_table, sin_table = rotary_tables(SEQ_LEN)
    queries = reduced_precision(rotate(projected[:, 0], cos_table, sin_table))
    keys_rot = reduced_precision(rotate(projected[:, 1], cos_table, sin_table))
    values = reduced_precision(projected[:, 2])
    scores = low_back(jnp.einsum('qhd,khd->hqk', queries, keys_rot, precision=high) * HEAD_DIM ** (-0.5))
    key_pos = jnp.arange(SEQ_LEN)
    allowed = (key_pos[None, :] <= key_pos[:, None]) & (key_pos[None, :] < length)
    attn_prob = reduced_precision(jax.nn.softmax(jnp.where(allowed[None], scores, -1e+30), axis=-1))
    attn_o = jnp.einsum('hqk,khd->qhd', attn_prob, values, precision=high).reshape(SEQ_LEN, D)
    attn_o = reduced_precision(low_back(attn_o))
    attn_out = jnp.dot(attn_o, weight_mat[:, 3 * D:4 * D], precision=high)
    preact = low_back(jnp.dot(normalized_input, weight_mat[:, 4 * D:4 * D + FF], precision=high) + in_bias)
    hidden = reduced_precision(jax.nn.gelu(preact, approximate=True))
    mlp_out = jnp.dot(hidden, weight_mat[:, 4 * D + FF:].T, precision=high) + out_bias
    valid_rows = (key_pos < length).astype(jnp.float32)[:, None]
    return valid_rows * (resid + attn_out + mlp_out)

def adamw(gradient, first_m, second_v, current, decay, step_count):
    corr_one = 1.0 - jnp.power(jnp.float32(beta_one), step_count)
    corr_two = 1.0 - jnp.power(jnp.float32(beta_two), step_count)
    new_first = beta_one * first_m + (1.0 - beta_one) * gradient
    new_second = beta_two * second_v + (1.0 - beta_two) * gradient * gradient
    change = -learn_rate * (new_first / corr_one / (jnp.sqrt(new_second / corr_two) + adam_eps) + decay * current)
    return (new_first, new_second, change)

def reference(hidden_in, cotangent, lengths, weights, moment_m, moment_v, vectors, vector_m, vector_v):
    seq_count = lengths.shape[0]
    group_size = math.gcd(seq_count, max(1, 4096 // SEQ_LEN))
    groups = seq_count // group_size
    inputs_f32 = hidden_in.astype(jnp.float32).reshape(groups, group_size, SEQ_LEN, D)
    cot_f32 = cotangent.astype(jnp.float32).reshape(groups, group_size, SEQ_LEN, D)
    length_groups = lengths.astype(jnp.int32).reshape(groups, group_size)
    weight_f32 = weights.astype(jnp.float32)

    def forward(inputs_all, weight_mat, vector_f32):

        def group_step(carried, inputs):
            group_x, group_len = inputs
            return (carried, jax.vmap(lambda seq_input, seq_length: layer(seq_input, weight_mat, vector_f32, seq_length))(group_x, group_len))
        _, outputs = lax.scan(jax.checkpoint(group_step), jnp.float32(0.0), (inputs_all, length_groups))
        return outputs
    outputs, pullback = jax.vjp(forward, inputs_f32, weight_f32, vectors)
    grad_x, grad_w, grad_vec = pullback(cot_f32)
    step_count = jnp.float32(STEP)
    new_m, new_v, weight_update = adamw(grad_w, moment_m, moment_v, weight_f32, decay_rate, step_count)
    vec_m, vec_v, vec_update = adamw(grad_vec, vector_m, vector_v, vectors, 0.0, step_count)
    hidden_out = outputs.reshape(seq_count * SEQ_LEN, D).astype(jnp.bfloat16)
    grad_in = grad_x.reshape(seq_count * SEQ_LEN, D).astype(jnp.bfloat16)
    return (hidden_out, grad_in, grad_w, new_m, new_v, weight_update, grad_vec, vec_m, vec_v, vec_update)
```

```python
import functools

import jax
import jax.numpy as jnp
import numpy as np
from jax import lax
from jax.experimental import pallas as pl
from jax.experimental.pallas import tpu as pltpu
from jax.sharding import PartitionSpec as P

D = 1024
HEADS = 16
HEAD_DIM = 64
ROT = 32
FF = 4096
T = 1024
STEP = 10

B1 = 0.9
B2 = 0.95
LR = 0.02
DECAY = 0.1
ADAM_EPS = 1e-08
NORM_EPS = 1e-05
GC = 0.7978845608028654
GA = 0.044715
LOG2E = 1.4426950408889634
LN2 = 0.6931471805599453

BF = jnp.bfloat16
F32 = jnp.float32
VLIM = 58 * 1024 * 1024
NN = (((1,), (0,)), ((), ()))
NT = (((1,), (1,)), ((), ()))
TN = (((0,), (0,)), ((), ()))
TT = (((0,), (1,)), ((), ()))
TILE = 512
SIZES = (1536, 1536, 1024)
MB = 1024
TB = 256


def mm(a, b, dims=NN):
    return lax.dot_general(a, b, dims, preferred_element_type=F32)


def params():
    return pltpu.CompilerParams(
        dimension_semantics=("arbitrary",), vmem_limit_bytes=VLIM
    )


def once(shape):
    return pl.BlockSpec(shape, lambda *_: (0,) * len(shape), pipeline_mode=pl.Buffered(1))


def cost(flops, nbytes, trans=0):
    return pl.CostEstimate(
        flops=int(flops), bytes_accessed=int(nbytes), transcendentals=int(trans)
    )


def prep_kernel(hr, blocks, ids, x_ref, c_ref, g_ref, b_ref, n_ref, nt_ref, d_ref, dt_ref, db_ref, s_ref):
    i = pl.program_id(0)
    x = x_ref[...].astype(F32)
    mean = jnp.mean(x, -1, keepdims=True)
    xc = x - mean
    var = jnp.mean(xc * xc, -1, keepdims=True)
    n = xc * lax.rsqrt(var + NORM_EPS) * g_ref[...] + b_ref[...]
    n_ref[...] = n.astype(BF)
    row = i * TB + lax.broadcasted_iota(jnp.int32, (TB, 1), 0)
    dy = jnp.where(row < ids[0], c_ref[...].astype(F32), 0.0)
    d_ref[...] = dy.astype(BF)

    @pl.when(i == 0)
    def _():
        db_ref[...] = jnp.zeros_like(db_ref)

    db_ref[...] += jnp.sum(dy, 0, keepdims=True)
    for val, out in ((n, nt_ref), (dy, dt_ref)):
        s_ref[...] = val.T.astype(BF)
        for b in range(2 * blocks):
            off = pl.multiple_of(ids[1 + b], hr)
            out[b * hr : (b + 1) * hr, :] = s_ref[pl.ds(off, hr), :]


def prep(ids, x, cot, gain, shift, hr, blocks):
    row = lambda i, *_: (i, 0)
    col = lambda i, *_: (0, i)
    fix = lambda i, *_: (0, 0)
    return pl.pallas_call(
        functools.partial(prep_kernel, hr, blocks),
        grid_spec=pltpu.PrefetchScalarGridSpec(
            num_scalar_prefetch=1,
            grid=(T // TB,),
            in_specs=[
                pl.BlockSpec((TB, D), row),
                pl.BlockSpec((TB, D), row),
                pl.BlockSpec((1, D), fix),
                pl.BlockSpec((1, D), fix),
            ],
            out_specs=[
                pl.BlockSpec((TB, D), row),
                pl.BlockSpec((D, TB), col),
                pl.BlockSpec((TB, D), row),
                pl.BlockSpec((D, TB), col),
                pl.BlockSpec((1, D), fix),
            ],
            scratch_shapes=[pltpu.VMEM((D, TB), BF)],
        ),
        out_shape=[
            jax.ShapeDtypeStruct((T, D), BF),
            jax.ShapeDtypeStruct((D, T), BF),
            jax.ShapeDtypeStruct((T, D), BF),
            jax.ShapeDtypeStruct((D, T), BF),
            jax.ShapeDtypeStruct((1, D), F32),
        ],
        compiler_params=params(),
        cost_estimate=cost(T * D * 20, T * D * 12),
    )(ids, x, cot, gain, shift)


def place(dst, srcs, ids, base):
    for k, src in enumerate(srcs):
        rows = src.shape[0]
        dst[pl.ds(pl.multiple_of(ids[base + k], rows), rows), :] = src[...]


def mlp_kernel(np_, first, ids, n_ref, nt_ref, d_ref, dt_ref, b_ref, *refs):
    win = refs[:np_]
    wout = refs[np_ : 2 * np_]
    refs = refs[2 * np_ :]
    if not first:
        oin, gin = refs[:2]
        refs = refs[2:]
    gm_ref, gt_ref, db_ref, o_ref, g_ref, wi, wo, h_s, p_s = refs
    j = pl.program_id(0)
    place(wi, win, ids, 0)
    place(wo, wout, ids, 0)
    bias = b_ref[...]
    wi_v = wi[...]
    wo_v = wo[...]
    db = jnp.zeros((1, TILE), F32)
    for t in range(T // MB):
        rows = slice(t * MB, (t + 1) * MB)
        pre = mm(n_ref[rows, :], wi_v) + bias
        dh = mm(d_ref[rows, :], wo_v)
        sq = pre * pre
        th = jnp.tanh(GC * pre * (1.0 + GA * sq))
        half = 0.5 * (1.0 + th)
        h = (pre * half).astype(BF)
        slope = half + 0.5 * pre * (1.0 - th * th) * (GC + (3.0 * GA * GC) * sq)
        dp = (dh * slope).astype(BF)
        h_s[rows, :] = h
        p_s[rows, :] = dp
        db = db + jnp.sum(dp.astype(F32), 0, keepdims=True)
        ov = mm(h, wo_v, NT)
        gv = mm(wi_v, dp, NT)

        if first:

            @pl.when(j == 0)
            def _():
                o_ref[rows, :] = ov
                g_ref[:, rows] = gv

        else:

            @pl.when(j == 0)
            def _():
                o_ref[rows, :] = oin[rows, :] + ov
                g_ref[:, rows] = gin[:, rows] + gv

        @pl.when(j > 0)
        def _():
            o_ref[rows, :] += ov
            g_ref[:, rows] += gv

    db_ref[...] = db
    hv = h_s[...]
    pv = p_s[...]
    half_d = D // 2
    gt_ref[1] = mm(dt_ref[half_d:, :], hv).astype(BF)
    gt_ref[0] = mm(nt_ref[half_d:, :], pv).astype(BF)
    gm_ref[1] = mm(dt_ref[:half_d, :], hv).astype(BF)
    gm_ref[0] = mm(nt_ref[:half_d, :], pv).astype(BF)


def mlp(ids, n, nt, dy, dyt, bias, weights, pieces, offset, size, acc):
    first = acc is None
    nt_cols = size // TILE
    tall = lambda cols: pl.BlockSpec((T, cols), lambda j, *_: (0, 0))
    own_rows = weights.shape[0]
    in_base = (4 * D + offset) // TILE
    out_base = (4 * D + FF + offset) // TILE
    wspecs = []
    for base_own, base in ((in_base, offset // TILE), (out_base, (FF + offset) // TILE)):
        if own_rows:
            wspecs.append(pl.BlockSpec((own_rows, TILE), lambda j, *_, b=base_own: (0, b + j)))
        for p in pieces:
            wspecs.append(pl.BlockSpec((p.shape[0], TILE), lambda j, *_, b=base: (0, b + j)))
    wargs = [weights, *pieces]
    bb = offset // TILE
    gspec = pl.BlockSpec((2, D // 2, TILE), lambda j, *_: (0, 0, j))
    gshape = jax.ShapeDtypeStruct((2, D // 2, size), BF)
    return pl.pallas_call(
        functools.partial(mlp_kernel, len(wargs), first),
        grid_spec=pltpu.PrefetchScalarGridSpec(
            num_scalar_prefetch=1,
            grid=(nt_cols,),
            in_specs=[
                once((T, D)),
                once((D, T)),
                once((T, D)),
                once((D, T)),
                pl.BlockSpec((1, TILE), lambda j, *_: (0, bb + j)),
                *wspecs,
                *([] if first else [once((T, D)), once((D, T))]),
            ],
            out_specs=[
                gspec,
                gspec,
                pl.BlockSpec((1, TILE), lambda j, *_: (0, j)),
                once((T, D)),
                once((D, T)),
            ],
            scratch_shapes=[
                pltpu.VMEM((D, TILE), BF),
                pltpu.VMEM((D, TILE), BF),
                pltpu.VMEM((T, TILE), BF),
                pltpu.VMEM((T, TILE), BF),
            ],
        ),
        out_shape=[
            gshape,
            gshape,
            jax.ShapeDtypeStruct((1, size), F32),
            jax.ShapeDtypeStruct((T, D), F32),
            jax.ShapeDtypeStruct((D, T), F32),
        ],
        compiler_params=params(),
        cost_estimate=cost(12 * T * D * size, 8 * D * size + 24 * T * D, T * size),
    )(ids, n, nt, dy, dyt, bias, *wargs, *wargs, *([] if first else acc))


def proj_kernel(np_, ids, n_ref, d_ref, cos_ref, sin_ref, *refs):
    wq = refs[:np_]
    wo = refs[np_ : 2 * np_]
    out_ref, dout_ref, w_s, wo_s = refs[2 * np_ :]
    j = pl.program_id(0)
    place(w_s, wq, ids, 0)
    r = mm(w_s[...], n_ref[...], TT)

    def rotated(scale):
        for h in range(TB // HEAD_DIM):
            b = h * HEAD_DIM
            u = r[b : b + 16, :]
            w = r[b + 16 : b + 32, :]
            cs = cos_ref[...]
            sn = sin_ref[...]
            turned = [u * cs - w * sn, w * cs + u * sn, r[b + 32 : b + 64, :]]
            out_ref[b : b + 64, :] = (jnp.concatenate(turned, 0) * scale).astype(BF)

    @pl.when(j < 4)
    def _():
        rotated(LOG2E * HEAD_DIM ** (-0.5))

    @pl.when((j >= 4) & (j < 8))
    def _():
        rotated(1.0)

    @pl.when(j >= 8)
    def _():
        out_ref[...] = r.astype(BF)

    @pl.when(j == 0)
    def _():
        place(wo_s, wo, ids, 0)
        for t in range(D // TB):
            rows = slice(t * TB, (t + 1) * TB)
            dout_ref[rows, :] = mm(wo_s[rows, :], d_ref[...], NT).astype(BF)


def proj(ids, n, dy, cos, sin, weights, pieces):
    wargs = [weights, *pieces]
    return pl.pallas_call(
        functools.partial(proj_kernel, len(wargs)),
        grid_spec=pltpu.PrefetchScalarGridSpec(
            num_scalar_prefetch=1,
            grid=(3 * D // TB,),
            in_specs=[
                once((T, D)),
                once((T, D)),
                once((16, T)),
                once((16, T)),
                *[pl.BlockSpec((w.shape[0], TB), lambda j, *_: (0, j)) for w in wargs],
                *[
                    pl.BlockSpec((w.shape[0], D), lambda j, *_: (0, 3), pipeline_mode=pl.Buffered(1))
                    for w in wargs
                ],
            ],
            out_specs=[
                pl.BlockSpec((TB, T), lambda j, *_: (j, 0)),
                once((D, T)),
            ],
            scratch_shapes=[pltpu.VMEM((D, TB), BF), pltpu.VMEM((D, D), BF)],
        ),
        out_shape=[
            jax.ShapeDtypeStruct((3 * D, T), BF),
            jax.ShapeDtypeStruct((D, T), BF),
        ],
        compiler_params=params(),
        cost_estimate=cost(8 * T * D * D, 20 * T * D),
    )(ids, n, dy, cos, sin, *wargs, *wargs)


QB = 512
HPS = 2


def attn_kernel(n_alias, len_ref, q_ref, k_ref, v_ref, do_ref, cos_ref, sin_ref, *refs):
    o_ref, dq_ref, dk_ref, dv_ref = refs[n_alias:]
    sub = lax.broadcasted_iota(jnp.int32, (HEAD_DIM, T), 0)
    lane = lax.broadcasted_iota(jnp.int32, (HEAD_DIM, T), 1)
    bias = jnp.where((sub == 0) & (lane >= len_ref[0]), -1e30, 0.0)
    ones = jnp.where(sub == 0, 1.0, 0.0).astype(BF)
    none = jnp.zeros((HEAD_DIM, T), F32)
    ki = lax.broadcasted_iota(jnp.int32, (QB, QB), 0)
    qi = lax.broadcasted_iota(jnp.int32, (QB, QB), 1)

    def unrot(val, cs, sn, out, base, cols):
        a = val[0:16, :]
        b = val[16:32, :]
        turned = [a * cs + b * sn, b * cs - a * sn, val[32:64, :]]
        out[base : base + 64, cols] = jnp.concatenate(turned, 0).astype(BF)

    for h in range(HPS):
        b = h * HEAD_DIM
        hs = slice(b, b + HEAD_DIM)
        q = q_ref[hs, :]
        k = k_ref[hs, :]
        v = v_ref[hs, :]
        qa = jnp.concatenate([q, ones], 0)
        ka = jnp.concatenate([k.astype(F32), bias], 0).T.astype(BF)
        vt = jnp.concatenate([v.astype(F32), none], 0).T.astype(BF)
        dk = [jnp.zeros((HEAD_DIM, QB), F32) for _ in range(T // QB)]
        dv = [jnp.zeros((HEAD_DIM, QB), F32) for _ in range(T // QB)]
        for i in range(T // QB):
            qs = slice(i * QB, (i + 1) * QB)
            kk = (i + 1) * QB
            st = mm(ka[:kk, :], qa[:, qs])
            diag = jnp.where(ki <= qi, st[kk - QB :, :], -1e30)
            st = diag if i == 0 else jnp.concatenate([st[: kk - QB, :], diag], 0)
            e = jnp.exp2(st - jnp.max(st, 0, keepdims=True))
            rl = 1.0 / jnp.sum(e, 0, keepdims=True)
            eb = e.astype(BF)
            ot = mm(v[:, :kk], eb) * rl
            o_ref[hs, qs] = ot.astype(BF)
            dn = (do_ref[hs, qs].astype(F32) * rl).astype(BF)
            delta = jnp.sum(dn.astype(F32) * ot, 0, keepdims=True)
            da = jnp.concatenate([dn, none[:, qs].astype(BF)], 0)
            ds = (e * (mm(vt[:kk, :], da) - delta)).astype(BF)
            dq = mm(k[:, :kk], ds) * (HEAD_DIM ** (-0.5))
            unrot(dq, cos_ref[:, qs], sin_ref[:, qs], dq_ref, b, qs)
            dvi = mm(dn, eb, NT)
            dki = mm(q[:, qs], ds, NT)
            for t in range(i + 1):
                ts = slice(t * QB, (t + 1) * QB)
                dv[t] = dv[t] + dvi[:, ts]
                dk[t] = dk[t] + dki[:, ts]
        for t in range(T // QB):
            ts = slice(t * QB, (t + 1) * QB)
            dv_ref[hs, ts] = dv[t].astype(BF)
            unrot(dk[t] * LN2, cos_ref[:, ts], sin_ref[:, ts], dk_ref, b, ts)


def attend(length, qkv, dot_, cos, sin, first, heads, before):
    rows = HPS * HEAD_DIM
    steps = HEADS // HPS
    at = first // HPS
    spec = lambda base: pl.BlockSpec((rows, T), lambda h, *_: (base + at + h, 0))
    shape = jax.ShapeDtypeStruct((D, T), BF)
    alias = [] if before is None else list(before)
    return pl.pallas_call(
        functools.partial(attn_kernel, len(alias)),
        grid_spec=pltpu.PrefetchScalarGridSpec(
            num_scalar_prefetch=1,
            grid=(heads // HPS,),
            in_specs=[
                spec(0),
                spec(steps),
                spec(2 * steps),
                spec(0),
                once((16, T)),
                once((16, T)),
            ]
            + [pl.BlockSpec(memory_space=pl.ANY)] * len(alias),
            out_specs=[spec(0)] * 4,
        ),
        out_shape=[shape] * 4,
        input_output_aliases={7 + i: i for i in range(len(alias))},
        compiler_params=params(),
        cost_estimate=cost(12 * T * T * D, 18 * T * D, T * T * HEADS // 2),
    )(length, qkv, qkv, qkv, dot_, cos, sin, *alias)


def agrad_kernel(hr, order, blocks, ids, nt_ref, dy_ref, o_ref, dq_ref, dk_ref, dv_ref, m_ref, t_ref, g_s):
    j = pl.program_id(0)
    half_d = D // 2
    for at, src in enumerate((dq_ref, dk_ref, dv_ref)):

        @pl.when((j >= 2 * at) & (j < 2 * at + 2))
        def _(src=src):
            val = src[...]
            for out, first in ((m_ref, 0), (t_ref, half_d)):
                g = mm(nt_ref[first : first + half_d, :], val, NT).astype(BF)
                for b in range(blocks):
                    k = order[b]
                    out[0, b * hr : (b + 1) * hr, :] = g[k * hr : (k + 1) * hr, :]

    @pl.when(j >= 6)
    def _():
        g_s[...] = mm(o_ref[...], dy_ref[...]).astype(BF)
        for b in range(blocks):
            m_ref[0, b * hr : (b + 1) * hr, :] = g_s[pl.ds(pl.multiple_of(ids[b], hr), hr), :]
            t_ref[0, b * hr : (b + 1) * hr, :] = g_s[pl.ds(pl.multiple_of(ids[blocks + b], hr), hr), :]


def attn_grads(ids, nt, dy, ot, dq, dk, dv, hr, order):
    blocks = len(order)

    def grab(at):
        return pl.BlockSpec((TILE, T), lambda j, *_: (jnp.clip(j - 2 * at, 0, 1), 0))

    gspec = pl.BlockSpec((1, D // 2, TILE), lambda j, *_: (j // 4, 0, j % 4))
    gshape = jax.ShapeDtypeStruct((2, D // 2, 2 * D), BF)
    return pl.pallas_call(
        functools.partial(agrad_kernel, hr, order, blocks),
        grid_spec=pltpu.PrefetchScalarGridSpec(
            num_scalar_prefetch=1,
            grid=(4 * D // TILE,),
            in_specs=[
                once((D, T)),
                pl.BlockSpec((T, TILE), lambda j, *_: (0, jnp.clip(j - 6, 0, 1))),
                once((D, T)),
                grab(0),
                grab(1),
                grab(2),
            ],
            out_specs=[gspec, gspec],
            scratch_shapes=[pltpu.VMEM((D, TILE), BF)],
        ),
        out_shape=[gshape] * 2,
        compiler_params=params(),
        cost_estimate=cost(8 * T * D * D, 20 * T * D),
    )(ids, nt, dy, ot, dq, dk, dv)


def final_kernel(np_, ids, x_ref, dy_ref, g_ref, bo_ref, o_ref, dq_ref, dk_ref, dv_ref, ao_ref, ag_ref, *refs):
    wq = refs[:np_]
    out_ref, gin_ref, v_ref, w_s = refs[np_:]
    i = pl.program_id(0)

    @pl.when(i == 0)
    def _():
        place(w_s, wq, ids, 1)

    x = x_ref[...].astype(F32)
    row = i * TB + lax.broadcasted_iota(jnp.int32, (TB, 1), 0)
    attn = mm(o_ref[...], w_s[:, 3 * D :], TN)
    out = x + attn + ao_ref[...] + bo_ref[...]
    out_ref[...] = jnp.where(row < ids[0], out, 0.0).astype(BF)
    dn = (
        ag_ref[...]
        + mm(w_s[:, :D], dq_ref[...])
        + mm(w_s[:, D : 2 * D], dk_ref[...])
        + mm(w_s[:, 2 * D : 3 * D], dv_ref[...])
    ).T
    mean = jnp.mean(x, -1, keepdims=True)
    xc = x - mean
    inv = lax.rsqrt(jnp.mean(xc * xc, -1, keepdims=True) + NORM_EPS)
    xh = xc * inv
    g = dn * g_ref[...]
    gx = dn * xh
    ln = inv * (
        g - jnp.mean(g, -1, keepdims=True) - xh * jnp.mean(g * xh, -1, keepdims=True)
    )
    gin_ref[...] = (dy_ref[...].astype(F32) + ln).astype(BF)

    @pl.when(i == 0)
    def _():
        v_ref[...] = jnp.zeros_like(v_ref)

    v_ref[0:1, :] += jnp.sum(gx, 0, keepdims=True)
    v_ref[1:2, :] += jnp.sum(dn, 0, keepdims=True)


def final(ids, x, dy, gain, b_out, ot, dq, dk, dv, acc_o, acc_g, weights, pieces):
    row = pl.BlockSpec((TB, D), lambda i, *_: (i, 0))
    col = pl.BlockSpec((D, TB), lambda i, *_: (0, i))
    vec = pl.BlockSpec((1, D), lambda i, *_: (0, 0))
    wargs = [weights, *pieces]
    return pl.pallas_call(
        functools.partial(final_kernel, len(wargs)),
        grid_spec=pltpu.PrefetchScalarGridSpec(
            num_scalar_prefetch=1,
            grid=(T // TB,),
            in_specs=[
                row,
                row,
                vec,
                vec,
                col,
                col,
                col,
                col,
                row,
                col,
                *[once((w.shape[0], 4 * D)) for w in wargs],
            ],
            out_specs=[row, row, pl.BlockSpec((8, D), lambda i, *_: (0, 0))],
            scratch_shapes=[pltpu.VMEM((D, 4 * D), BF)],
        ),
        out_shape=[
            jax.ShapeDtypeStruct((T, D), BF),
            jax.ShapeDtypeStruct((T, D), BF),
            jax.ShapeDtypeStruct((8, D), F32),
        ],
        compiler_params=params(),
        cost_estimate=cost(8 * T * D * D, 40 * T * D),
    )(ids, x, dy, gain, b_out, ot, dq, dk, dv, acc_o, acc_g, *wargs)


C1 = float(1.0 - np.float32(B1) ** np.float32(STEP))
C2 = float(1.0 - np.float32(B2) ** np.float32(STEP))


def adam_math(g, m, v, w, decay):
    nm = B1 * m + (1.0 - B1) * g
    nv = B2 * v + (1.0 - B2) * g * g
    up = -LR * (nm / C1 / (jnp.sqrt(nv / C2) + ADAM_EPS) + decay * w)
    return nm, nv, up


AC = 512


def adam_kernel(n_alias, ids, sm, rm, so, ro, m_ref, v_ref, w_ref, *refs):
    wg_ref, nm_ref, nv_ref, up_ref = refs[n_alias:]
    summed = pl.program_id(0) == ids[1]
    hr = sm.shape[0]
    mine = jnp.where(summed, sm[...].astype(F32), rm[...].astype(F32))
    other = jnp.where(summed, so[...].astype(F32), ro[...].astype(F32))
    lead = ids[0] == 0
    for h, g in enumerate((jnp.where(lead, mine, other), jnp.where(lead, other, mine))):
        rows = slice(h * hr, (h + 1) * hr)
        nm, nv, up = adam_math(g, m_ref[rows, :], v_ref[rows, :], w_ref[rows, :].astype(F32), DECAY)
        wg_ref[rows, :] = g
        nm_ref[rows, :] = nm
        nv_ref[rows, :] = nv
        up_ref[rows, :] = up


def adam(ids, grads, cols, m, v, w, outs):
    rows, width = m.shape
    hr = rows // 2
    n = grads[0].shape[1]
    pick = lambda hit: pl.BlockSpec(
        (hr, AC), lambda p, j, ids: (0, jnp.where((p == ids[1]) == hit, j, 0))
    )
    b0, b1 = cols[0] // AC, cols[1] // AC
    big = pl.BlockSpec((rows, AC), lambda p, j, ids: (0, jnp.where(p == 0, b0, b1) + j))
    alias = [] if outs is None else list(outs)
    return pl.pallas_call(
        functools.partial(adam_kernel, len(alias)),
        grid_spec=pltpu.PrefetchScalarGridSpec(
            num_scalar_prefetch=1,
            grid=(2, n // AC),
            in_specs=[pick(True), pick(False), pick(True), pick(False), big, big, big]
            + [pl.BlockSpec(memory_space=pl.ANY)] * len(alias),
            out_specs=[big] * 4,
        ),
        out_shape=[jax.ShapeDtypeStruct((rows, width), F32)] * 4,
        input_output_aliases={8 + i: i for i in range(len(alias))},
        compiler_params=pltpu.CompilerParams(
            dimension_semantics=("arbitrary", "arbitrary"), vmem_limit_bytes=VLIM
        ),
        cost_estimate=cost(2 * rows * n * 20, 2 * rows * n * 28),
    )(ids, *grads, m, v, w, *alias)


def after(values, *waits):
    flat = lax.optimization_barrier((*values, *waits))
    return list(flat[: len(values)])


def on_device(shards, reps, hidden_in, cotangent, lengths, weights, moment_m, moment_v, vectors, vector_m, vector_v):
    s = lax.axis_index("shard")
    rep = lax.axis_index("rep")
    c = rep % 2
    z = rep // 2
    zs = reps // 2
    swap = [(i, i ^ 1) for i in range(reps)]
    rows = weights.shape[0]
    hr = rows // 2
    i32 = jnp.int32
    cube = shards == 4 and zs & (zs - 1) == 0 and zs >= 4
    xn = [(i, i ^ 1) for i in range(shards)]
    yn = [(i, i ^ 2) for i in range(shards)]
    zsteps = [3] + [1 << k for k in range(2, 16) if 1 << k < zs]
    zn = lambda bit: [(i, i ^ (2 * bit)) for i in range(reps)]
    own = ((z ^ (z // 2)) % 2) if cube else jnp.int32(0)

    if cube:
        x_order, y_order = (1, 3, 0, 2), (2, 3, 0, 1)
        x_rows = [(s ^ r) * rows for r in x_order]
        y_rows = [(s ^ r) * rows for r in y_order]
        y_in_x = tuple(x_order.index(r) for r in y_order)
    else:
        x_rows = y_rows = [r * rows for r in range(shards)]
        y_in_x = tuple(range(shards))
    cut = lambda at: [b + c * hr for b in at] + [b + (1 - c) * hr for b in at]
    x_off, y_off = cut(x_rows), cut(y_rows)
    stack = lambda *v: jnp.stack([jnp.asarray(x, i32) for x in v])
    length = lengths.astype(i32)
    gain = vectors[:D].reshape(1, D)
    shift = vectors[D : 2 * D].reshape(1, D)
    b_out = vectors[2 * D : 3 * D].reshape(1, D)
    b_in = vectors[3 * D :].reshape(1, FF)
    half_w = lax.dynamic_slice_in_dim(weights, c * hr, hr, 0)

    def part_of(cols):
        return jnp.concatenate([half_w[:, a:b] for a, b in cols], 1)

    q = hr // 2

    def gather_first(part):
        return [lax.ppermute(part, "shard", xn), lax.ppermute(part, "shard", yn)]

    def gather_second(first):
        rx, ry = first
        return [lax.ppermute(rx[:q], "shard", yn), lax.ppermute(ry[q:], "shard", xn)]

    def swapped(mine):
        return mine + [lax.ppermute(p, "rep", swap) for p in mine]

    def gather_whole(part):
        full = lax.all_gather(part, "shard", axis=0, tiled=True)
        other = lax.ppermute(full, "rep", swap)
        return [p[b * hr : (b + 1) * hr] for p in (full, other) for b in range(shards)]

    offsets = [0]
    for size in SIZES:
        offsets.append(offsets[-1] + size)
    apart, fpart = part_of([(0, 4 * D)]), part_of([(4 * D, 4 * D + 2 * FF)])
    if cube:
        base = [(s ^ 1) * rows, (s ^ 2) * rows, (s ^ 3) * rows, (s ^ 3) * rows + q]
        offs = [b + c * hr for b in base] + [b + (1 - c) * hr for b in base]
        one = gather_first(apart)
        one = one + gather_second(one)
        (fpart,) = after([fpart], *one)
        apieces = swapped(one)
        two = gather_first(fpart)
    else:
        offs = cut([b * rows for b in range(shards)])
        apieces = gather_whole(apart)
        two = gather_whole(fpart)
    piece_off = stack(s * rows, *offs)
    len_piece_off = stack(length[0], s * rows, *offs)

    n, nt, dy, dyt, db_out = prep(
        stack(length[0], *x_off), hidden_in, cotangent, gain, shift, hr, shards
    )

    add = lambda *v: sum(x.astype(F32) for x in v).astype(BF)

    class Reduce:
        def __init__(self, mine, theirs, y_first=False):
            self.mine, self.theirs = mine, theirs
            self.ways = (yn, xn) if y_first else (xn, yn)
            self.at = 0
            self.sums = None

        def step(self):
            k, self.at = self.at, self.at + 1
            m = self.mine
            if k == 0:
                sent = self.theirs
                self.got = lax.ppermute(sent, "rep", swap)
            elif not cube:
                if k > 1:
                    return []
                groups = [[2 * j + e for j in range(zs)] for e in range(2)]
                both = add(m, self.got)
                both = lax.psum_scatter(both, "shard", scatter_dimension=1, tiled=True)
                both = lax.psum(both, "rep", axis_index_groups=groups)
                self.sums = (both[0], both[1])
                return []
            elif k == 1:
                sent = add(m[:, : 2 * hr], self.got[:, : 2 * hr])
                self.first = lax.ppermute(sent, "shard", self.ways[0])
                return [sent, self.first]
            elif k == 2:
                sent = add(m[:, 3 * hr :], self.got[:, 3 * hr :], self.first[:, hr:])
                self.second = lax.ppermute(sent, "shard", self.ways[1])
                return [sent, self.second]
            elif k == 3:
                total = add(
                    m[:, 2 * hr : 3 * hr], self.got[:, 2 * hr : 3 * hr], self.first[:, :hr], self.second
                )
                lead = own == 0
                sent = jnp.where(lead, total[1], total[0])
                self.keep = jnp.where(lead, total[0], total[1])
                self.back = lax.ppermute(sent, "rep", zn(1))
                return [sent, self.back]
            elif k <= 3 + len(zsteps):
                self.keep = add(self.keep, self.back)
                self.back = lax.ppermute(self.keep, "rep", zn(zsteps[k - 4]))
                return [self.keep, self.back]
            elif k == 4 + len(zsteps):
                self.keep = add(self.keep, self.back)
                self.back = lax.ppermute(self.keep, "rep", zn(1))
                self.sums = (self.keep, self.back)
                return [self.keep, self.back]
            return [self.theirs, self.got]

        def result(self):
            while self.sums is None:
                self.step()
            return [*self.sums, *[lax.ppermute(v, "rep", swap) for v in self.sums]]

    flight = []

    def turn(values, *steps):
        nonlocal flight
        waits = flight
        flight = []
        for red in steps:
            moved = red.step() if red.sums is None else []
            waits = waits + moved[:1]
            flight = flight + moved[1:]
        return after(values, *waits) if waits else list(values)

    inv_freq = jnp.power(F32(10000.0), -jnp.arange(0, ROT, 2, dtype=F32) / ROT)
    angles = inv_freq[:, None] * jnp.arange(T, dtype=F32)[None, :]
    cos, sin = jnp.cos(angles), jnp.sin(angles)
    qkv, dot_ = proj(piece_off, n, dy, cos, sin, weights, apieces)
    half = HEADS // 2
    heads = attend(length, qkv, dot_, cos, sin, 0, half, None)
    if cube:
        (qkv,) = after([qkv], *two, heads[0])
        three = gather_second(two)
        fpieces = swapped(two)
    ot, dq, dk, dv = attend(length, qkv, dot_, cos, sin, half, half, heads)
    dyg = dy
    if cube:
        (dyg,) = after([dy], ot, *three, *fpieces)
        other = swapped(three)
        fpieces = fpieces[:2] + other[:2] + fpieces[2:] + other[2:]
    else:
        fpieces = two
    reds = [Reduce(*attn_grads(stack(*y_off), nt, dyg, ot, dq, dk, dv, hr, y_in_x), True)]
    places = [(0, 2 * D)]
    reds[0].step()

    acc = None
    dbs = []
    nk = n
    for at, size in zip(offsets, SIZES):
        (nk,) = turn([nk], *reds)
        grads_m, grads_t, db_in, *acc = mlp(
            piece_off, nk, nt, dy, dyt, b_in, weights, fpieces, at, size, acc
        )
        dbs.append(db_in)
        reds.append(Reduce(grads_m, grads_t))
        reds[-1].step()
        places.append((4 * D + at, 4 * D + FF + at))

    (ot,) = turn([ot], *reds)
    out, grad_in, vsum = final(
        len_piece_off, hidden_in, dy, gain, b_out, ot, dq, dk, dv, *acc, weights, apieces
    )
    vec = jnp.concatenate([vsum[0], vsum[1], db_out[0], *[d[0] for d in dbs]])
    if cube:
        vec = vec.reshape(-1, 128)
        vec = vec + lax.ppermute(vec, "rep", swap)
        for way in (xn, yn):
            vec = vec + lax.ppermute(vec, "shard", way)
        for bit in [1] + zsteps:
            vec = vec + lax.ppermute(vec, "rep", zn(bit))
        vec = vec.reshape(-1)
    else:
        vec = lax.psum(vec, ("rep", "shard"))
    core = stack(c, own)
    big = None
    turn([], *reds)
    for i, cols in enumerate(places):
        grads = reds[i].result()
        (moment_m,) = turn([moment_m], *reds[i + 1 :])
        big = adam(core, grads, cols, moment_m, moment_v, weights, big)
    vm, vv, vu = adam_math(vec, vector_m, vector_v, vectors, 0.0)
    return (out, grad_in, *big, vec, vm, vv, vu)


def solution(mesh):
    tok = P(("rep", "shard"), None)
    w = P("shard", None)
    return jax.shard_map(
        functools.partial(on_device, mesh.shape["shard"], mesh.shape["rep"]),
        mesh=mesh,
        in_specs=(tok, tok, P(("rep", "shard")), w, w, w, P(), P(), P()),
        out_specs=(tok, tok, w, w, w, w, P(), P(), P(), P()),
        check_vma=False,
    )
```

```python
import functools

import jax
import jax.numpy as jnp
import numpy as np
from jax import lax
from jax.experimental import pallas as pl
from jax.experimental.pallas import tpu as pltpu
from jax.sharding import PartitionSpec as P

D = 1024
HEADS = 16
HEAD_DIM = 64
ROT = 32
FF = 4096
T = 1024
STEP = 10

B1 = 0.9
B2 = 0.95
LR = 0.02
DECAY = 0.1
ADAM_EPS = 1e-08
NORM_EPS = 1e-05
GC = 0.7978845608028654
GA = 0.044715
LOG2E = 1.4426950408889634
LN2 = 0.6931471805599453

BF = jnp.bfloat16
F32 = jnp.float32
VLIM = 58 * 1024 * 1024
NN = (((1,), (0,)), ((), ()))
NT = (((1,), (1,)), ((), ()))
TN = (((0,), (0,)), ((), ()))
TT = (((0,), (1,)), ((), ()))
TILE = 512
SIZES = (2048, 1024, 1024)
MB = 1024
TB = 256


def mm(a, b, dims=NN):
    return lax.dot_general(a, b, dims, preferred_element_type=F32)


def params():
    return pltpu.CompilerParams(
        dimension_semantics=("arbitrary",), vmem_limit_bytes=VLIM
    )


def once(shape):
    return pl.BlockSpec(shape, lambda *_: (0,) * len(shape), pipeline_mode=pl.Buffered(1))


def cost(us):
    return pl.CostEstimate(flops=int(us * 1.15e9), bytes_accessed=1024, transcendentals=0)


def prep_kernel(hr, blocks, ids, x_ref, c_ref, g_ref, b_ref, n_ref, nt_ref, d_ref, dt_ref, db_ref, s_ref):
    i = pl.program_id(0)
    x = x_ref[...].astype(F32)
    mean = jnp.mean(x, -1, keepdims=True)
    xc = x - mean
    var = jnp.mean(xc * xc, -1, keepdims=True)
    n = xc * lax.rsqrt(var + NORM_EPS) * g_ref[...] + b_ref[...]
    n_ref[...] = n.astype(BF)
    row = i * TB + lax.broadcasted_iota(jnp.int32, (TB, 1), 0)
    dy = jnp.where(row < ids[0], c_ref[...].astype(F32), 0.0)
    d_ref[...] = dy.astype(BF)

    @pl.when(i == 0)
    def _():
        db_ref[...] = jnp.zeros_like(db_ref)

    db_ref[...] += jnp.sum(dy, 0, keepdims=True)
    for val, out in ((n, nt_ref), (dy, dt_ref)):
        s_ref[...] = val.T.astype(BF)
        for b in range(2 * blocks):
            off = pl.multiple_of(ids[1 + b], hr)
            out[b * hr : (b + 1) * hr, :] = s_ref[pl.ds(off, hr), :]


def prep(ids, x, cot, gain, shift, hr, blocks):
    row = lambda i, *_: (i, 0)
    col = lambda i, *_: (0, i)
    fix = lambda i, *_: (0, 0)
    return pl.pallas_call(
        functools.partial(prep_kernel, hr, blocks),
        grid_spec=pltpu.PrefetchScalarGridSpec(
            num_scalar_prefetch=1,
            grid=(T // TB,),
            in_specs=[
                pl.BlockSpec((TB, D), row),
                pl.BlockSpec((TB, D), row),
                pl.BlockSpec((1, D), fix),
                pl.BlockSpec((1, D), fix),
            ],
            out_specs=[
                pl.BlockSpec((TB, D), row),
                pl.BlockSpec((D, TB), col),
                pl.BlockSpec((TB, D), row),
                pl.BlockSpec((D, TB), col),
                pl.BlockSpec((1, D), fix),
            ],
            scratch_shapes=[pltpu.VMEM((D, TB), BF)],
        ),
        out_shape=[
            jax.ShapeDtypeStruct((T, D), BF),
            jax.ShapeDtypeStruct((D, T), BF),
            jax.ShapeDtypeStruct((T, D), BF),
            jax.ShapeDtypeStruct((D, T), BF),
            jax.ShapeDtypeStruct((1, D), F32),
        ],
        compiler_params=params(),
        cost_estimate=cost(8),
    )(ids, x, cot, gain, shift)


def place(dst, srcs, ids, base):
    for k, src in enumerate(srcs):
        rows = src.shape[0]
        dst[pl.ds(pl.multiple_of(ids[base + k], rows), rows), :] = src[...]


def mlp_kernel(np_, first, ids, n_ref, nt_ref, d_ref, dt_ref, b_ref, *refs):
    win = refs[:np_]
    wout = refs[np_ : 2 * np_]
    refs = refs[2 * np_ :]
    if not first:
        oin, gin = refs[:2]
        refs = refs[2:]
    gm_ref, gt_ref, db_ref, o_ref, g_ref, wi, wo, h_s, p_s = refs
    j = pl.program_id(0)
    place(wi, win, ids, 0)
    place(wo, wout, ids, 0)
    bias = b_ref[...]
    wi_v = wi[...]
    wo_v = wo[...]
    db = jnp.zeros((1, TILE), F32)
    for t in range(T // MB):
        rows = slice(t * MB, (t + 1) * MB)
        pre = mm(n_ref[rows, :], wi_v) + bias
        dh = mm(d_ref[rows, :], wo_v)
        sq = pre * pre
        th = jnp.tanh(GC * pre * (1.0 + GA * sq))
        half = 0.5 * (1.0 + th)
        h = (pre * half).astype(BF)
        slope = half + 0.5 * pre * (1.0 - th * th) * (GC + (3.0 * GA * GC) * sq)
        dp = (dh * slope).astype(BF)
        h_s[rows, :] = h
        p_s[rows, :] = dp
        db = db + jnp.sum(dp.astype(F32), 0, keepdims=True)
        ov = mm(h, wo_v, NT)
        gv = mm(wi_v, dp, NT)

        if first:

            @pl.when(j == 0)
            def _():
                o_ref[rows, :] = ov
                g_ref[:, rows] = gv

        else:

            @pl.when(j == 0)
            def _():
                o_ref[rows, :] = oin[rows, :] + ov
                g_ref[:, rows] = gin[:, rows] + gv

        @pl.when(j > 0)
        def _():
            o_ref[rows, :] += ov
            g_ref[:, rows] += gv

    db_ref[...] = db
    hv = h_s[...]
    pv = p_s[...]
    half_d = D // 2
    gt_ref[1] = mm(dt_ref[half_d:, :], hv).astype(BF)
    gt_ref[0] = mm(nt_ref[half_d:, :], pv).astype(BF)
    gm_ref[1] = mm(dt_ref[:half_d, :], hv).astype(BF)
    gm_ref[0] = mm(nt_ref[:half_d, :], pv).astype(BF)


def mlp(ids, n, nt, dy, dyt, bias, weights, pieces, offset, size, acc):
    first = acc is None
    nt_cols = size // TILE
    tall = lambda cols: pl.BlockSpec((T, cols), lambda j, *_: (0, 0))
    own_rows = weights.shape[0]
    in_base = (4 * D + offset) // TILE
    out_base = (4 * D + FF + offset) // TILE
    wspecs = []
    for base_own, base in ((in_base, offset // TILE), (out_base, (FF + offset) // TILE)):
        if own_rows:
            wspecs.append(pl.BlockSpec((own_rows, TILE), lambda j, *_, b=base_own: (0, b + j)))
        for p in pieces:
            wspecs.append(pl.BlockSpec((p.shape[0], TILE), lambda j, *_, b=base: (0, b + j)))
    wargs = [weights, *pieces]
    bb = offset // TILE
    gspec = pl.BlockSpec((2, D // 2, TILE), lambda j, *_: (0, 0, j))
    gshape = jax.ShapeDtypeStruct((2, D // 2, size), BF)
    return pl.pallas_call(
        functools.partial(mlp_kernel, len(wargs), first),
        grid_spec=pltpu.PrefetchScalarGridSpec(
            num_scalar_prefetch=1,
            grid=(nt_cols,),
            in_specs=[
                once((T, D)),
                once((D, T)),
                once((T, D)),
                once((D, T)),
                pl.BlockSpec((1, TILE), lambda j, *_: (0, bb + j)),
                *wspecs,
                *([] if first else [once((T, D)), once((D, T))]),
            ],
            out_specs=[
                gspec,
                gspec,
                pl.BlockSpec((1, TILE), lambda j, *_: (0, j)),
                once((T, D)),
                once((D, T)),
            ],
            scratch_shapes=[
                pltpu.VMEM((D, TILE), BF),
                pltpu.VMEM((D, TILE), BF),
                pltpu.VMEM((T, TILE), BF),
                pltpu.VMEM((T, TILE), BF),
            ],
        ),
        out_shape=[
            gshape,
            gshape,
            jax.ShapeDtypeStruct((1, size), F32),
            jax.ShapeDtypeStruct((T, D), F32),
            jax.ShapeDtypeStruct((D, T), F32),
        ],
        compiler_params=params(),
        cost_estimate=cost(43 * size / 2048),
    )(ids, n, nt, dy, dyt, bias, *wargs, *wargs, *([] if first else acc))


def proj_kernel(np_, ids, n_ref, d_ref, cos_ref, sin_ref, *refs):
    wq = refs[:np_]
    wo = refs[np_ : 2 * np_]
    out_ref, dout_ref, w_s, wo_s = refs[2 * np_ :]
    j = pl.program_id(0)
    place(w_s, wq, ids, 0)
    r = mm(w_s[...], n_ref[...], TT)

    def rotated(scale):
        for h in range(TB // HEAD_DIM):
            b = h * HEAD_DIM
            u = r[b : b + 16, :]
            w = r[b + 16 : b + 32, :]
            cs = cos_ref[...]
            sn = sin_ref[...]
            turned = [u * cs - w * sn, w * cs + u * sn, r[b + 32 : b + 64, :]]
            out_ref[b : b + 64, :] = (jnp.concatenate(turned, 0) * scale).astype(BF)

    @pl.when(j < 4)
    def _():
        rotated(LOG2E * HEAD_DIM ** (-0.5))

    @pl.when((j >= 4) & (j < 8))
    def _():
        rotated(1.0)

    @pl.when(j >= 8)
    def _():
        out_ref[...] = r.astype(BF)

    @pl.when(j == 0)
    def _():
        place(wo_s, wo, ids, 0)
        for t in range(D // TB):
            rows = slice(t * TB, (t + 1) * TB)
            dout_ref[rows, :] = mm(wo_s[rows, :], d_ref[...], NT).astype(BF)


def proj(ids, n, dy, cos, sin, weights, pieces):
    wargs = [weights, *pieces]
    return pl.pallas_call(
        functools.partial(proj_kernel, len(wargs)),
        grid_spec=pltpu.PrefetchScalarGridSpec(
            num_scalar_prefetch=1,
            grid=(3 * D // TB,),
            in_specs=[
                once((T, D)),
                once((T, D)),
                once((16, T)),
                once((16, T)),
                *[pl.BlockSpec((w.shape[0], TB), lambda j, *_: (0, j)) for w in wargs],
                *[
                    pl.BlockSpec((w.shape[0], D), lambda j, *_: (0, 3), pipeline_mode=pl.Buffered(1))
                    for w in wargs
                ],
            ],
            out_specs=[
                pl.BlockSpec((TB, T), lambda j, *_: (j, 0)),
                once((D, T)),
            ],
            scratch_shapes=[pltpu.VMEM((D, TB), BF), pltpu.VMEM((D, D), BF)],
        ),
        out_shape=[
            jax.ShapeDtypeStruct((3 * D, T), BF),
            jax.ShapeDtypeStruct((D, T), BF),
        ],
        compiler_params=params(),
        cost_estimate=cost(20),
    )(ids, n, dy, cos, sin, *wargs, *wargs)


QB = 512
HPS = 2


def attn_kernel(n_alias, len_ref, q_ref, k_ref, v_ref, do_ref, cos_ref, sin_ref, *refs):
    o_ref, dq_ref, dk_ref, dv_ref = refs[n_alias:]
    sub = lax.broadcasted_iota(jnp.int32, (HEAD_DIM, T), 0)
    lane = lax.broadcasted_iota(jnp.int32, (HEAD_DIM, T), 1)
    bias = jnp.where((sub == 0) & (lane >= len_ref[0]), -1e30, 0.0)
    ones = jnp.where(sub == 0, 1.0, 0.0).astype(BF)
    none = jnp.zeros((HEAD_DIM, T), F32)
    ki = lax.broadcasted_iota(jnp.int32, (QB, QB), 0)
    qi = lax.broadcasted_iota(jnp.int32, (QB, QB), 1)

    def unrot(val, cs, sn, out, base, cols):
        a = val[0:16, :]
        b = val[16:32, :]
        turned = [a * cs + b * sn, b * cs - a * sn, val[32:64, :]]
        out[base : base + 64, cols] = jnp.concatenate(turned, 0).astype(BF)

    for h in range(HPS):
        b = h * HEAD_DIM
        hs = slice(b, b + HEAD_DIM)
        q = q_ref[hs, :]
        k = k_ref[hs, :]
        v = v_ref[hs, :]
        qa = jnp.concatenate([q, ones], 0)
        ka = jnp.concatenate([k.astype(F32), bias], 0).T.astype(BF)
        vt = jnp.concatenate([v.astype(F32), none], 0).T.astype(BF)
        dk = [jnp.zeros((HEAD_DIM, QB), F32) for _ in range(T // QB)]
        dv = [jnp.zeros((HEAD_DIM, QB), F32) for _ in range(T // QB)]
        for i in range(T // QB):
            qs = slice(i * QB, (i + 1) * QB)
            kk = (i + 1) * QB
            st = mm(ka[:kk, :], qa[:, qs])
            diag = jnp.where(ki <= qi, st[kk - QB :, :], -1e30)
            st = diag if i == 0 else jnp.concatenate([st[: kk - QB, :], diag], 0)
            e = jnp.exp2(st - jnp.max(st, 0, keepdims=True))
            rl = 1.0 / jnp.sum(e, 0, keepdims=True)
            eb = e.astype(BF)
            ot = mm(v[:, :kk], eb) * rl
            o_ref[hs, qs] = ot.astype(BF)
            dn = (do_ref[hs, qs].astype(F32) * rl).astype(BF)
            delta = jnp.sum(dn.astype(F32) * ot, 0, keepdims=True)
            da = jnp.concatenate([dn, none[:, qs].astype(BF)], 0)
            ds = (e * (mm(vt[:kk, :], da) - delta)).astype(BF)
            dq = mm(k[:, :kk], ds) * (HEAD_DIM ** (-0.5))
            unrot(dq, cos_ref[:, qs], sin_ref[:, qs], dq_ref, b, qs)
            dvi = mm(dn, eb, NT)
            dki = mm(q[:, qs], ds, NT)
            for t in range(i + 1):
                ts = slice(t * QB, (t + 1) * QB)
                dv[t] = dv[t] + dvi[:, ts]
                dk[t] = dk[t] + dki[:, ts]
        for t in range(T // QB):
            ts = slice(t * QB, (t + 1) * QB)
            dv_ref[hs, ts] = dv[t].astype(BF)
            unrot(dk[t] * LN2, cos_ref[:, ts], sin_ref[:, ts], dk_ref, b, ts)


def attend(length, qkv, dot_, cos, sin, first, heads, before):
    rows = HPS * HEAD_DIM
    steps = HEADS // HPS
    at = first // HPS
    spec = lambda base: pl.BlockSpec((rows, T), lambda h, *_: (base + at + h, 0))
    shape = jax.ShapeDtypeStruct((D, T), BF)
    alias = [] if before is None else list(before)
    return pl.pallas_call(
        functools.partial(attn_kernel, len(alias)),
        grid_spec=pltpu.PrefetchScalarGridSpec(
            num_scalar_prefetch=1,
            grid=(heads // HPS,),
            in_specs=[
                spec(0),
                spec(steps),
                spec(2 * steps),
                spec(0),
                once((16, T)),
                once((16, T)),
            ]
            + [pl.BlockSpec(memory_space=pl.ANY)] * len(alias),
            out_specs=[spec(0)] * 4,
        ),
        out_shape=[shape] * 4,
        input_output_aliases={7 + i: i for i in range(len(alias))},
        compiler_params=params(),
        cost_estimate=cost(46 * heads / HEADS),
    )(length, qkv, qkv, qkv, dot_, cos, sin, *alias)


def agrad_kernel(hr, order, blocks, ids, nt_ref, dy_ref, o_ref, dq_ref, dk_ref, dv_ref, m_ref, t_ref, g_s):
    j = pl.program_id(0)
    half_d = D // 2
    for at, src in enumerate((dq_ref, dk_ref, dv_ref)):

        @pl.when((j >= 2 * at) & (j < 2 * at + 2))
        def _(src=src):
            val = src[...]
            for out, first in ((m_ref, 0), (t_ref, half_d)):
                g = mm(nt_ref[first : first + half_d, :], val, NT).astype(BF)
                for b in range(blocks):
                    k = order[b]
                    out[0, b * hr : (b + 1) * hr, :] = g[k * hr : (k + 1) * hr, :]

    @pl.when(j >= 6)
    def _():
        g_s[...] = mm(o_ref[...], dy_ref[...]).astype(BF)
        for b in range(blocks):
            m_ref[0, b * hr : (b + 1) * hr, :] = g_s[pl.ds(pl.multiple_of(ids[b], hr), hr), :]
            t_ref[0, b * hr : (b + 1) * hr, :] = g_s[pl.ds(pl.multiple_of(ids[blocks + b], hr), hr), :]


def attn_grads(ids, nt, dy, ot, dq, dk, dv, hr, order):
    blocks = len(order)

    def grab(at):
        return pl.BlockSpec((TILE, T), lambda j, *_: (jnp.clip(j - 2 * at, 0, 1), 0))

    gspec = pl.BlockSpec((1, D // 2, TILE), lambda j, *_: (j // 4, 0, j % 4))
    gshape = jax.ShapeDtypeStruct((2, D // 2, 2 * D), BF)
    return pl.pallas_call(
        functools.partial(agrad_kernel, hr, order, blocks),
        grid_spec=pltpu.PrefetchScalarGridSpec(
            num_scalar_prefetch=1,
            grid=(4 * D // TILE,),
            in_specs=[
                once((D, T)),
                pl.BlockSpec((T, TILE), lambda j, *_: (0, jnp.clip(j - 6, 0, 1))),
                once((D, T)),
                grab(0),
                grab(1),
                grab(2),
            ],
            out_specs=[gspec, gspec],
            scratch_shapes=[pltpu.VMEM((D, TILE), BF)],
        ),
        out_shape=[gshape] * 2,
        compiler_params=params(),
        cost_estimate=cost(17),
    )(ids, nt, dy, ot, dq, dk, dv)


def final_kernel(np_, ids, x_ref, dy_ref, g_ref, bo_ref, o_ref, dq_ref, dk_ref, dv_ref, ao_ref, ag_ref, *refs):
    wq = refs[:np_]
    out_ref, gin_ref, v_ref, w_s = refs[np_:]
    i = pl.program_id(0)

    @pl.when(i == 0)
    def _():
        place(w_s, wq, ids, 1)

    x = x_ref[...].astype(F32)
    row = i * TB + lax.broadcasted_iota(jnp.int32, (TB, 1), 0)
    attn = mm(o_ref[...], w_s[:, 3 * D :], TN)
    out = x + attn + ao_ref[...] + bo_ref[...]
    out_ref[...] = jnp.where(row < ids[0], out, 0.0).astype(BF)
    dn = (
        ag_ref[...]
        + mm(w_s[:, :D], dq_ref[...])
        + mm(w_s[:, D : 2 * D], dk_ref[...])
        + mm(w_s[:, 2 * D : 3 * D], dv_ref[...])
    ).T
    mean = jnp.mean(x, -1, keepdims=True)
    xc = x - mean
    inv = lax.rsqrt(jnp.mean(xc * xc, -1, keepdims=True) + NORM_EPS)
    xh = xc * inv
    g = dn * g_ref[...]
    gx = dn * xh
    ln = inv * (
        g - jnp.mean(g, -1, keepdims=True) - xh * jnp.mean(g * xh, -1, keepdims=True)
    )
    gin_ref[...] = (dy_ref[...].astype(F32) + ln).astype(BF)

    @pl.when(i == 0)
    def _():
        v_ref[...] = jnp.zeros_like(v_ref)

    v_ref[0:1, :] += jnp.sum(gx, 0, keepdims=True)
    v_ref[1:2, :] += jnp.sum(dn, 0, keepdims=True)


def final(ids, x, dy, gain, b_out, ot, dq, dk, dv, acc_o, acc_g, weights, pieces):
    row = pl.BlockSpec((TB, D), lambda i, *_: (i, 0))
    col = pl.BlockSpec((D, TB), lambda i, *_: (0, i))
    vec = pl.BlockSpec((1, D), lambda i, *_: (0, 0))
    wargs = [weights, *pieces]
    return pl.pallas_call(
        functools.partial(final_kernel, len(wargs)),
        grid_spec=pltpu.PrefetchScalarGridSpec(
            num_scalar_prefetch=1,
            grid=(T // TB,),
            in_specs=[
                row,
                row,
                vec,
                vec,
                col,
                col,
                col,
                col,
                row,
                col,
                *[once((w.shape[0], 4 * D)) for w in wargs],
            ],
            out_specs=[row, row, pl.BlockSpec((8, D), lambda i, *_: (0, 0))],
            scratch_shapes=[pltpu.VMEM((D, 4 * D), BF)],
        ),
        out_shape=[
            jax.ShapeDtypeStruct((T, D), BF),
            jax.ShapeDtypeStruct((T, D), BF),
            jax.ShapeDtypeStruct((8, D), F32),
        ],
        compiler_params=params(),
        cost_estimate=cost(20),
    )(ids, x, dy, gain, b_out, ot, dq, dk, dv, acc_o, acc_g, *wargs)


C1 = float(1.0 - np.float32(B1) ** np.float32(STEP))
C2 = float(1.0 - np.float32(B2) ** np.float32(STEP))


def adam_math(g, m, v, w, decay):
    nm = B1 * m + (1.0 - B1) * g
    nv = B2 * v + (1.0 - B2) * g * g
    up = -LR * (nm / C1 / (jnp.sqrt(nv / C2) + ADAM_EPS) + decay * w)
    return nm, nv, up


AC = 1024


def adam_kernel(n_alias, ids, sm, rm, so, ro, m_ref, v_ref, w_ref, *refs):
    wg_ref, nm_ref, nv_ref, up_ref = refs[n_alias:]
    summed = pl.program_id(0) == ids[1]
    hr = sm.shape[0]
    mine = jnp.where(summed, sm[...].astype(F32), rm[...].astype(F32))
    other = jnp.where(summed, so[...].astype(F32), ro[...].astype(F32))
    lead = ids[0] == 0
    for h, g in enumerate((jnp.where(lead, mine, other), jnp.where(lead, other, mine))):
        rows = slice(h * hr, (h + 1) * hr)
        nm, nv, up = adam_math(g, m_ref[rows, :], v_ref[rows, :], w_ref[rows, :].astype(F32), DECAY)
        wg_ref[rows, :] = g
        nm_ref[rows, :] = nm
        nv_ref[rows, :] = nv
        up_ref[rows, :] = up


def adam(ids, grads, cols, m, v, w, outs):
    rows, width = m.shape
    hr = rows // 2
    n = grads[0].shape[1]
    pick = lambda hit: pl.BlockSpec(
        (hr, AC), lambda p, j, ids: (0, jnp.where((p == ids[1]) == hit, j, 0))
    )
    b0, b1 = cols[0] // AC, cols[1] // AC
    big = pl.BlockSpec((rows, AC), lambda p, j, ids: (0, jnp.where(p == 0, b0, b1) + j))
    alias = [] if outs is None else list(outs)
    return pl.pallas_call(
        functools.partial(adam_kernel, len(alias)),
        grid_spec=pltpu.PrefetchScalarGridSpec(
            num_scalar_prefetch=1,
            grid=(2, n // AC),
            in_specs=[pick(True), pick(False), pick(True), pick(False), big, big, big]
            + [pl.BlockSpec(memory_space=pl.ANY)] * len(alias),
            out_specs=[big] * 4,
        ),
        out_shape=[jax.ShapeDtypeStruct((rows, width), F32)] * 4,
        input_output_aliases={8 + i: i for i in range(len(alias))},
        compiler_params=pltpu.CompilerParams(
            dimension_semantics=("arbitrary", "arbitrary"), vmem_limit_bytes=VLIM
        ),
        cost_estimate=cost(12 * n / 2048),
    )(ids, *grads, m, v, w, *alias)


def after(values, *waits):
    flat = lax.optimization_barrier((*values, *waits))
    return list(flat[: len(values)])


def on_device(shards, reps, hidden_in, cotangent, lengths, weights, moment_m, moment_v, vectors, vector_m, vector_v):
    s = lax.axis_index("shard")
    rep = lax.axis_index("rep")
    c = rep % 2
    z = rep // 2
    zs = reps // 2
    swap = [(i, i ^ 1) for i in range(reps)]
    rows = weights.shape[0]
    hr = rows // 2
    i32 = jnp.int32
    cube = shards == 4 and zs & (zs - 1) == 0 and zs >= 4
    xn = [(i, i ^ 1) for i in range(shards)]
    yn = [(i, i ^ 2) for i in range(shards)]
    zsteps = [3] + [1 << k for k in range(2, 16) if 1 << k < zs]
    zn = lambda bit: [(i, i ^ (2 * bit)) for i in range(reps)]
    own = ((z ^ (z // 2)) % 2) if cube else jnp.int32(0)

    if cube:
        x_order, y_order = (1, 3, 0, 2), (2, 3, 0, 1)
        x_rows = [(s ^ r) * rows for r in x_order]
        y_rows = [(s ^ r) * rows for r in y_order]
        y_in_x = tuple(x_order.index(r) for r in y_order)
    else:
        x_rows = y_rows = [r * rows for r in range(shards)]
        y_in_x = tuple(range(shards))
    cut = lambda at: [b + c * hr for b in at] + [b + (1 - c) * hr for b in at]
    x_off, y_off = cut(x_rows), cut(y_rows)
    stack = lambda *v: jnp.stack([jnp.asarray(x, i32) for x in v])
    length = lengths.astype(i32)
    gain = vectors[:D].reshape(1, D)
    shift = vectors[D : 2 * D].reshape(1, D)
    b_out = vectors[2 * D : 3 * D].reshape(1, D)
    b_in = vectors[3 * D :].reshape(1, FF)
    half_w = lax.dynamic_slice_in_dim(weights, c * hr, hr, 0)

    n, nt, dy, dyt, db_out = prep(
        stack(length[0], *x_off), hidden_in, cotangent, gain, shift, hr, shards
    )

    def part_of(cols):
        return jnp.concatenate([half_w[:, a:b] for a, b in cols], 1)

    q = hr // 2

    def gather_first(part):
        return [lax.ppermute(part, "shard", xn), lax.ppermute(part, "shard", yn)]

    def gather_second(first):
        rx, ry = first
        return [lax.ppermute(rx[:q], "shard", yn), lax.ppermute(ry[q:], "shard", xn)]

    def swapped(mine):
        return mine + [lax.ppermute(p, "rep", swap) for p in mine]

    def gather_whole(part):
        full = lax.all_gather(part, "shard", axis=0, tiled=True)
        other = lax.ppermute(full, "rep", swap)
        return [p[b * hr : (b + 1) * hr] for p in (full, other) for b in range(shards)]

    offsets = [0]
    for size in SIZES:
        offsets.append(offsets[-1] + size)
    apart, fpart = part_of([(0, 4 * D)]), part_of([(4 * D, 4 * D + 2 * FF)])
    if cube:
        base = [(s ^ 1) * rows, (s ^ 2) * rows, (s ^ 3) * rows, (s ^ 3) * rows + q]
        offs = [b + c * hr for b in base] + [b + (1 - c) * hr for b in base]
        one = gather_first(apart)
        one = after(one, n)
        one = one + gather_second(one)
        (fpart,) = after([fpart], *one)
        apieces = swapped(one)
        two = gather_first(fpart)
    else:
        offs = cut([b * rows for b in range(shards)])
        apieces = gather_whole(apart)
        two = gather_whole(fpart)
    piece_off = stack(s * rows, *offs)
    len_piece_off = stack(length[0], s * rows, *offs)

    add = lambda *v: sum(x.astype(F32) for x in v).astype(BF)

    cuts = 4

    class Reduce:
        def __init__(self, mine, theirs, y_first=False):
            self.mine = mine
            self.ways = (yn, xn) if y_first else (xn, yn)
            self.at = 0
            self.sums = None
            h = mine.shape[1] // (cuts // 2)
            self.got = [
                [lax.ppermute(theirs[e, b * h : (b + 1) * h], "rep", swap) for e in range(2)]
                for b in range(cuts // 2)
            ]
            self.brought = None

        def settle(self, last):
            if self.brought is not None:
                (self.brought,) = after([self.brought], last)

        def step(self):
            self.at += 1
            k = self.at
            m = self.mine
            near, far = [jnp.stack(v) for v in self.got]
            if not cube:
                groups = [[2 * j + e for j in range(zs)] for e in range(2)]
                both = add(m, jnp.concatenate([near, far], 1))
                both = lax.psum_scatter(both, "shard", scatter_dimension=1, tiled=True)
                both = lax.psum(both, "rep", axis_index_groups=groups)
                self.sums = (both[0], both[1])
                return []
            if k == 1:
                sent = add(m[:, : 2 * hr], near)
                self.brought = lax.ppermute(sent, "shard", self.ways[0])
            elif k == 2:
                self.first = self.brought
                sent = add(m[:, 3 * hr :], far[:, hr:], self.first[:, hr:])
                self.brought = lax.ppermute(sent, "shard", self.ways[1])
            elif k == 3:
                total = add(m[:, 2 * hr : 3 * hr], far[:, :hr], self.first[:, :hr], self.brought)
                lead = own == 0
                sent = jnp.where(lead, total[1], total[0])
                self.keep = jnp.where(lead, total[0], total[1])
                self.brought = lax.ppermute(sent, "rep", zn(1))
            elif k <= 3 + len(zsteps):
                sent = self.keep = add(self.keep, self.brought)
                self.brought = lax.ppermute(sent, "rep", zn(zsteps[k - 4]))
            else:
                sent = self.keep = add(self.keep, self.brought)
                self.brought = lax.ppermute(sent, "rep", zn(1))
                self.sums = (sent, self.brought)
            return [sent, self.brought]

        def result(self):
            while self.sums is None:
                self.step()
            return [*self.sums, *[lax.ppermute(v, "rep", swap) for v in self.sums]]

    flight = []

    def turn(values, last, *steps):
        nonlocal flight
        waits = flight
        flight = []
        for red in steps:
            if red.sums is None:
                red.settle(last)
                moved = red.step()
                waits = waits + moved[:1]
                flight = flight + moved[1:]
        return after(values, *waits) if waits else list(values)

    inv_freq = jnp.power(F32(10000.0), -jnp.arange(0, ROT, 2, dtype=F32) / ROT)
    angles = inv_freq[:, None] * jnp.arange(T, dtype=F32)[None, :]
    cos, sin = jnp.cos(angles), jnp.sin(angles)
    qkv, dot_ = proj(piece_off, n, dy, cos, sin, weights, apieces)
    half = HEADS // 2
    heads = attend(length, qkv, dot_, cos, sin, 0, half, None)
    if cube:
        *two, qkv = after([*two, qkv], heads[0])
        three = gather_second(two)
        fpieces = swapped(two)
    ot, dq, dk, dv = attend(length, qkv, dot_, cos, sin, half, half, heads)
    dyg = dy
    if cube:
        (dyg,) = after([dy], ot, *three, *fpieces)
        other = swapped(three)
        fpieces = fpieces[:2] + other[:2] + fpieces[2:] + other[2:]
    else:
        fpieces = two
    reds = [Reduce(*attn_grads(stack(*y_off), nt, dyg, ot, dq, dk, dv, hr, y_in_x), True)]
    places = [(0, 2 * D)]
    acc = None
    dbs = []
    nk = n
    for at, size in zip(offsets, SIZES):
        (nk,) = turn([nk], dbs[-1] if dbs else dv, *reds)
        grads_m, grads_t, db_in, *acc = mlp(
            piece_off, nk, nt, dy, dyt, b_in, weights, fpieces, at, size, acc
        )
        dbs.append(db_in)
        reds.append(Reduce(grads_m, grads_t))
        places.append((4 * D + at, 4 * D + FF + at))

    (ot,) = turn([ot], dbs[-1], *reds)
    out, grad_in, vsum = final(
        len_piece_off, hidden_in, dy, gain, b_out, ot, dq, dk, dv, *acc, weights, apieces
    )
    vec = jnp.concatenate([vsum[0], vsum[1], db_out[0], *[d[0] for d in dbs]])
    if cube:
        vec = vec.reshape(-1, 128)
        vec = vec + lax.ppermute(vec, "rep", swap)
        for way in (xn, yn):
            vec = vec + lax.ppermute(vec, "shard", way)
        for bit in [1] + zsteps:
            vec = vec + lax.ppermute(vec, "rep", zn(bit))
        vec = vec.reshape(-1)
    else:
        vec = lax.psum(vec, ("rep", "shard"))
    core = stack(c, own)
    big = None
    last = vsum
    turn([], last, *reds)
    for i, cols in enumerate(places):
        grads = reds[i].result()
        (moment_m,) = turn([moment_m], last, *reds[i + 1 :])
        big = adam(core, grads, cols, moment_m, moment_v, weights, big)
        last = big[0][:8, :128]
    vm, vv, vu = adam_math(vec, vector_m, vector_v, vectors, 0.0)
    return (out, grad_in, *big, vec, vm, vv, vu)


def solution(mesh):
    tok = P(("rep", "shard"), None)
    w = P("shard", None)
    return jax.shard_map(
        functools.partial(on_device, mesh.shape["shard"], mesh.shape["rep"]),
        mesh=mesh,
        in_specs=(tok, tok, P(("rep", "shard")), w, w, w, P(), P(), P()),
        out_specs=(tok, tok, w, w, w, w, P(), P(), P(), P()),
        check_vma=False,
    )
```

```python
import functools

import jax
import jax.numpy as jnp
import numpy as np
from jax import lax
from jax.experimental import pallas as pl
from jax.experimental.pallas import tpu as pltpu
from jax.sharding import PartitionSpec as P

D = 1024
HEADS = 16
HEAD_DIM = 64
ROT = 32
FF = 4096
T = 1024
STEP = 10

B1 = 0.9
B2 = 0.95
LR = 0.02
DECAY = 0.1
ADAM_EPS = 1e-08
NORM_EPS = 1e-05
GC = 0.7978845608028654
GA = 0.044715
LOG2E = 1.4426950408889634
LN2 = 0.6931471805599453

BF = jnp.bfloat16
F32 = jnp.float32
VLIM = 58 * 1024 * 1024
NN = (((1,), (0,)), ((), ()))
NT = (((1,), (1,)), ((), ()))
TN = (((0,), (0,)), ((), ()))
TT = (((0,), (1,)), ((), ()))
TILE = 512
SIZES = (1536, 1536, 1024)
MB = 1024
TB = 256
PT = 512
FT = 256


def mm(a, b, dims=NN):
    return lax.dot_general(a, b, dims, preferred_element_type=F32)


def params():
    return pltpu.CompilerParams(
        dimension_semantics=("arbitrary",), vmem_limit_bytes=VLIM
    )


def once(shape):
    return pl.BlockSpec(shape, lambda *_: (0,) * len(shape), pipeline_mode=pl.Buffered(1))


def cost(us):
    return pl.CostEstimate(flops=int(us * 1.15e9), bytes_accessed=1024, transcendentals=0)


def prep_kernel(hr, blocks, ids, x_ref, c_ref, g_ref, b_ref, n_ref, nt_ref, d_ref, dt_ref, db_ref, s_ref):
    i = pl.program_id(0)
    x = x_ref[...].astype(F32)
    mean = jnp.mean(x, -1, keepdims=True)
    xc = x - mean
    var = jnp.mean(xc * xc, -1, keepdims=True)
    n = xc * lax.rsqrt(var + NORM_EPS) * g_ref[...] + b_ref[...]
    n_ref[...] = n.astype(BF)
    row = i * TB + lax.broadcasted_iota(jnp.int32, (TB, 1), 0)
    dy = jnp.where(row < ids[0], c_ref[...].astype(F32), 0.0)
    d_ref[...] = dy.astype(BF)

    @pl.when(i == 0)
    def _():
        db_ref[...] = jnp.zeros_like(db_ref)

    db_ref[...] += jnp.sum(dy, 0, keepdims=True)
    for val, out in ((n, nt_ref), (dy, dt_ref)):
        s_ref[...] = val.T.astype(BF)
        for b in range(2 * blocks):
            off = pl.multiple_of(ids[1 + b], hr)
            out[b * hr : (b + 1) * hr, :] = s_ref[pl.ds(off, hr), :]


def prep(ids, x, cot, gain, shift, hr, blocks):
    row = lambda i, *_: (i, 0)
    col = lambda i, *_: (0, i)
    fix = lambda i, *_: (0, 0)
    return pl.pallas_call(
        functools.partial(prep_kernel, hr, blocks),
        grid_spec=pltpu.PrefetchScalarGridSpec(
            num_scalar_prefetch=1,
            grid=(T // TB,),
            in_specs=[
                pl.BlockSpec((TB, D), row),
                pl.BlockSpec((TB, D), row),
                pl.BlockSpec((1, D), fix),
                pl.BlockSpec((1, D), fix),
            ],
            out_specs=[
                pl.BlockSpec((TB, D), row),
                pl.BlockSpec((D, TB), col),
                pl.BlockSpec((TB, D), row),
                pl.BlockSpec((D, TB), col),
                pl.BlockSpec((1, D), fix),
            ],
            scratch_shapes=[pltpu.VMEM((D, TB), BF)],
        ),
        out_shape=[
            jax.ShapeDtypeStruct((T, D), BF),
            jax.ShapeDtypeStruct((D, T), BF),
            jax.ShapeDtypeStruct((T, D), BF),
            jax.ShapeDtypeStruct((D, T), BF),
            jax.ShapeDtypeStruct((1, D), F32),
        ],
        compiler_params=params(),
        cost_estimate=cost(8),
    )(ids, x, cot, gain, shift)


def place(dst, srcs, ids, base):
    for k, src in enumerate(srcs):
        rows = src.shape[0]
        dst[pl.ds(pl.multiple_of(ids[base + k], rows), rows), :] = src[...]


def spread(g, e, mine, near, far):
    a, b = D // 2, 3 * D // 4
    mine[e] = g[:a, :]
    near[...] = g[a:b, :]
    far[e] = g[b:, :]


def grad_shapes(n):
    return [
        jax.ShapeDtypeStruct(v, BF)
        for v in ((2, D // 2, n), (D // 4, n), (D // 4, n), (2, D // 4, n))
    ]


def mlp_kernel(np_, first, ids, n_ref, nt_ref, d_ref, dt_ref, b_ref, *refs):
    win = refs[:np_]
    wout = refs[np_ : 2 * np_]
    refs = refs[2 * np_ :]
    if not first:
        oin, gin = refs[:2]
        refs = refs[2:]
    gm, g0, g1, gf = refs[:4]
    db_ref, o_ref, g_ref, wi, wo, h_s, p_s = refs[4:]
    j = pl.program_id(0)
    place(wi, win, ids, 0)
    place(wo, wout, ids, 0)
    bias = b_ref[...]
    wi_v = wi[...]
    wo_v = wo[...]
    db = jnp.zeros((1, TILE), F32)
    for t in range(T // MB):
        rows = slice(t * MB, (t + 1) * MB)
        pre = mm(n_ref[rows, :], wi_v) + bias
        dh = mm(d_ref[rows, :], wo_v)
        sq = pre * pre
        th = jnp.tanh(GC * pre * (1.0 + GA * sq))
        half = 0.5 * (1.0 + th)
        h = (pre * half).astype(BF)
        slope = half + 0.5 * pre * (1.0 - th * th) * (GC + (3.0 * GA * GC) * sq)
        dp = (dh * slope).astype(BF)
        h_s[rows, :] = h
        p_s[rows, :] = dp
        db = db + jnp.sum(dp.astype(F32), 0, keepdims=True)
        ov = mm(h, wo_v, NT)
        gv = mm(wi_v, dp, NT)

        if first:

            @pl.when(j == 0)
            def _():
                o_ref[rows, :] = ov
                g_ref[:, rows] = gv

        else:

            @pl.when(j == 0)
            def _():
                o_ref[rows, :] = oin[rows, :] + ov
                g_ref[:, rows] = gin[:, rows] + gv

        @pl.when(j > 0)
        def _():
            o_ref[rows, :] += ov
            g_ref[:, rows] += gv

    db_ref[...] = db
    hv = h_s[...]
    pv = p_s[...]
    for e, (left, right) in enumerate(((nt_ref, pv), (dt_ref, hv))):
        spread(mm(left[...], right).astype(BF), e, gm, (g0, g1)[e], gf)


def mlp(ids, n, nt, dy, dyt, bias, weights, pieces, offset, size, acc):
    first = acc is None
    nt_cols = size // TILE
    tall = lambda cols: pl.BlockSpec((T, cols), lambda j, *_: (0, 0))
    own_rows = weights.shape[0]
    in_base = (4 * D + offset) // TILE
    out_base = (4 * D + FF + offset) // TILE
    wspecs = []
    for base_own, base in ((in_base, offset // TILE), (out_base, (FF + offset) // TILE)):
        if own_rows:
            wspecs.append(pl.BlockSpec((own_rows, TILE), lambda j, *_, b=base_own: (0, b + j)))
        for p in pieces:
            wspecs.append(pl.BlockSpec((p.shape[0], TILE), lambda j, *_, b=base: (0, b + j)))
    wargs = [weights, *pieces]
    bb = offset // TILE
    flat = pl.BlockSpec((D // 4, TILE), lambda j, *_: (0, j))
    deep = lambda r: pl.BlockSpec((2, r, TILE), lambda j, *_: (0, 0, j))
    gspecs = [deep(D // 2), flat, flat, deep(D // 4)]
    return pl.pallas_call(
        functools.partial(mlp_kernel, len(wargs), first),
        grid_spec=pltpu.PrefetchScalarGridSpec(
            num_scalar_prefetch=1,
            grid=(nt_cols,),
            in_specs=[
                once((T, D)),
                once((D, T)),
                once((T, D)),
                once((D, T)),
                pl.BlockSpec((1, TILE), lambda j, *_: (0, bb + j)),
                *wspecs,
                *([] if first else [once((T, D)), once((D, T))]),
            ],
            out_specs=[
                *gspecs,
                pl.BlockSpec((1, TILE), lambda j, *_: (0, j)),
                once((T, D)),
                once((D, T)),
            ],
            scratch_shapes=[
                pltpu.VMEM((D, TILE), BF),
                pltpu.VMEM((D, TILE), BF),
                pltpu.VMEM((T, TILE), BF),
                pltpu.VMEM((T, TILE), BF),
            ],
        ),
        out_shape=[
            *grad_shapes(size),
            jax.ShapeDtypeStruct((1, size), F32),
            jax.ShapeDtypeStruct((T, D), F32),
            jax.ShapeDtypeStruct((D, T), F32),
        ],
        compiler_params=params(),
        cost_estimate=cost(43 * size / 2048),
    )(ids, n, nt, dy, dyt, bias, *wargs, *wargs, *([] if first else acc))


def proj_kernel(np_, ids, n_ref, d_ref, cos_ref, sin_ref, *refs):
    wq = refs[:np_]
    wo = refs[np_ : 2 * np_]
    out_ref, dout_ref, w_s, wo_s = refs[2 * np_ :]
    j = pl.program_id(0)
    place(w_s, wq, ids, 0)
    r = mm(w_s[...], n_ref[...], TT)

    def rotated(scale):
        for h in range(PT // HEAD_DIM):
            b = h * HEAD_DIM
            u = r[b : b + 16, :]
            w = r[b + 16 : b + 32, :]
            cs = cos_ref[...]
            sn = sin_ref[...]
            turned = [u * cs - w * sn, w * cs + u * sn, r[b + 32 : b + 64, :]]
            out_ref[b : b + 64, :] = (jnp.concatenate(turned, 0) * scale).astype(BF)

    @pl.when(j < D // PT)
    def _():
        rotated(LOG2E * HEAD_DIM ** (-0.5))

    @pl.when((j >= D // PT) & (j < 2 * D // PT))
    def _():
        rotated(1.0)

    @pl.when(j >= 2 * D // PT)
    def _():
        out_ref[...] = r.astype(BF)

    @pl.when(j == 0)
    def _():
        place(wo_s, wo, ids, 0)
        dout_ref[...] = mm(wo_s[...], d_ref[...], NT).astype(BF)


def proj(ids, n, dy, cos, sin, weights, pieces):
    wargs = [weights, *pieces]
    return pl.pallas_call(
        functools.partial(proj_kernel, len(wargs)),
        grid_spec=pltpu.PrefetchScalarGridSpec(
            num_scalar_prefetch=1,
            grid=(3 * D // PT,),
            in_specs=[
                once((T, D)),
                once((T, D)),
                once((16, T)),
                once((16, T)),
                *[pl.BlockSpec((w.shape[0], PT), lambda j, *_: (0, j)) for w in wargs],
                *[
                    pl.BlockSpec((w.shape[0], D), lambda j, *_: (0, 3), pipeline_mode=pl.Buffered(1))
                    for w in wargs
                ],
            ],
            out_specs=[
                pl.BlockSpec((PT, T), lambda j, *_: (j, 0)),
                once((D, T)),
            ],
            scratch_shapes=[pltpu.VMEM((D, PT), BF), pltpu.VMEM((D, D), BF)],
        ),
        out_shape=[
            jax.ShapeDtypeStruct((3 * D, T), BF),
            jax.ShapeDtypeStruct((D, T), BF),
        ],
        compiler_params=params(),
        cost_estimate=cost(20),
    )(ids, n, dy, cos, sin, *wargs, *wargs)


QB = 512
HPS = 2


def attn_kernel(n_alias, len_ref, q_ref, k_ref, v_ref, do_ref, cos_ref, sin_ref, *refs):
    o_ref, dq_ref, dk_ref, dv_ref = refs[n_alias:]
    sub = lax.broadcasted_iota(jnp.int32, (HEAD_DIM, T), 0)
    lane = lax.broadcasted_iota(jnp.int32, (HEAD_DIM, T), 1)
    bias = jnp.where((sub == 0) & (lane >= len_ref[0]), -1e30, 0.0)
    ones = jnp.where(sub == 0, 1.0, 0.0).astype(BF)
    none = jnp.zeros((HEAD_DIM, T), F32)
    ki = lax.broadcasted_iota(jnp.int32, (QB, QB), 0)
    qi = lax.broadcasted_iota(jnp.int32, (QB, QB), 1)

    def unrot(val, cs, sn, out, base, cols):
        a = val[0:16, :]
        b = val[16:32, :]
        turned = [a * cs + b * sn, b * cs - a * sn, val[32:64, :]]
        out[base : base + 64, cols] = jnp.concatenate(turned, 0).astype(BF)

    for h in range(HPS):
        b = h * HEAD_DIM
        hs = slice(b, b + HEAD_DIM)
        q = q_ref[hs, :]
        k = k_ref[hs, :]
        v = v_ref[hs, :]
        qa = jnp.concatenate([q, ones], 0)
        ka = jnp.concatenate([k.astype(F32), bias], 0).T.astype(BF)
        vt = jnp.concatenate([v.astype(F32), none], 0).T.astype(BF)
        dk = [jnp.zeros((HEAD_DIM, QB), F32) for _ in range(T // QB)]
        dv = [jnp.zeros((HEAD_DIM, QB), F32) for _ in range(T // QB)]
        for i in range(T // QB):
            qs = slice(i * QB, (i + 1) * QB)
            kk = (i + 1) * QB
            st = mm(ka[:kk, :], qa[:, qs])
            diag = jnp.where(ki <= qi, st[kk - QB :, :], -1e30)
            st = diag if i == 0 else jnp.concatenate([st[: kk - QB, :], diag], 0)
            e = jnp.exp2(st - jnp.max(st, 0, keepdims=True))
            rl = 1.0 / jnp.sum(e, 0, keepdims=True)
            eb = e.astype(BF)
            ot = mm(v[:, :kk], eb) * rl
            o_ref[hs, qs] = ot.astype(BF)
            dn = (do_ref[hs, qs].astype(F32) * rl).astype(BF)
            delta = jnp.sum(dn.astype(F32) * ot, 0, keepdims=True)
            da = jnp.concatenate([dn, none[:, qs].astype(BF)], 0)
            ds = (e * (mm(vt[:kk, :], da) - delta)).astype(BF)
            dq = mm(k[:, :kk], ds) * (HEAD_DIM ** (-0.5))
            unrot(dq, cos_ref[:, qs], sin_ref[:, qs], dq_ref, b, qs)
            dvi = mm(dn, eb, NT)
            dki = mm(q[:, qs], ds, NT)
            for t in range(i + 1):
                ts = slice(t * QB, (t + 1) * QB)
                dv[t] = dv[t] + dvi[:, ts]
                dk[t] = dk[t] + dki[:, ts]
        for t in range(T // QB):
            ts = slice(t * QB, (t + 1) * QB)
            dv_ref[hs, ts] = dv[t].astype(BF)
            unrot(dk[t] * LN2, cos_ref[:, ts], sin_ref[:, ts], dk_ref, b, ts)


def attend(length, qkv, dot_, cos, sin, first, heads, before):
    rows = HPS * HEAD_DIM
    steps = HEADS // HPS
    at = first // HPS
    spec = lambda base: pl.BlockSpec((rows, T), lambda h, *_: (base + at + h, 0))
    shape = jax.ShapeDtypeStruct((D, T), BF)
    alias = [] if before is None else list(before)
    return pl.pallas_call(
        functools.partial(attn_kernel, len(alias)),
        grid_spec=pltpu.PrefetchScalarGridSpec(
            num_scalar_prefetch=1,
            grid=(heads // HPS,),
            in_specs=[
                spec(0),
                spec(steps),
                spec(2 * steps),
                spec(0),
                once((16, T)),
                once((16, T)),
            ]
            + [pl.BlockSpec(memory_space=pl.ANY)] * len(alias),
            out_specs=[spec(0)] * 4,
        ),
        out_shape=[shape] * 4,
        input_output_aliases={7 + i: i for i in range(len(alias))},
        compiler_params=params(),
        cost_estimate=cost(46 * heads / HEADS),
    )(length, qkv, qkv, qkv, dot_, cos, sin, *alias)


def agrad_kernel(hr, blocks, ids, nt_ref, dy_ref, o_ref, dq_ref, dk_ref, dv_ref, gm, g0, g1, gf, g_s):
    j = pl.program_id(0)
    for at, (src, near) in enumerate(((dq_ref, g0), (dk_ref, g0), (dv_ref, g1))):

        @pl.when((j >= 2 * at) & (j < 2 * at + 2))
        def _(src=src, near=near):
            spread(mm(nt_ref[...], src[...], NT).astype(BF), 0, gm, near, gf)

    @pl.when(j >= 6)
    def _():
        g_s[...] = mm(o_ref[...], dy_ref[...]).astype(BF)
        rows = [pl.multiple_of(ids[b], hr) for b in range(2 * blocks)]
        spread(jnp.concatenate([g_s[pl.ds(k, hr), :] for k in rows], 0), 0, gm, g1, gf)


def attn_grads(ids, nt, dy, ot, dq, dk, dv, hr, blocks):
    def grab(at):
        return pl.BlockSpec((TILE, T), lambda j, *_: (jnp.clip(j - 2 * at, 0, 1), 0))

    deep = lambda r: pl.BlockSpec((1, r, TILE), lambda j, *_: (j // 4, 0, j % 4))
    gspecs = [
        deep(D // 2),
        pl.BlockSpec((D // 4, TILE), lambda j, *_: (0, jnp.minimum(j, 3))),
        pl.BlockSpec((D // 4, TILE), lambda j, *_: (0, jnp.maximum(j - 4, 0))),
        deep(D // 4),
    ]
    return pl.pallas_call(
        functools.partial(agrad_kernel, hr, blocks),
        grid_spec=pltpu.PrefetchScalarGridSpec(
            num_scalar_prefetch=1,
            grid=(4 * D // TILE,),
            in_specs=[
                once((D, T)),
                pl.BlockSpec((T, TILE), lambda j, *_: (0, jnp.clip(j - 6, 0, 1))),
                once((D, T)),
                grab(0),
                grab(1),
                grab(2),
            ],
            out_specs=gspecs,
            scratch_shapes=[pltpu.VMEM((D, TILE), BF)],
        ),
        out_shape=grad_shapes(2 * D),
        compiler_params=params(),
        cost_estimate=cost(17),
    )(ids, nt, dy, ot, dq, dk, dv)


def final_kernel(np_, ids, x_ref, dy_ref, g_ref, bo_ref, o_ref, dq_ref, dk_ref, dv_ref, ao_ref, ag_ref, *refs):
    wq = refs[:np_]
    out_ref, gin_ref, v_ref, w_s = refs[np_:]
    i = pl.program_id(0)

    @pl.when(i == 0)
    def _():
        place(w_s, wq, ids, 1)

    x = x_ref[...].astype(F32)
    row = i * FT + lax.broadcasted_iota(jnp.int32, (FT, 1), 0)
    attn = mm(o_ref[...], w_s[:, 3 * D :], TN)
    out = x + attn + ao_ref[...] + bo_ref[...]
    out_ref[...] = jnp.where(row < ids[0], out, 0.0).astype(BF)
    dn = (
        ag_ref[...]
        + mm(w_s[:, :D], dq_ref[...])
        + mm(w_s[:, D : 2 * D], dk_ref[...])
        + mm(w_s[:, 2 * D : 3 * D], dv_ref[...])
    ).T
    mean = jnp.mean(x, -1, keepdims=True)
    xc = x - mean
    inv = lax.rsqrt(jnp.mean(xc * xc, -1, keepdims=True) + NORM_EPS)
    xh = xc * inv
    g = dn * g_ref[...]
    gx = dn * xh
    ln = inv * (
        g - jnp.mean(g, -1, keepdims=True) - xh * jnp.mean(g * xh, -1, keepdims=True)
    )
    gin_ref[...] = (dy_ref[...].astype(F32) + ln).astype(BF)

    @pl.when(i == 0)
    def _():
        v_ref[...] = jnp.zeros_like(v_ref)

    v_ref[0:1, :] += jnp.sum(gx, 0, keepdims=True)
    v_ref[1:2, :] += jnp.sum(dn, 0, keepdims=True)


def final(ids, x, dy, gain, b_out, ot, dq, dk, dv, acc_o, acc_g, weights, pieces):
    row = pl.BlockSpec((FT, D), lambda i, *_: (i, 0))
    col = pl.BlockSpec((D, FT), lambda i, *_: (0, i))
    vec = pl.BlockSpec((1, D), lambda i, *_: (0, 0))
    wargs = [weights, *pieces]
    return pl.pallas_call(
        functools.partial(final_kernel, len(wargs)),
        grid_spec=pltpu.PrefetchScalarGridSpec(
            num_scalar_prefetch=1,
            grid=(T // FT,),
            in_specs=[
                row,
                row,
                vec,
                vec,
                col,
                col,
                col,
                col,
                row,
                col,
                *[once((w.shape[0], 4 * D)) for w in wargs],
            ],
            out_specs=[row, row, pl.BlockSpec((8, D), lambda i, *_: (0, 0))],
            scratch_shapes=[pltpu.VMEM((D, 4 * D), BF)],
        ),
        out_shape=[
            jax.ShapeDtypeStruct((T, D), BF),
            jax.ShapeDtypeStruct((T, D), BF),
            jax.ShapeDtypeStruct((8, D), F32),
        ],
        compiler_params=params(),
        cost_estimate=cost(20),
    )(ids, x, dy, gain, b_out, ot, dq, dk, dv, acc_o, acc_g, *wargs)


C1 = float(1.0 - np.float32(B1) ** np.float32(STEP))
C2 = float(1.0 - np.float32(B2) ** np.float32(STEP))


def adam_math(g, m, v, w, decay):
    nm = B1 * m + (1.0 - B1) * g
    nv = B2 * v + (1.0 - B2) * g * g
    up = -LR * (nm / C1 / (jnp.sqrt(nv / C2) + ADAM_EPS) + decay * w)
    return nm, nv, up


def adam_kernel(n_alias, ids, sm, rm, so, ro, m_ref, v_ref, w_ref, *refs):
    wg_ref, nm_ref, nv_ref, up_ref, end_ref = refs[n_alias:]
    end_ref[...] = jnp.zeros_like(end_ref)
    summed = pl.program_id(0) == ids[1]
    hr = sm.shape[0]
    mine = jnp.where(summed, sm[...].astype(F32), rm[...].astype(F32))
    other = jnp.where(summed, so[...].astype(F32), ro[...].astype(F32))
    lead = ids[0] == 0
    for h, g in enumerate((jnp.where(lead, mine, other), jnp.where(lead, other, mine))):
        rows = slice(h * hr, (h + 1) * hr)
        nm, nv, up = adam_math(g, m_ref[rows, :], v_ref[rows, :], w_ref[rows, :].astype(F32), DECAY)
        wg_ref[rows, :] = g
        nm_ref[rows, :] = nm
        nv_ref[rows, :] = nv
        up_ref[rows, :] = up


def adam(ids, grads, cols, m, v, w, outs):
    rows, width = m.shape
    hr = rows // 2
    n = grads[0].shape[1]
    AC = 1024 if n % 1024 == 0 else 512
    pick = lambda hit: pl.BlockSpec(
        (hr, AC), lambda p, j, ids: (0, jnp.where((p == ids[1]) == hit, j, 0))
    )
    b0, b1 = cols[0] // AC, cols[1] // AC
    big = pl.BlockSpec((rows, AC), lambda p, j, ids: (0, jnp.where(p == 0, b0, b1) + j))
    alias = [] if outs is None else list(outs)
    return pl.pallas_call(
        functools.partial(adam_kernel, len(alias)),
        grid_spec=pltpu.PrefetchScalarGridSpec(
            num_scalar_prefetch=1,
            grid=(2, n // AC),
            in_specs=[pick(True), pick(False), pick(True), pick(False), big, big, big]
            + [pl.BlockSpec(memory_space=pl.ANY)] * len(alias),
            out_specs=[big] * 4 + [pl.BlockSpec((8, 128), lambda p, j, ids: (0, 0))],
        ),
        out_shape=[jax.ShapeDtypeStruct((rows, width), F32)] * 4
        + [jax.ShapeDtypeStruct((8, 128), F32)],
        input_output_aliases={8 + i: i for i in range(len(alias))},
        compiler_params=pltpu.CompilerParams(
            dimension_semantics=("arbitrary", "arbitrary"), vmem_limit_bytes=VLIM
        ),
        cost_estimate=cost(12 * n / 2048),
    )(ids, *grads, m, v, w, *alias)


def after(values, *waits):
    flat = lax.optimization_barrier((*values, *waits))
    return list(flat[: len(values)])


def on_device(shards, reps, hidden_in, cotangent, lengths, weights, moment_m, moment_v, vectors, vector_m, vector_v):
    s = lax.axis_index("shard")
    rep = lax.axis_index("rep")
    c = rep % 2
    z = rep // 2
    zs = reps // 2
    swap = [(i, i ^ 1) for i in range(reps)]
    rows = weights.shape[0]
    hr = rows // 2
    i32 = jnp.int32
    cube = shards == 4 and zs & (zs - 1) == 0 and zs >= 4
    xn = [(i, i ^ 1) for i in range(shards)]
    yn = [(i, i ^ 2) for i in range(shards)]
    zsteps = [3] + [1 << k for k in range(2, 16) if 1 << k < zs]
    zn = lambda bit: [(i, i ^ (2 * bit)) for i in range(reps)]
    own = ((z ^ (z // 2)) % 2) if cube else jnp.int32(0)

    if cube:
        y_rows = [(s ^ r) * rows for r in (2, 3, 0, 1)]
    else:
        y_rows = [r * rows for r in range(shards)]
    cut = lambda at: [b + c * hr for b in at] + [b + (1 - c) * hr for b in at]
    y_off = cut(y_rows)
    stack = lambda *v: jnp.stack([jnp.asarray(x, i32) for x in v])
    length = lengths.astype(i32)
    gain = vectors[:D].reshape(1, D)
    shift = vectors[D : 2 * D].reshape(1, D)
    b_out = vectors[2 * D : 3 * D].reshape(1, D)
    b_in = vectors[3 * D :].reshape(1, FF)
    half_w = lax.dynamic_slice_in_dim(weights, c * hr, hr, 0)

    n, nt, dy, dyt, db_out = prep(
        stack(length[0], *y_off), hidden_in, cotangent, gain, shift, hr, shards
    )

    def part_of(cols):
        return jnp.concatenate([half_w[:, a:b] for a, b in cols], 1)

    q = hr // 2

    def gather_first(part):
        a, b = part[:q], part[q:]
        return [
            lax.ppermute(p, "shard", way) for p, way in ((a, xn), (b, yn), (b, xn), (a, yn))
        ]

    def gather_second(first):
        return [lax.ppermute(first[0], "shard", yn), lax.ppermute(first[1], "shard", xn)]

    def swapped(mine):
        return mine + [lax.ppermute(p, "rep", swap) for p in mine]

    def gather_whole(part):
        full = lax.all_gather(part, "shard", axis=0, tiled=True)
        other = lax.ppermute(full, "rep", swap)
        return [p[b * hr : (b + 1) * hr] for p in (full, other) for b in range(shards)]

    offsets = [0]
    for size in SIZES:
        offsets.append(offsets[-1] + size)
    apart, fpart = part_of([(0, 4 * D)]), part_of([(4 * D, 4 * D + 2 * FF)])
    if cube:
        base = [(s ^ r) * rows + e * q for r, e in ((1, 0), (2, 1), (1, 1), (2, 0), (3, 0), (3, 1))]
        offs = [b + c * hr for b in base] + [b + (1 - c) * hr for b in base]
        one = gather_first(apart)
        one[:2] = after(one[:2], n)
        one = one + gather_second(one)
        (fpart,) = after([fpart], *one)
        apieces = swapped(one)
        two = gather_first(fpart)
    else:
        offs = cut([b * rows for b in range(shards)])
        apieces = gather_whole(apart)
        two = gather_whole(fpart)
    piece_off = stack(s * rows, *offs)
    len_piece_off = stack(length[0], s * rows, *offs)

    add = lambda *v: sum(x.astype(F32) for x in v).astype(BF)

    class Reduce:
        def __init__(self, grads):
            self.mine = grads[0]
            self.got = [lax.ppermute(g, "rep", swap) for g in grads[1:]]
            self.at = 0
            self.sums = None
            self.brought = []

        def settle(self, last):
            if self.brought:
                self.brought = after(self.brought, last)

        def step(self):
            self.at += 1
            k = self.at
            m, far, old = self.mine, self.got[2], self.brought
            if not cube:
                groups = [[2 * j + e for j in range(zs)] for e in range(2)]
                both = add(m, jnp.concatenate([jnp.stack(self.got[:2]), far], 1))
                both = lax.psum_scatter(both, "shard", scatter_dimension=1, tiled=True)
                both = lax.psum(both, "rep", axis_index_groups=groups)
                self.sums = (both[0], both[1])
                return [], []
            if k == 1:
                sent = add(m[:, : 2 * hr], jnp.stack(self.got[:2]))
                way = ("shard", yn)
            elif k == 2:
                self.first = old[0]
                sent = add(m[:, 3 * hr :], far[:, hr:], old[0][:, hr:])
                way = ("shard", xn)
            elif k == 3:
                total = add(m[:, 2 * hr : 3 * hr], far[:, :hr], self.first[:, :hr], old[0])
                lead = own == 0
                sent = jnp.where(lead, total[1], total[0])
                self.keep = jnp.where(lead, total[0], total[1])
                way = ("rep", zn(1))
            else:
                sent = self.keep = add(self.keep, old[0])
                last = k == 4 + len(zsteps)
                way = ("rep", zn(1 if last else zsteps[k - 4]))
            self.brought = [lax.ppermute(sent, *way)]
            if k == 4 + len(zsteps):
                self.sums = (self.keep, self.brought[0])
            return [sent], self.brought

        def result(self):
            while self.sums is None:
                self.step()
            return [*self.sums, *[lax.ppermute(v, "rep", swap) for v in self.sums]]

    flight = []

    def turn(values, last, *steps):
        nonlocal flight
        waits = flight
        flight = []
        for red in steps:
            if red.sums is None:
                red.settle(last)
                moved = red.step()
                waits = waits + moved[0]
                flight = flight + moved[1]
        return after(values, *waits) if waits else list(values)

    inv_freq = jnp.power(F32(10000.0), -jnp.arange(0, ROT, 2, dtype=F32) / ROT)
    angles = inv_freq[:, None] * jnp.arange(T, dtype=F32)[None, :]
    cos, sin = jnp.cos(angles), jnp.sin(angles)
    qkv, dot_ = proj(piece_off, n, dy, cos, sin, weights, apieces)
    half = HEADS // 2
    heads = attend(length, qkv, dot_, cos, sin, 0, half, None)
    if cube:
        *two, qkv = after([*two, qkv], heads[0])
        three = gather_second(two)
        fpieces = swapped(two)
    ot, dq, dk, dv = attend(length, qkv, dot_, cos, sin, half, half, heads)
    dyg = dy
    if cube:
        (dyg,) = after([dy], ot, *three, *fpieces)
        other = swapped(three)
        fpieces = fpieces[:4] + other[:2] + fpieces[4:] + other[2:]
    else:
        fpieces = two
    reds = [Reduce(attn_grads(stack(*y_off), nt, dyg, ot, dq, dk, dv, hr, shards))]
    places = [(0, 2 * D)]
    acc = None
    dbs = []
    nk = n
    for at, size in zip(offsets, SIZES):
        (nk,) = turn([nk], dbs[-1] if dbs else dv, *reds)
        *grads, db_in, acc_o, acc_g = mlp(
            piece_off, nk, nt, dy, dyt, b_in, weights, fpieces, at, size, acc
        )
        acc = (acc_o, acc_g)
        dbs.append(db_in)
        reds.append(Reduce(grads))
        places.append((4 * D + at, 4 * D + FF + at))

    (ot,) = turn([ot], dbs[-1], *reds)
    out, grad_in, vsum = final(
        len_piece_off, hidden_in, dy, gain, b_out, ot, dq, dk, dv, *acc, weights, apieces
    )
    core = stack(c, own)
    (first_core,) = turn([core], vsum, *reds)
    *big, end = adam(first_core, reds[0].result(), places[0], moment_m, moment_v, weights, None)
    vec = jnp.concatenate([vsum[0], vsum[1], db_out[0], *[d[0] for d in dbs]])
    (vec,) = after([vec], end)
    if cube:
        vec = vec.reshape(-1, 128)
        vec = vec + lax.ppermute(vec, "rep", swap)
        for way in (xn, yn):
            vec = vec + lax.ppermute(vec, "shard", way)
        for bit in [1] + zsteps:
            vec = vec + lax.ppermute(vec, "rep", zn(bit))
        vec = vec.reshape(-1)
    else:
        vec = lax.psum(vec, ("rep", "shard"))
    for i in range(1, len(reds)):
        turn([], end, *reds[i:])
        *big, end = adam(core, reds[i].result(), places[i], moment_m, moment_v, weights, big)
    vm, vv, vu = adam_math(vec, vector_m, vector_v, vectors, 0.0)
    return (out, grad_in, *big, vec, vm, vv, vu)


def solution(mesh):
    tok = P(("rep", "shard"), None)
    w = P("shard", None)
    return jax.shard_map(
        functools.partial(on_device, mesh.shape["shard"], mesh.shape["rep"]),
        mesh=mesh,
        in_specs=(tok, tok, P(("rep", "shard")), w, w, w, P(), P(), P()),
        out_specs=(tok, tok, w, w, w, w, P(), P(), P(), P()),
        check_vma=False,
    )
```

```python
import functools

import jax
import jax.numpy as jnp
import numpy as np
from jax import lax
from jax.experimental import pallas as pl
from jax.experimental.pallas import tpu as pltpu
from jax.sharding import PartitionSpec as P

D = 1024
HEADS = 16
HEAD_DIM = 64
ROT = 32
FF = 4096
T = 1024
STEP = 10

B1 = 0.9
B2 = 0.95
LR = 0.02
DECAY = 0.1
ADAM_EPS = 1e-08
NORM_EPS = 1e-05
GC = 0.7978845608028654
GA = 0.044715
LOG2E = 1.4426950408889634
LN2 = 0.6931471805599453

BF = jnp.bfloat16
F32 = jnp.float32
VLIM = 58 * 1024 * 1024
NN = (((1,), (0,)), ((), ()))
NT = (((1,), (1,)), ((), ()))
TN = (((0,), (0,)), ((), ()))
TT = (((0,), (1,)), ((), ()))
TILE = 512
SIZES = (2048, 1024, 1024)
MB = 1024
TB = 256
PT = 512
FT = 256


def mm(a, b, dims=NN):
    return lax.dot_general(a, b, dims, preferred_element_type=F32)


def params():
    return pltpu.CompilerParams(
        dimension_semantics=("arbitrary",), vmem_limit_bytes=VLIM
    )


def once(shape):
    return pl.BlockSpec(shape, lambda *_: (0,) * len(shape), pipeline_mode=pl.Buffered(1))


def cost(us):
    return pl.CostEstimate(flops=int(us * 1.15e9), bytes_accessed=1024, transcendentals=0)


def prep_kernel(hr, blocks, ids, x_ref, c_ref, g_ref, b_ref, n_ref, nt_ref, d_ref, dt_ref, db_ref, s_ref):
    i = pl.program_id(0)
    x = x_ref[...].astype(F32)
    mean = jnp.mean(x, -1, keepdims=True)
    xc = x - mean
    var = jnp.mean(xc * xc, -1, keepdims=True)
    n = xc * lax.rsqrt(var + NORM_EPS) * g_ref[...] + b_ref[...]
    n_ref[...] = n.astype(BF)
    row = i * TB + lax.broadcasted_iota(jnp.int32, (TB, 1), 0)
    dy = jnp.where(row < ids[0], c_ref[...].astype(F32), 0.0)
    d_ref[...] = dy.astype(BF)

    @pl.when(i == 0)
    def _():
        db_ref[...] = jnp.zeros_like(db_ref)

    db_ref[...] += jnp.sum(dy, 0, keepdims=True)
    for val, out in ((n, nt_ref), (dy, dt_ref)):
        s_ref[...] = val.T.astype(BF)
        for b in range(2 * blocks):
            off = pl.multiple_of(ids[1 + b], hr)
            out[b * hr : (b + 1) * hr, :] = s_ref[pl.ds(off, hr), :]


def prep(ids, x, cot, gain, shift, hr, blocks):
    row = lambda i, *_: (i, 0)
    col = lambda i, *_: (0, i)
    fix = lambda i, *_: (0, 0)
    return pl.pallas_call(
        functools.partial(prep_kernel, hr, blocks),
        grid_spec=pltpu.PrefetchScalarGridSpec(
            num_scalar_prefetch=1,
            grid=(T // TB,),
            in_specs=[
                pl.BlockSpec((TB, D), row),
                pl.BlockSpec((TB, D), row),
                pl.BlockSpec((1, D), fix),
                pl.BlockSpec((1, D), fix),
            ],
            out_specs=[
                pl.BlockSpec((TB, D), row),
                pl.BlockSpec((D, TB), col),
                pl.BlockSpec((TB, D), row),
                pl.BlockSpec((D, TB), col),
                pl.BlockSpec((1, D), fix),
            ],
            scratch_shapes=[pltpu.VMEM((D, TB), BF)],
        ),
        out_shape=[
            jax.ShapeDtypeStruct((T, D), BF),
            jax.ShapeDtypeStruct((D, T), BF),
            jax.ShapeDtypeStruct((T, D), BF),
            jax.ShapeDtypeStruct((D, T), BF),
            jax.ShapeDtypeStruct((1, D), F32),
        ],
        compiler_params=params(),
        cost_estimate=cost(8),
    )(ids, x, cot, gain, shift)


def place(dst, srcs, ids, base):
    for k, src in enumerate(srcs):
        rows = src.shape[0]
        dst[pl.ds(pl.multiple_of(ids[base + k], rows), rows), :] = src[...]


def spread(g, e, mine, near, far):
    a, b = D // 2, 3 * D // 4
    mine[e] = g[:a, :]
    near[...] = g[a:b, :]
    far[e] = g[b:, :]


def grad_shapes(n):
    return [
        jax.ShapeDtypeStruct(v, BF)
        for v in ((2, D // 2, n), (D // 4, n), (D // 4, n), (2, D // 4, n))
    ]


def mlp_kernel(np_, first, ids, n_ref, nt_ref, d_ref, dt_ref, b_ref, *refs):
    win = refs[:np_]
    wout = refs[np_ : 2 * np_]
    refs = refs[2 * np_ :]
    if not first:
        oin, gin = refs[:2]
        refs = refs[2:]
    gm, g0, g1, gf = refs[:4]
    db_ref, o_ref, g_ref, wi, wo, h_s, p_s = refs[4:]
    j = pl.program_id(0)
    place(wi, win, ids, 0)
    place(wo, wout, ids, 0)
    bias = b_ref[...]
    wi_v = wi[...]
    wo_v = wo[...]
    db = jnp.zeros((1, TILE), F32)
    for t in range(T // MB):
        rows = slice(t * MB, (t + 1) * MB)
        pre = mm(n_ref[rows, :], wi_v) + bias
        dh = mm(d_ref[rows, :], wo_v)
        sq = pre * pre
        th = jnp.tanh(GC * pre * (1.0 + GA * sq))
        half = 0.5 * (1.0 + th)
        h = (pre * half).astype(BF)
        slope = half + 0.5 * pre * (1.0 - th * th) * (GC + (3.0 * GA * GC) * sq)
        dp = (dh * slope).astype(BF)
        h_s[rows, :] = h
        p_s[rows, :] = dp
        db = db + jnp.sum(dp.astype(F32), 0, keepdims=True)
        ov = mm(h, wo_v, NT)
        gv = mm(wi_v, dp, NT)

        if first:

            @pl.when(j == 0)
            def _():
                o_ref[rows, :] = ov
                g_ref[:, rows] = gv

        else:

            @pl.when(j == 0)
            def _():
                o_ref[rows, :] = oin[rows, :] + ov
                g_ref[:, rows] = gin[:, rows] + gv

        @pl.when(j > 0)
        def _():
            o_ref[rows, :] += ov
            g_ref[:, rows] += gv

    db_ref[...] = db
    hv = h_s[...]
    pv = p_s[...]
    for e, (left, right) in enumerate(((nt_ref, pv), (dt_ref, hv))):
        spread(mm(left[...], right).astype(BF), e, gm, (g0, g1)[e], gf)


def mlp(ids, n, nt, dy, dyt, bias, weights, pieces, offset, size, acc):
    first = acc is None
    nt_cols = size // TILE
    tall = lambda cols: pl.BlockSpec((T, cols), lambda j, *_: (0, 0))
    own_rows = weights.shape[0]
    in_base = (4 * D + offset) // TILE
    out_base = (4 * D + FF + offset) // TILE
    wspecs = []
    for base_own, base in ((in_base, offset // TILE), (out_base, (FF + offset) // TILE)):
        if own_rows:
            wspecs.append(pl.BlockSpec((own_rows, TILE), lambda j, *_, b=base_own: (0, b + j)))
        for p in pieces:
            wspecs.append(pl.BlockSpec((p.shape[0], TILE), lambda j, *_, b=base: (0, b + j)))
    wargs = [weights, *pieces]
    bb = offset // TILE
    flat = pl.BlockSpec((D // 4, TILE), lambda j, *_: (0, j))
    deep = lambda r: pl.BlockSpec((2, r, TILE), lambda j, *_: (0, 0, j))
    gspecs = [deep(D // 2), flat, flat, deep(D // 4)]
    return pl.pallas_call(
        functools.partial(mlp_kernel, len(wargs), first),
        grid_spec=pltpu.PrefetchScalarGridSpec(
            num_scalar_prefetch=1,
            grid=(nt_cols,),
            in_specs=[
                once((T, D)),
                once((D, T)),
                once((T, D)),
                once((D, T)),
                pl.BlockSpec((1, TILE), lambda j, *_: (0, bb + j)),
                *wspecs,
                *([] if first else [once((T, D)), once((D, T))]),
            ],
            out_specs=[
                *gspecs,
                pl.BlockSpec((1, TILE), lambda j, *_: (0, j)),
                once((T, D)),
                once((D, T)),
            ],
            scratch_shapes=[
                pltpu.VMEM((D, TILE), BF),
                pltpu.VMEM((D, TILE), BF),
                pltpu.VMEM((T, TILE), BF),
                pltpu.VMEM((T, TILE), BF),
            ],
        ),
        out_shape=[
            *grad_shapes(size),
            jax.ShapeDtypeStruct((1, size), F32),
            jax.ShapeDtypeStruct((T, D), F32),
            jax.ShapeDtypeStruct((D, T), F32),
        ],
        compiler_params=params(),
        cost_estimate=cost(43 * size / 2048),
    )(ids, n, nt, dy, dyt, bias, *wargs, *wargs, *([] if first else acc))


def proj_kernel(np_, ids, n_ref, d_ref, cos_ref, sin_ref, *refs):
    wq = refs[:np_]
    wo = refs[np_ : 2 * np_]
    out_ref, dout_ref, w_s, wo_s = refs[2 * np_ :]
    j = pl.program_id(0)
    place(w_s, wq, ids, 0)
    r = mm(w_s[...], n_ref[...], TT)

    def rotated(scale):
        for h in range(PT // HEAD_DIM):
            b = h * HEAD_DIM
            u = r[b : b + 16, :]
            w = r[b + 16 : b + 32, :]
            cs = cos_ref[...]
            sn = sin_ref[...]
            turned = [u * cs - w * sn, w * cs + u * sn, r[b + 32 : b + 64, :]]
            out_ref[b : b + 64, :] = (jnp.concatenate(turned, 0) * scale).astype(BF)

    @pl.when(j < D // PT)
    def _():
        rotated(LOG2E * HEAD_DIM ** (-0.5))

    @pl.when((j >= D // PT) & (j < 2 * D // PT))
    def _():
        rotated(1.0)

    @pl.when(j >= 2 * D // PT)
    def _():
        out_ref[...] = r.astype(BF)

    @pl.when(j == 0)
    def _():
        place(wo_s, wo, ids, 0)
        dout_ref[...] = mm(wo_s[...], d_ref[...], NT).astype(BF)


def proj(ids, n, dy, cos, sin, weights, pieces):
    wargs = [weights, *pieces]
    return pl.pallas_call(
        functools.partial(proj_kernel, len(wargs)),
        grid_spec=pltpu.PrefetchScalarGridSpec(
            num_scalar_prefetch=1,
            grid=(3 * D // PT,),
            in_specs=[
                once((T, D)),
                once((T, D)),
                once((16, T)),
                once((16, T)),
                *[pl.BlockSpec((w.shape[0], PT), lambda j, *_: (0, j)) for w in wargs],
                *[
                    pl.BlockSpec((w.shape[0], D), lambda j, *_: (0, 3), pipeline_mode=pl.Buffered(1))
                    for w in wargs
                ],
            ],
            out_specs=[
                pl.BlockSpec((PT, T), lambda j, *_: (j, 0)),
                once((D, T)),
            ],
            scratch_shapes=[pltpu.VMEM((D, PT), BF), pltpu.VMEM((D, D), BF)],
        ),
        out_shape=[
            jax.ShapeDtypeStruct((3 * D, T), BF),
            jax.ShapeDtypeStruct((D, T), BF),
        ],
        compiler_params=params(),
        cost_estimate=cost(20),
    )(ids, n, dy, cos, sin, *wargs, *wargs)


QB = 512
HPS = 2


def attn_kernel(n_alias, len_ref, q_ref, k_ref, v_ref, do_ref, cos_ref, sin_ref, *refs):
    o_ref, dq_ref, dk_ref, dv_ref = refs[n_alias:]
    sub = lax.broadcasted_iota(jnp.int32, (HEAD_DIM, T), 0)
    lane = lax.broadcasted_iota(jnp.int32, (HEAD_DIM, T), 1)
    bias = jnp.where((sub == 0) & (lane >= len_ref[0]), -1e30, 0.0)
    ones = jnp.where(sub == 0, 1.0, 0.0).astype(BF)
    none = jnp.zeros((HEAD_DIM, T), F32)
    ki = lax.broadcasted_iota(jnp.int32, (QB, QB), 0)
    qi = lax.broadcasted_iota(jnp.int32, (QB, QB), 1)

    def unrot(val, cs, sn, out, base, cols):
        a = val[0:16, :]
        b = val[16:32, :]
        turned = [a * cs + b * sn, b * cs - a * sn, val[32:64, :]]
        out[base : base + 64, cols] = jnp.concatenate(turned, 0).astype(BF)

    for h in range(HPS):
        b = h * HEAD_DIM
        hs = slice(b, b + HEAD_DIM)
        q = q_ref[hs, :]
        k = k_ref[hs, :]
        v = v_ref[hs, :]
        qa = jnp.concatenate([q, ones], 0)
        ka = jnp.concatenate([k.astype(F32), bias], 0).T.astype(BF)
        vt = jnp.concatenate([v.astype(F32), none], 0).T.astype(BF)
        dk = [jnp.zeros((HEAD_DIM, QB), F32) for _ in range(T // QB)]
        dv = [jnp.zeros((HEAD_DIM, QB), F32) for _ in range(T // QB)]
        for i in range(T // QB):
            qs = slice(i * QB, (i + 1) * QB)
            kk = (i + 1) * QB
            st = mm(ka[:kk, :], qa[:, qs])
            diag = jnp.where(ki <= qi, st[kk - QB :, :], -1e30)
            st = diag if i == 0 else jnp.concatenate([st[: kk - QB, :], diag], 0)
            e = jnp.exp2(st - jnp.max(st, 0, keepdims=True))
            rl = 1.0 / jnp.sum(e, 0, keepdims=True)
            eb = e.astype(BF)
            ot = mm(v[:, :kk], eb) * rl
            o_ref[hs, qs] = ot.astype(BF)
            dn = (do_ref[hs, qs].astype(F32) * rl).astype(BF)
            delta = jnp.sum(dn.astype(F32) * ot, 0, keepdims=True)
            da = jnp.concatenate([dn, none[:, qs].astype(BF)], 0)
            ds = (e * (mm(vt[:kk, :], da) - delta)).astype(BF)
            dq = mm(k[:, :kk], ds) * (HEAD_DIM ** (-0.5))
            unrot(dq, cos_ref[:, qs], sin_ref[:, qs], dq_ref, b, qs)
            dvi = mm(dn, eb, NT)
            dki = mm(q[:, qs], ds, NT)
            for t in range(i + 1):
                ts = slice(t * QB, (t + 1) * QB)
                dv[t] = dv[t] + dvi[:, ts]
                dk[t] = dk[t] + dki[:, ts]
        for t in range(T // QB):
            ts = slice(t * QB, (t + 1) * QB)
            dv_ref[hs, ts] = dv[t].astype(BF)
            unrot(dk[t] * LN2, cos_ref[:, ts], sin_ref[:, ts], dk_ref, b, ts)


def attend(length, qkv, dot_, cos, sin, first, heads, before):
    rows = HPS * HEAD_DIM
    steps = HEADS // HPS
    at = first // HPS
    spec = lambda base: pl.BlockSpec((rows, T), lambda h, *_: (base + at + h, 0))
    shape = jax.ShapeDtypeStruct((D, T), BF)
    alias = [] if before is None else list(before)
    return pl.pallas_call(
        functools.partial(attn_kernel, len(alias)),
        grid_spec=pltpu.PrefetchScalarGridSpec(
            num_scalar_prefetch=1,
            grid=(heads // HPS,),
            in_specs=[
                spec(0),
                spec(steps),
                spec(2 * steps),
                spec(0),
                once((16, T)),
                once((16, T)),
            ]
            + [pl.BlockSpec(memory_space=pl.ANY)] * len(alias),
            out_specs=[spec(0)] * 4,
        ),
        out_shape=[shape] * 4,
        input_output_aliases={7 + i: i for i in range(len(alias))},
        compiler_params=params(),
        cost_estimate=cost(46 * heads / HEADS),
    )(length, qkv, qkv, qkv, dot_, cos, sin, *alias)


def agrad_kernel(hr, blocks, ids, nt_ref, dy_ref, o_ref, dq_ref, dk_ref, dv_ref, gm, g0, g1, gf, g_s):
    j = pl.program_id(0)
    for at, (src, near) in enumerate(((dq_ref, g0), (dk_ref, g0), (dv_ref, g1))):

        @pl.when((j >= 2 * at) & (j < 2 * at + 2))
        def _(src=src, near=near):
            spread(mm(nt_ref[...], src[...], NT).astype(BF), 0, gm, near, gf)

    @pl.when(j >= 6)
    def _():
        g_s[...] = mm(o_ref[...], dy_ref[...]).astype(BF)
        rows = [pl.multiple_of(ids[b], hr) for b in range(2 * blocks)]
        spread(jnp.concatenate([g_s[pl.ds(k, hr), :] for k in rows], 0), 0, gm, g1, gf)


def attn_grads(ids, nt, dy, ot, dq, dk, dv, hr, blocks):
    def grab(at):
        return pl.BlockSpec((TILE, T), lambda j, *_: (jnp.clip(j - 2 * at, 0, 1), 0))

    deep = lambda r: pl.BlockSpec((1, r, TILE), lambda j, *_: (j // 4, 0, j % 4))
    gspecs = [
        deep(D // 2),
        pl.BlockSpec((D // 4, TILE), lambda j, *_: (0, jnp.minimum(j, 3))),
        pl.BlockSpec((D // 4, TILE), lambda j, *_: (0, jnp.maximum(j - 4, 0))),
        deep(D // 4),
    ]
    return pl.pallas_call(
        functools.partial(agrad_kernel, hr, blocks),
        grid_spec=pltpu.PrefetchScalarGridSpec(
            num_scalar_prefetch=1,
            grid=(4 * D // TILE,),
            in_specs=[
                once((D, T)),
                pl.BlockSpec((T, TILE), lambda j, *_: (0, jnp.clip(j - 6, 0, 1))),
                once((D, T)),
                grab(0),
                grab(1),
                grab(2),
            ],
            out_specs=gspecs,
            scratch_shapes=[pltpu.VMEM((D, TILE), BF)],
        ),
        out_shape=grad_shapes(2 * D),
        compiler_params=params(),
        cost_estimate=cost(17),
    )(ids, nt, dy, ot, dq, dk, dv)


def final_kernel(np_, ids, x_ref, dy_ref, g_ref, bo_ref, o_ref, dq_ref, dk_ref, dv_ref, ao_ref, ag_ref, *refs):
    wq = refs[:np_]
    out_ref, gin_ref, v_ref, w_s = refs[np_:]
    i = pl.program_id(0)

    @pl.when(i == 0)
    def _():
        place(w_s, wq, ids, 1)

    x = x_ref[...].astype(F32)
    row = i * FT + lax.broadcasted_iota(jnp.int32, (FT, 1), 0)
    attn = mm(o_ref[...], w_s[:, 3 * D :], TN)
    out = x + attn + ao_ref[...] + bo_ref[...]
    out_ref[...] = jnp.where(row < ids[0], out, 0.0).astype(BF)
    dn = (
        ag_ref[...]
        + mm(w_s[:, :D], dq_ref[...])
        + mm(w_s[:, D : 2 * D], dk_ref[...])
        + mm(w_s[:, 2 * D : 3 * D], dv_ref[...])
    ).T
    mean = jnp.mean(x, -1, keepdims=True)
    xc = x - mean
    inv = lax.rsqrt(jnp.mean(xc * xc, -1, keepdims=True) + NORM_EPS)
    xh = xc * inv
    g = dn * g_ref[...]
    gx = dn * xh
    ln = inv * (
        g - jnp.mean(g, -1, keepdims=True) - xh * jnp.mean(g * xh, -1, keepdims=True)
    )
    gin_ref[...] = (dy_ref[...].astype(F32) + ln).astype(BF)

    @pl.when(i == 0)
    def _():
        v_ref[...] = jnp.zeros_like(v_ref)

    v_ref[0:1, :] += jnp.sum(gx, 0, keepdims=True)
    v_ref[1:2, :] += jnp.sum(dn, 0, keepdims=True)


def final(ids, x, dy, gain, b_out, ot, dq, dk, dv, acc_o, acc_g, weights, pieces):
    row = pl.BlockSpec((FT, D), lambda i, *_: (i, 0))
    col = pl.BlockSpec((D, FT), lambda i, *_: (0, i))
    vec = pl.BlockSpec((1, D), lambda i, *_: (0, 0))
    wargs = [weights, *pieces]
    return pl.pallas_call(
        functools.partial(final_kernel, len(wargs)),
        grid_spec=pltpu.PrefetchScalarGridSpec(
            num_scalar_prefetch=1,
            grid=(T // FT,),
            in_specs=[
                row,
                row,
                vec,
                vec,
                col,
                col,
                col,
                col,
                row,
                col,
                *[once((w.shape[0], 4 * D)) for w in wargs],
            ],
            out_specs=[row, row, pl.BlockSpec((8, D), lambda i, *_: (0, 0))],
            scratch_shapes=[pltpu.VMEM((D, 4 * D), BF)],
        ),
        out_shape=[
            jax.ShapeDtypeStruct((T, D), BF),
            jax.ShapeDtypeStruct((T, D), BF),
            jax.ShapeDtypeStruct((8, D), F32),
        ],
        compiler_params=params(),
        cost_estimate=cost(20),
    )(ids, x, dy, gain, b_out, ot, dq, dk, dv, acc_o, acc_g, *wargs)


C1 = float(1.0 - np.float32(B1) ** np.float32(STEP))
C2 = float(1.0 - np.float32(B2) ** np.float32(STEP))


def adam_math(g, m, v, w, decay):
    nm = B1 * m + (1.0 - B1) * g
    nv = B2 * v + (1.0 - B2) * g * g
    up = -LR * (nm / C1 / (jnp.sqrt(nv / C2) + ADAM_EPS) + decay * w)
    return nm, nv, up


def adam_kernel(n_alias, first, ids, sm, rm, so, ro, m_ref, v_ref, w_ref, *refs):
    wg_ref, nm_ref, nv_ref, up_ref, end_ref = refs[n_alias:]
    end_ref[...] = jnp.zeros_like(end_ref)
    summed = pl.program_id(0) + first == ids[1]
    hr = sm.shape[0]
    mine = jnp.where(summed, sm[...].astype(F32), rm[...].astype(F32))
    other = jnp.where(summed, so[...].astype(F32), ro[...].astype(F32))
    lead = ids[0] == 0
    for h, g in enumerate((jnp.where(lead, mine, other), jnp.where(lead, other, mine))):
        rows = slice(h * hr, (h + 1) * hr)
        nm, nv, up = adam_math(g, m_ref[rows, :], v_ref[rows, :], w_ref[rows, :].astype(F32), DECAY)
        wg_ref[rows, :] = g
        nm_ref[rows, :] = nm
        nv_ref[rows, :] = nv
        up_ref[rows, :] = up


def adam(ids, grads, cols, m, v, w, outs, first=0, count=2):
    rows, width = m.shape
    hr = rows // 2
    n = grads[0].shape[1]
    AC = 1024 if n % 1024 == 0 else 512
    pick = lambda hit: pl.BlockSpec(
        (hr, AC), lambda p, j, ids: (0, jnp.where((p + first == ids[1]) == hit, j, 0))
    )
    b0, b1 = cols[0] // AC, cols[1] // AC
    big = pl.BlockSpec((rows, AC), lambda p, j, ids: (0, jnp.where(p + first == 0, b0, b1) + j))
    alias = [] if outs is None else list(outs)
    return pl.pallas_call(
        functools.partial(adam_kernel, len(alias), first),
        grid_spec=pltpu.PrefetchScalarGridSpec(
            num_scalar_prefetch=1,
            grid=(count, n // AC),
            in_specs=[pick(True), pick(False), pick(True), pick(False), big, big, big]
            + [pl.BlockSpec(memory_space=pl.ANY)] * len(alias),
            out_specs=[big] * 4 + [pl.BlockSpec((8, 128), lambda p, j, ids: (0, 0))],
        ),
        out_shape=[jax.ShapeDtypeStruct((rows, width), F32)] * 4
        + [jax.ShapeDtypeStruct((8, 128), F32)],
        input_output_aliases={8 + i: i for i in range(len(alias))},
        compiler_params=pltpu.CompilerParams(
            dimension_semantics=("arbitrary", "arbitrary"), vmem_limit_bytes=VLIM
        ),
        cost_estimate=cost(6 * count * n / 2048),
    )(ids, *grads, m, v, w, *alias)


def after(values, *waits):
    flat = lax.optimization_barrier((*values, *waits))
    return list(flat[: len(values)])


def on_device(shards, reps, hidden_in, cotangent, lengths, weights, moment_m, moment_v, vectors, vector_m, vector_v):
    s = lax.axis_index("shard")
    rep = lax.axis_index("rep")
    c = rep % 2
    z = rep // 2
    zs = reps // 2
    swap = [(i, i ^ 1) for i in range(reps)]
    rows = weights.shape[0]
    hr = rows // 2
    i32 = jnp.int32
    cube = shards == 4 and zs & (zs - 1) == 0 and zs >= 4
    xn = [(i, i ^ 1) for i in range(shards)]
    yn = [(i, i ^ 2) for i in range(shards)]
    zsteps = [3] + [1 << k for k in range(2, 16) if 1 << k < zs]
    zn = lambda bit: [(i, i ^ (2 * bit)) for i in range(reps)]
    own = ((z ^ (z // 2)) % 2) if cube else jnp.int32(0)

    if cube:
        y_rows = [(s ^ r) * rows for r in (2, 3, 0, 1)]
    else:
        y_rows = [r * rows for r in range(shards)]
    cut = lambda at: [b + c * hr for b in at] + [b + (1 - c) * hr for b in at]
    y_off = cut(y_rows)
    stack = lambda *v: jnp.stack([jnp.asarray(x, i32) for x in v])
    length = lengths.astype(i32)
    gain = vectors[:D].reshape(1, D)
    shift = vectors[D : 2 * D].reshape(1, D)
    b_out = vectors[2 * D : 3 * D].reshape(1, D)
    b_in = vectors[3 * D :].reshape(1, FF)
    half_w = lax.dynamic_slice_in_dim(weights, c * hr, hr, 0)

    n, nt, dy, dyt, db_out = prep(
        stack(length[0], *y_off), hidden_in, cotangent, gain, shift, hr, shards
    )

    def part_of(cols):
        return jnp.concatenate([half_w[:, a:b] for a, b in cols], 1)

    q = hr // 2

    def gather_first(part):
        a, b = part[:q], part[q:]
        return [
            lax.ppermute(p, "shard", way) for p, way in ((a, xn), (b, yn), (b, xn), (a, yn))
        ]

    def gather_second(first):
        return [lax.ppermute(first[0], "shard", yn), lax.ppermute(first[1], "shard", xn)]

    def swapped(mine):
        return mine + [lax.ppermute(p, "rep", swap) for p in mine]

    def gather_whole(part):
        full = lax.all_gather(part, "shard", axis=0, tiled=True)
        other = lax.ppermute(full, "rep", swap)
        return [p[b * hr : (b + 1) * hr] for p in (full, other) for b in range(shards)]

    offsets = [0]
    for size in SIZES:
        offsets.append(offsets[-1] + size)
    apart, fpart = part_of([(0, 4 * D)]), part_of([(4 * D, 4 * D + 2 * FF)])
    if cube:
        base = [(s ^ r) * rows + e * q for r, e in ((1, 0), (2, 1), (1, 1), (2, 0), (3, 0), (3, 1))]
        offs = [b + c * hr for b in base] + [b + (1 - c) * hr for b in base]
        one = gather_first(apart)
        one[:2] = after(one[:2], n)
        one = one + gather_second(one)
        (fpart,) = after([fpart], *one)
        apieces = swapped(one)
        two = gather_first(fpart)
    else:
        offs = cut([b * rows for b in range(shards)])
        apieces = gather_whole(apart)
        two = gather_whole(fpart)
    piece_off = stack(s * rows, *offs)
    len_piece_off = stack(length[0], s * rows, *offs)

    add = lambda *v: sum(x.astype(F32) for x in v).astype(BF)

    class Reduce:
        def __init__(self, grads):
            self.mine = grads[0]
            self.got = [lax.ppermute(g, "rep", swap) for g in grads[1:]]
            self.at = 0
            self.sums = None
            self.brought = []

        def settle(self, last):
            if self.brought:
                self.brought = after(self.brought, last)

        def step(self):
            self.at += 1
            k = self.at
            m, far, old = self.mine, self.got[2], self.brought
            if not cube:
                groups = [[2 * j + e for j in range(zs)] for e in range(2)]
                both = add(m, jnp.concatenate([jnp.stack(self.got[:2]), far], 1))
                both = lax.psum_scatter(both, "shard", scatter_dimension=1, tiled=True)
                both = lax.psum(both, "rep", axis_index_groups=groups)
                self.sums = (both[0], both[1])
                return [], []
            if k == 1:
                sent = add(m[:, : 2 * hr], jnp.stack(self.got[:2]))
                way = ("shard", yn)
            elif k == 2:
                self.first = old[0]
                sent = add(m[:, 3 * hr :], far[:, hr:], old[0][:, hr:])
                way = ("shard", xn)
            elif k == 3:
                total = add(m[:, 2 * hr : 3 * hr], far[:, :hr], self.first[:, :hr], old[0])
                lead = own == 0
                sent = jnp.where(lead, total[1], total[0])
                self.keep = jnp.where(lead, total[0], total[1])
                way = ("rep", zn(1))
            else:
                sent = self.keep = add(self.keep, old[0])
                last = k == 4 + len(zsteps)
                way = ("rep", zn(1 if last else zsteps[k - 4]))
            self.brought = [lax.ppermute(sent, *way)]
            if k == 4 + len(zsteps):
                self.sums = (self.keep, self.brought[0])
            return [sent], self.brought

        def result(self):
            while self.sums is None:
                self.step()
            return [*self.sums, *[lax.ppermute(v, "rep", swap) for v in self.sums]]

    flight = []

    def turn(values, last, *steps):
        nonlocal flight
        waits = flight
        flight = []
        for red in steps:
            if red.sums is None:
                red.settle(last)
                moved = red.step()
                waits = waits + moved[0]
                flight = flight + moved[1]
        return after(values, *waits) if waits else list(values)

    inv_freq = jnp.power(F32(10000.0), -jnp.arange(0, ROT, 2, dtype=F32) / ROT)
    angles = inv_freq[:, None] * jnp.arange(T, dtype=F32)[None, :]
    cos, sin = jnp.cos(angles), jnp.sin(angles)
    qkv, dot_ = proj(piece_off, n, dy, cos, sin, weights, apieces)
    half = HEADS // 2
    heads = attend(length, qkv, dot_, cos, sin, 0, half, None)
    if cube:
        *two, qkv = after([*two, qkv], heads[0])
        three = gather_second(two)
        fpieces = swapped(two)
    ot, dq, dk, dv = attend(length, qkv, dot_, cos, sin, half, half, heads)
    dyg = dy
    if cube:
        (dyg,) = after([dy], ot, *three, *fpieces)
        other = swapped(three)
        fpieces = fpieces[:4] + other[:2] + fpieces[4:] + other[2:]
    else:
        fpieces = two
    reds = [Reduce(attn_grads(stack(*y_off), nt, dyg, ot, dq, dk, dv, hr, shards))]
    places = [(0, 2 * D)]
    acc = None
    dbs = []
    nk = n
    for at, size in zip(offsets, SIZES):
        (nk,) = turn([nk], dbs[-1] if dbs else dv, *reds)
        *grads, db_in, acc_o, acc_g = mlp(
            piece_off, nk, nt, dy, dyt, b_in, weights, fpieces, at, size, acc
        )
        acc = (acc_o, acc_g)
        dbs.append(db_in)
        reds.append(Reduce(grads))
        places.append((4 * D + at, 4 * D + FF + at))

    (ot,) = turn([ot], dbs[-1], *reds)
    out, grad_in, vsum = final(
        len_piece_off, hidden_in, dy, gain, b_out, ot, dq, dk, dv, *acc, weights, apieces
    )
    core = stack(c, own)
    def push(last, *steps):
        waits = []
        for red in steps:
            if red.sums is None:
                red.settle(last)
                waits = waits + red.step()[0]
        return after([core], *waits)[0] if waits else core

    args = moment_m, moment_v, weights
    ids = push(vsum, *reds)
    done = reds[0].result()
    *big, end = adam(ids, done, places[0], *args, None, 0, 1)
    ids = push(end, *reds[2:])
    *big, end = adam(ids, done, places[0], *args, big, 1, 1)
    vec = jnp.concatenate([vsum[0], vsum[1], db_out[0], *[d[0] for d in dbs]])
    (vec,) = after([vec], end)
    if cube:
        vec = vec.reshape(-1, 128)
        vec = vec + lax.ppermute(vec, "rep", swap)
        for way in (xn, yn):
            vec = vec + lax.ppermute(vec, "shard", way)
        for bit in [1] + zsteps:
            vec = vec + lax.ppermute(vec, "rep", zn(bit))
        vec = vec.reshape(-1)
    else:
        vec = lax.psum(vec, ("rep", "shard"))
    ids = push(end, reds[1], *reds[3:])
    done = reds[1].result()
    *big, end = adam(ids, done, places[1], *args, big, 0, 1)
    ids = push(end, *reds[2:])
    *big, end = adam(ids, done, places[1], *args, big, 1, 1)
    for red, place_ in zip(reds[2:], places[2:]):
        *big, end = adam(core, red.result(), place_, *args, big)
    vm, vv, vu = adam_math(vec, vector_m, vector_v, vectors, 0.0)
    return (out, grad_in, *big, vec, vm, vv, vu)


def solution(mesh):
    tok = P(("rep", "shard"), None)
    w = P("shard", None)
    return jax.shard_map(
        functools.partial(on_device, mesh.shape["shard"], mesh.shape["rep"]),
        mesh=mesh,
        in_specs=(tok, tok, P(("rep", "shard")), w, w, w, P(), P(), P()),
        out_specs=(tok, tok, w, w, w, w, P(), P(), P(), P()),
        check_vma=False,
    )
```

```python
import functools

import jax
import jax.numpy as jnp
import numpy as np
from jax import lax
from jax.experimental import pallas as pl
from jax.experimental.pallas import tpu as pltpu
from jax.sharding import PartitionSpec as P

D = 1024
HEADS = 16
HEAD_DIM = 64
ROT = 32
FF = 4096
T = 1024
STEP = 10

B1 = 0.9
B2 = 0.95
LR = 0.02
DECAY = 0.1
ADAM_EPS = 1e-08
NORM_EPS = 1e-05
GC = 0.7978845608028654
GA = 0.044715
LOG2E = 1.4426950408889634
LN2 = 0.6931471805599453

BF = jnp.bfloat16
F32 = jnp.float32
VLIM = 58 * 1024 * 1024
NN = (((1,), (0,)), ((), ()))
NT = (((1,), (1,)), ((), ()))
TN = (((0,), (0,)), ((), ()))
TT = (((0,), (1,)), ((), ()))
TILE = 512
SIZES = (2048, 1024, 1024)
MB = 1024
TB = 256
PT = 512
FT = 256


def mm(a, b, dims=NN):
    return lax.dot_general(a, b, dims, preferred_element_type=F32)


def params():
    return pltpu.CompilerParams(
        dimension_semantics=("arbitrary",), vmem_limit_bytes=VLIM
    )


def once(shape):
    return pl.BlockSpec(shape, lambda *_: (0,) * len(shape), pipeline_mode=pl.Buffered(1))


def cost(us):
    return pl.CostEstimate(flops=int(us * 1.15e9), bytes_accessed=1024, transcendentals=0)


def prep_kernel(hr, blocks, ids, x_ref, c_ref, g_ref, b_ref, n_ref, nt_ref, d_ref, dt_ref, db_ref, s_ref):
    i = pl.program_id(0)
    x = x_ref[...].astype(F32)
    mean = jnp.mean(x, -1, keepdims=True)
    xc = x - mean
    var = jnp.mean(xc * xc, -1, keepdims=True)
    n = xc * lax.rsqrt(var + NORM_EPS) * g_ref[...] + b_ref[...]
    n_ref[...] = n.astype(BF)
    row = i * TB + lax.broadcasted_iota(jnp.int32, (TB, 1), 0)
    dy = jnp.where(row < ids[0], c_ref[...].astype(F32), 0.0)
    d_ref[...] = dy.astype(BF)

    @pl.when(i == 0)
    def _():
        db_ref[...] = jnp.zeros_like(db_ref)

    db_ref[...] += jnp.sum(dy, 0, keepdims=True)
    for val, out in ((n, nt_ref), (dy, dt_ref)):
        s_ref[...] = val.T.astype(BF)
        for b in range(2 * blocks):
            off = pl.multiple_of(ids[1 + b], hr)
            out[b * hr : (b + 1) * hr, :] = s_ref[pl.ds(off, hr), :]


def prep(ids, x, cot, gain, shift, hr, blocks):
    row = lambda i, *_: (i, 0)
    col = lambda i, *_: (0, i)
    fix = lambda i, *_: (0, 0)
    return pl.pallas_call(
        functools.partial(prep_kernel, hr, blocks),
        grid_spec=pltpu.PrefetchScalarGridSpec(
            num_scalar_prefetch=1,
            grid=(T // TB,),
            in_specs=[
                pl.BlockSpec((TB, D), row),
                pl.BlockSpec((TB, D), row),
                pl.BlockSpec((1, D), fix),
                pl.BlockSpec((1, D), fix),
            ],
            out_specs=[
                pl.BlockSpec((TB, D), row),
                pl.BlockSpec((D, TB), col),
                pl.BlockSpec((TB, D), row),
                pl.BlockSpec((D, TB), col),
                pl.BlockSpec((1, D), fix),
            ],
            scratch_shapes=[pltpu.VMEM((D, TB), BF)],
        ),
        out_shape=[
            jax.ShapeDtypeStruct((T, D), BF),
            jax.ShapeDtypeStruct((D, T), BF),
            jax.ShapeDtypeStruct((T, D), BF),
            jax.ShapeDtypeStruct((D, T), BF),
            jax.ShapeDtypeStruct((1, D), F32),
        ],
        compiler_params=params(),
        cost_estimate=cost(8),
    )(ids, x, cot, gain, shift)


def place(dst, srcs, ids, base):
    for k, src in enumerate(srcs):
        rows = src.shape[0]
        dst[pl.ds(pl.multiple_of(ids[base + k], rows), rows), :] = src[...]


def spread(g, e, mine, near, far):
    a, b = D // 2, 3 * D // 4
    mine[e] = g[:a, :]
    near[...] = g[a:b, :]
    far[e] = g[b:, :]


def grad_shapes(n):
    return [
        jax.ShapeDtypeStruct(v, BF)
        for v in ((2, D // 2, n), (D // 4, n), (D // 4, n), (2, D // 4, n))
    ]


def mlp_kernel(np_, first, ids, n_ref, nt_ref, d_ref, dt_ref, b_ref, *refs):
    win = refs[:np_]
    wout = refs[np_ : 2 * np_]
    refs = refs[2 * np_ :]
    if not first:
        oin, gin = refs[:2]
        refs = refs[2:]
    gm, g0, g1, gf = refs[:4]
    db_ref, o_ref, g_ref, wi, wo, h_s, p_s = refs[4:]
    j = pl.program_id(0)
    place(wi, win, ids, 0)
    place(wo, wout, ids, 0)
    bias = b_ref[...]
    wi_v = wi[...]
    wo_v = wo[...]
    db = jnp.zeros((1, TILE), F32)
    for t in range(T // MB):
        rows = slice(t * MB, (t + 1) * MB)
        pre = mm(n_ref[rows, :], wi_v) + bias
        dh = mm(d_ref[rows, :], wo_v)
        sq = pre * pre
        th = jnp.tanh(GC * pre * (1.0 + GA * sq))
        half = 0.5 * (1.0 + th)
        h = (pre * half).astype(BF)
        slope = half + 0.5 * pre * (1.0 - th * th) * (GC + (3.0 * GA * GC) * sq)
        dp = (dh * slope).astype(BF)
        h_s[rows, :] = h
        p_s[rows, :] = dp
        db = db + jnp.sum(dp.astype(F32), 0, keepdims=True)
        ov = mm(h, wo_v, NT)
        gv = mm(wi_v, dp, NT)

        if first:

            @pl.when(j == 0)
            def _():
                o_ref[rows, :] = ov
                g_ref[:, rows] = gv

        else:

            @pl.when(j == 0)
            def _():
                o_ref[rows, :] = oin[rows, :] + ov
                g_ref[:, rows] = gin[:, rows] + gv

        @pl.when(j > 0)
        def _():
            o_ref[rows, :] += ov
            g_ref[:, rows] += gv

    db_ref[...] = db
    hv = h_s[...]
    pv = p_s[...]
    for e, (left, right) in enumerate(((nt_ref, pv), (dt_ref, hv))):
        spread(mm(left[...], right).astype(BF), e, gm, (g0, g1)[e], gf)


def mlp(ids, n, nt, dy, dyt, bias, weights, pieces, offset, size, acc):
    first = acc is None
    nt_cols = size // TILE
    tall = lambda cols: pl.BlockSpec((T, cols), lambda j, *_: (0, 0))
    own_rows = weights.shape[0]
    in_base = (4 * D + offset) // TILE
    out_base = (4 * D + FF + offset) // TILE
    wspecs = []
    for base_own, base in ((in_base, offset // TILE), (out_base, (FF + offset) // TILE)):
        if own_rows:
            wspecs.append(pl.BlockSpec((own_rows, TILE), lambda j, *_, b=base_own: (0, b + j)))
        for p in pieces:
            wspecs.append(pl.BlockSpec((p.shape[0], TILE), lambda j, *_, b=base: (0, b + j)))
    wargs = [weights, *pieces]
    bb = offset // TILE
    flat = pl.BlockSpec((D // 4, TILE), lambda j, *_: (0, j))
    deep = lambda r: pl.BlockSpec((2, r, TILE), lambda j, *_: (0, 0, j))
    gspecs = [deep(D // 2), flat, flat, deep(D // 4)]
    return pl.pallas_call(
        functools.partial(mlp_kernel, len(wargs), first),
        grid_spec=pltpu.PrefetchScalarGridSpec(
            num_scalar_prefetch=1,
            grid=(nt_cols,),
            in_specs=[
                once((T, D)),
                once((D, T)),
                once((T, D)),
                once((D, T)),
                pl.BlockSpec((1, TILE), lambda j, *_: (0, bb + j)),
                *wspecs,
                *([] if first else [once((T, D)), once((D, T))]),
            ],
            out_specs=[
                *gspecs,
                pl.BlockSpec((1, TILE), lambda j, *_: (0, j)),
                once((T, D)),
                once((D, T)),
            ],
            scratch_shapes=[
                pltpu.VMEM((D, TILE), BF),
                pltpu.VMEM((D, TILE), BF),
                pltpu.VMEM((T, TILE), BF),
                pltpu.VMEM((T, TILE), BF),
            ],
        ),
        out_shape=[
            *grad_shapes(size),
            jax.ShapeDtypeStruct((1, size), F32),
            jax.ShapeDtypeStruct((T, D), F32),
            jax.ShapeDtypeStruct((D, T), F32),
        ],
        compiler_params=params(),
        cost_estimate=cost(43 * size / 2048),
    )(ids, n, nt, dy, dyt, bias, *wargs, *wargs, *([] if first else acc))


def proj_kernel(np_, ids, n_ref, d_ref, cos_ref, sin_ref, *refs):
    wq = refs[:np_]
    wo = refs[np_ : 2 * np_]
    out_ref, dout_ref, w_s, wo_s = refs[2 * np_ :]
    j = pl.program_id(0)
    place(w_s, wq, ids, 0)
    r = mm(w_s[...], n_ref[...], TT)

    def rotated(scale):
        for h in range(PT // HEAD_DIM):
            b = h * HEAD_DIM
            u = r[b : b + 16, :]
            w = r[b + 16 : b + 32, :]
            cs = cos_ref[...]
            sn = sin_ref[...]
            turned = [u * cs - w * sn, w * cs + u * sn, r[b + 32 : b + 64, :]]
            out_ref[b : b + 64, :] = (jnp.concatenate(turned, 0) * scale).astype(BF)

    @pl.when(j < D // PT)
    def _():
        rotated(LOG2E * HEAD_DIM ** (-0.5))

    @pl.when((j >= D // PT) & (j < 2 * D // PT))
    def _():
        rotated(1.0)

    @pl.when(j >= 2 * D // PT)
    def _():
        out_ref[...] = r.astype(BF)

    @pl.when(j == 0)
    def _():
        place(wo_s, wo, ids, 0)
        dout_ref[...] = mm(wo_s[...], d_ref[...], NT).astype(BF)


def proj(ids, n, dy, cos, sin, weights, pieces):
    wargs = [weights, *pieces]
    return pl.pallas_call(
        functools.partial(proj_kernel, len(wargs)),
        grid_spec=pltpu.PrefetchScalarGridSpec(
            num_scalar_prefetch=1,
            grid=(3 * D // PT,),
            in_specs=[
                once((T, D)),
                once((T, D)),
                once((16, T)),
                once((16, T)),
                *[pl.BlockSpec((w.shape[0], PT), lambda j, *_: (0, j)) for w in wargs],
                *[
                    pl.BlockSpec((w.shape[0], D), lambda j, *_: (0, 3), pipeline_mode=pl.Buffered(1))
                    for w in wargs
                ],
            ],
            out_specs=[
                pl.BlockSpec((PT, T), lambda j, *_: (j, 0)),
                once((D, T)),
            ],
            scratch_shapes=[pltpu.VMEM((D, PT), BF), pltpu.VMEM((D, D), BF)],
        ),
        out_shape=[
            jax.ShapeDtypeStruct((3 * D, T), BF),
            jax.ShapeDtypeStruct((D, T), BF),
        ],
        compiler_params=params(),
        cost_estimate=cost(20),
    )(ids, n, dy, cos, sin, *wargs, *wargs)


QB = 512
HPS = 2


def attn_kernel(n_alias, len_ref, q_ref, k_ref, v_ref, do_ref, cos_ref, sin_ref, *refs):
    o_ref, dq_ref, dk_ref, dv_ref = refs[n_alias:]
    sub = lax.broadcasted_iota(jnp.int32, (HEAD_DIM, T), 0)
    lane = lax.broadcasted_iota(jnp.int32, (HEAD_DIM, T), 1)
    bias = jnp.where((sub == 0) & (lane >= len_ref[0]), -1e30, 0.0)
    ones = jnp.where(sub == 0, 1.0, 0.0).astype(BF)
    none = jnp.zeros((HEAD_DIM, T), F32)
    ki = lax.broadcasted_iota(jnp.int32, (QB, QB), 0)
    qi = lax.broadcasted_iota(jnp.int32, (QB, QB), 1)

    def unrot(val, cs, sn, out, base, cols):
        a = val[0:16, :]
        b = val[16:32, :]
        turned = [a * cs + b * sn, b * cs - a * sn, val[32:64, :]]
        out[base : base + 64, cols] = jnp.concatenate(turned, 0).astype(BF)

    for h in range(HPS):
        b = h * HEAD_DIM
        hs = slice(b, b + HEAD_DIM)
        q = q_ref[hs, :]
        k = k_ref[hs, :]
        v = v_ref[hs, :]
        qa = jnp.concatenate([q, ones], 0)
        ka = jnp.concatenate([k.astype(F32), bias], 0).T.astype(BF)
        vt = jnp.concatenate([v.astype(F32), none], 0).T.astype(BF)
        dk = [jnp.zeros((HEAD_DIM, QB), F32) for _ in range(T // QB)]
        dv = [jnp.zeros((HEAD_DIM, QB), F32) for _ in range(T // QB)]
        for i in range(T // QB):
            qs = slice(i * QB, (i + 1) * QB)
            kk = (i + 1) * QB
            st = mm(ka[:kk, :], qa[:, qs])
            diag = jnp.where(ki <= qi, st[kk - QB :, :], -1e30)
            st = diag if i == 0 else jnp.concatenate([st[: kk - QB, :], diag], 0)
            e = jnp.exp2(st - jnp.max(st, 0, keepdims=True))
            rl = 1.0 / jnp.sum(e, 0, keepdims=True)
            eb = e.astype(BF)
            ot = mm(v[:, :kk], eb) * rl
            o_ref[hs, qs] = ot.astype(BF)
            dn = (do_ref[hs, qs].astype(F32) * rl).astype(BF)
            delta = jnp.sum(dn.astype(F32) * ot, 0, keepdims=True)
            da = jnp.concatenate([dn, none[:, qs].astype(BF)], 0)
            ds = (e * (mm(vt[:kk, :], da) - delta)).astype(BF)
            dq = mm(k[:, :kk], ds) * (HEAD_DIM ** (-0.5))
            unrot(dq, cos_ref[:, qs], sin_ref[:, qs], dq_ref, b, qs)
            dvi = mm(dn, eb, NT)
            dki = mm(q[:, qs], ds, NT)
            for t in range(i + 1):
                ts = slice(t * QB, (t + 1) * QB)
                dv[t] = dv[t] + dvi[:, ts]
                dk[t] = dk[t] + dki[:, ts]
        for t in range(T // QB):
            ts = slice(t * QB, (t + 1) * QB)
            dv_ref[hs, ts] = dv[t].astype(BF)
            unrot(dk[t] * LN2, cos_ref[:, ts], sin_ref[:, ts], dk_ref, b, ts)


def attend(length, qkv, dot_, cos, sin, first, heads, before):
    rows = HPS * HEAD_DIM
    steps = HEADS // HPS
    at = first // HPS
    spec = lambda base: pl.BlockSpec((rows, T), lambda h, *_: (base + at + h, 0))
    shape = jax.ShapeDtypeStruct((D, T), BF)
    alias = [] if before is None else list(before)
    return pl.pallas_call(
        functools.partial(attn_kernel, len(alias)),
        grid_spec=pltpu.PrefetchScalarGridSpec(
            num_scalar_prefetch=1,
            grid=(heads // HPS,),
            in_specs=[
                spec(0),
                spec(steps),
                spec(2 * steps),
                spec(0),
                once((16, T)),
                once((16, T)),
            ]
            + [pl.BlockSpec(memory_space=pl.ANY)] * len(alias),
            out_specs=[spec(0)] * 4,
        ),
        out_shape=[shape] * 4,
        input_output_aliases={7 + i: i for i in range(len(alias))},
        compiler_params=params(),
        cost_estimate=cost(46 * heads / HEADS),
    )(length, qkv, qkv, qkv, dot_, cos, sin, *alias)


def agrad_kernel(hr, blocks, ids, nt_ref, dy_ref, o_ref, dq_ref, dk_ref, dv_ref, gm, g0, g1, gf, g_s):
    j = pl.program_id(0)
    for at, (src, near) in enumerate(((dq_ref, g0), (dk_ref, g0), (dv_ref, g1))):

        @pl.when((j >= 2 * at) & (j < 2 * at + 2))
        def _(src=src, near=near):
            spread(mm(nt_ref[...], src[...], NT).astype(BF), 0, gm, near, gf)

    @pl.when(j >= 6)
    def _():
        g_s[...] = mm(o_ref[...], dy_ref[...]).astype(BF)
        rows = [pl.multiple_of(ids[b], hr) for b in range(2 * blocks)]
        spread(jnp.concatenate([g_s[pl.ds(k, hr), :] for k in rows], 0), 0, gm, g1, gf)


def attn_grads(ids, nt, dy, ot, dq, dk, dv, hr, blocks):
    def grab(at):
        return pl.BlockSpec((TILE, T), lambda j, *_: (jnp.clip(j - 2 * at, 0, 1), 0))

    deep = lambda r: pl.BlockSpec((1, r, TILE), lambda j, *_: (j // 4, 0, j % 4))
    gspecs = [
        deep(D // 2),
        pl.BlockSpec((D // 4, TILE), lambda j, *_: (0, jnp.minimum(j, 3))),
        pl.BlockSpec((D // 4, TILE), lambda j, *_: (0, jnp.maximum(j - 4, 0))),
        deep(D // 4),
    ]
    return pl.pallas_call(
        functools.partial(agrad_kernel, hr, blocks),
        grid_spec=pltpu.PrefetchScalarGridSpec(
            num_scalar_prefetch=1,
            grid=(4 * D // TILE,),
            in_specs=[
                once((D, T)),
                pl.BlockSpec((T, TILE), lambda j, *_: (0, jnp.clip(j - 6, 0, 1))),
                once((D, T)),
                grab(0),
                grab(1),
                grab(2),
            ],
            out_specs=gspecs,
            scratch_shapes=[pltpu.VMEM((D, TILE), BF)],
        ),
        out_shape=grad_shapes(2 * D),
        compiler_params=params(),
        cost_estimate=cost(17),
    )(ids, nt, dy, ot, dq, dk, dv)


def final_kernel(np_, ids, x_ref, dy_ref, g_ref, bo_ref, o_ref, dq_ref, dk_ref, dv_ref, ao_ref, ag_ref, *refs):
    wq = refs[:np_]
    out_ref, gin_ref, v_ref, w_s = refs[np_:]
    i = pl.program_id(0)

    @pl.when(i == 0)
    def _():
        place(w_s, wq, ids, 1)

    x = x_ref[...].astype(F32)
    row = i * FT + lax.broadcasted_iota(jnp.int32, (FT, 1), 0)
    attn = mm(o_ref[...], w_s[:, 3 * D :], TN)
    out = x + attn + ao_ref[...] + bo_ref[...]
    out_ref[...] = jnp.where(row < ids[0], out, 0.0).astype(BF)
    dn = (
        ag_ref[...]
        + mm(w_s[:, :D], dq_ref[...])
        + mm(w_s[:, D : 2 * D], dk_ref[...])
        + mm(w_s[:, 2 * D : 3 * D], dv_ref[...])
    ).T
    mean = jnp.mean(x, -1, keepdims=True)
    xc = x - mean
    inv = lax.rsqrt(jnp.mean(xc * xc, -1, keepdims=True) + NORM_EPS)
    xh = xc * inv
    g = dn * g_ref[...]
    gx = dn * xh
    ln = inv * (
        g - jnp.mean(g, -1, keepdims=True) - xh * jnp.mean(g * xh, -1, keepdims=True)
    )
    gin_ref[...] = (dy_ref[...].astype(F32) + ln).astype(BF)

    @pl.when(i == 0)
    def _():
        v_ref[...] = jnp.zeros_like(v_ref)

    v_ref[0:1, :] += jnp.sum(gx, 0, keepdims=True)
    v_ref[1:2, :] += jnp.sum(dn, 0, keepdims=True)


def final(ids, x, dy, gain, b_out, ot, dq, dk, dv, acc_o, acc_g, weights, pieces):
    row = pl.BlockSpec((FT, D), lambda i, *_: (i, 0))
    col = pl.BlockSpec((D, FT), lambda i, *_: (0, i))
    vec = pl.BlockSpec((1, D), lambda i, *_: (0, 0))
    wargs = [weights, *pieces]
    return pl.pallas_call(
        functools.partial(final_kernel, len(wargs)),
        grid_spec=pltpu.PrefetchScalarGridSpec(
            num_scalar_prefetch=1,
            grid=(T // FT,),
            in_specs=[
                row,
                row,
                vec,
                vec,
                col,
                col,
                col,
                col,
                row,
                col,
                *[once((w.shape[0], 4 * D)) for w in wargs],
            ],
            out_specs=[row, row, pl.BlockSpec((8, D), lambda i, *_: (0, 0))],
            scratch_shapes=[pltpu.VMEM((D, 4 * D), BF)],
        ),
        out_shape=[
            jax.ShapeDtypeStruct((T, D), BF),
            jax.ShapeDtypeStruct((T, D), BF),
            jax.ShapeDtypeStruct((8, D), F32),
        ],
        compiler_params=params(),
        cost_estimate=cost(20),
    )(ids, x, dy, gain, b_out, ot, dq, dk, dv, acc_o, acc_g, *wargs)


C1 = float(1.0 - np.float32(B1) ** np.float32(STEP))
C2 = float(1.0 - np.float32(B2) ** np.float32(STEP))


def adam_math(g, m, v, w, decay):
    nm = B1 * m + (1.0 - B1) * g
    nv = B2 * v + (1.0 - B2) * g * g
    up = -LR * (nm / C1 / (jnp.sqrt(nv / C2) + ADAM_EPS) + decay * w)
    return nm, nv, up


def adam_kernel(n_alias, first, ids, sm, rm, so, ro, m_ref, v_ref, w_ref, *refs):
    wg_ref, nm_ref, nv_ref, up_ref, end_ref = refs[n_alias:]
    end_ref[...] = jnp.zeros_like(end_ref)
    summed = pl.program_id(0) + first == ids[1]
    hr = sm.shape[0]
    mine = jnp.where(summed, sm[...].astype(F32), rm[...].astype(F32))
    other = jnp.where(summed, so[...].astype(F32), ro[...].astype(F32))
    lead = ids[0] == 0
    for h, g in enumerate((jnp.where(lead, mine, other), jnp.where(lead, other, mine))):
        rows = slice(h * hr, (h + 1) * hr)
        nm, nv, up = adam_math(g, m_ref[rows, :], v_ref[rows, :], w_ref[rows, :].astype(F32), DECAY)
        wg_ref[rows, :] = g
        nm_ref[rows, :] = nm
        nv_ref[rows, :] = nv
        up_ref[rows, :] = up


def adam(ids, grads, cols, m, v, w, outs, first=0, count=2):
    rows, width = m.shape
    hr = rows // 2
    n = grads[0].shape[1]
    AC = 1024 if n % 1024 == 0 else 512
    pick = lambda hit: pl.BlockSpec(
        (hr, AC), lambda p, j, ids: (0, jnp.where((p + first == ids[1]) == hit, j, 0))
    )
    b0, b1 = cols[0] // AC, cols[1] // AC
    big = pl.BlockSpec((rows, AC), lambda p, j, ids: (0, jnp.where(p + first == 0, b0, b1) + j))
    alias = [] if outs is None else list(outs)
    return pl.pallas_call(
        functools.partial(adam_kernel, len(alias), first),
        grid_spec=pltpu.PrefetchScalarGridSpec(
            num_scalar_prefetch=1,
            grid=(count, n // AC),
            in_specs=[pick(True), pick(False), pick(True), pick(False), big, big, big]
            + [pl.BlockSpec(memory_space=pl.ANY)] * len(alias),
            out_specs=[big] * 4 + [pl.BlockSpec((8, 128), lambda p, j, ids: (0, 0))],
        ),
        out_shape=[jax.ShapeDtypeStruct((rows, width), F32)] * 4
        + [jax.ShapeDtypeStruct((8, 128), F32)],
        input_output_aliases={8 + i: i for i in range(len(alias))},
        compiler_params=pltpu.CompilerParams(
            dimension_semantics=("arbitrary", "arbitrary"), vmem_limit_bytes=VLIM
        ),
        cost_estimate=cost(6 * count * n / 2048),
    )(ids, *grads, m, v, w, *alias)


def after(values, *waits):
    flat = lax.optimization_barrier((*values, *waits))
    return list(flat[: len(values)])


def on_device(shards, reps, hidden_in, cotangent, lengths, weights, moment_m, moment_v, vectors, vector_m, vector_v):
    s = lax.axis_index("shard")
    rep = lax.axis_index("rep")
    c = rep % 2
    z = rep // 2
    zs = reps // 2
    swap = [(i, i ^ 1) for i in range(reps)]
    rows = weights.shape[0]
    hr = rows // 2
    i32 = jnp.int32
    cube = shards == 4 and zs & (zs - 1) == 0 and zs >= 4
    xn = [(i, i ^ 1) for i in range(shards)]
    yn = [(i, i ^ 2) for i in range(shards)]
    zsteps = [3] + [1 << k for k in range(2, 16) if 1 << k < zs]
    zn = lambda bit: [(i, i ^ (2 * bit)) for i in range(reps)]
    own = ((z ^ (z // 2)) % 2) if cube else jnp.int32(0)

    if cube:
        y_rows = [(s ^ r) * rows for r in (2, 3, 0, 1)]
    else:
        y_rows = [r * rows for r in range(shards)]
    cut = lambda at: [b + c * hr for b in at] + [b + (1 - c) * hr for b in at]
    y_off = cut(y_rows)
    stack = lambda *v: jnp.stack([jnp.asarray(x, i32) for x in v])
    length = lengths.astype(i32)
    gain = vectors[:D].reshape(1, D)
    shift = vectors[D : 2 * D].reshape(1, D)
    b_out = vectors[2 * D : 3 * D].reshape(1, D)
    b_in = vectors[3 * D :].reshape(1, FF)
    half_w = lax.dynamic_slice_in_dim(weights, c * hr, hr, 0)

    n, nt, dy, dyt, db_out = prep(
        stack(length[0], *y_off), hidden_in, cotangent, gain, shift, hr, shards
    )

    def part_of(cols):
        return jnp.concatenate([half_w[:, a:b] for a, b in cols], 1)

    q = hr // 2

    def gather_first(part):
        a, b = part[:q], part[q:]
        return [
            lax.ppermute(p, "shard", way) for p, way in ((a, xn), (b, yn), (b, xn), (a, yn))
        ]

    def gather_second(first):
        return [lax.ppermute(first[0], "shard", yn), lax.ppermute(first[1], "shard", xn)]

    def swapped(mine):
        return mine + [lax.ppermute(p, "rep", swap) for p in mine]

    def gather_whole(part):
        full = lax.all_gather(part, "shard", axis=0, tiled=True)
        other = lax.ppermute(full, "rep", swap)
        return [p[b * hr : (b + 1) * hr] for p in (full, other) for b in range(shards)]

    offsets = [0]
    for size in SIZES:
        offsets.append(offsets[-1] + size)
    apart, fpart = part_of([(0, 4 * D)]), part_of([(4 * D, 4 * D + 2 * FF)])
    if cube:
        base = [(s ^ r) * rows + e * q for r, e in ((1, 0), (2, 1), (1, 1), (2, 0), (3, 0), (3, 1))]
        offs = [b + c * hr for b in base] + [b + (1 - c) * hr for b in base]
        one = gather_first(apart)
        one[:2] = after(one[:2], n)
        one = one + gather_second(one)
        (fpart,) = after([fpart], *one)
        apieces = swapped(one)
        two = gather_first(fpart)
    else:
        offs = cut([b * rows for b in range(shards)])
        apieces = gather_whole(apart)
        two = gather_whole(fpart)
    piece_off = stack(s * rows, *offs)
    len_piece_off = stack(length[0], s * rows, *offs)

    add = lambda *v: sum(x.astype(F32) for x in v).astype(BF)

    class Reduce:
        def __init__(self, grads):
            self.mine = grads[0]
            self.got = [lax.ppermute(g, "rep", swap) for g in grads[1:]]
            self.at = 0
            self.sums = None
            self.brought = []

        def settle(self, last):
            if self.brought:
                self.brought = after(self.brought, last)

        def step(self):
            self.at += 1
            k = self.at
            m, far, old = self.mine, self.got[2], self.brought
            if not cube:
                groups = [[2 * j + e for j in range(zs)] for e in range(2)]
                both = add(m, jnp.concatenate([jnp.stack(self.got[:2]), far], 1))
                both = lax.psum_scatter(both, "shard", scatter_dimension=1, tiled=True)
                both = lax.psum(both, "rep", axis_index_groups=groups)
                self.sums = (both[0], both[1])
                return [], []
            if k == 1:
                sent = add(m[:, : 2 * hr], jnp.stack(self.got[:2]))
                way = ("shard", yn)
            elif k == 2:
                self.first = old[0]
                sent = add(m[:, 3 * hr :], far[:, hr:], old[0][:, hr:])
                way = ("shard", xn)
            elif k == 3:
                total = add(m[:, 2 * hr : 3 * hr], far[:, :hr], self.first[:, :hr], old[0])
                lead = own == 0
                sent = jnp.where(lead, total[1], total[0])
                self.keep = jnp.where(lead, total[0], total[1])
                way = ("rep", zn(1))
            else:
                sent = self.keep = add(self.keep, old[0])
                last = k == 4 + len(zsteps)
                way = ("rep", zn(1 if last else zsteps[k - 4]))
            self.brought = [lax.ppermute(sent, *way)]
            if k == 4 + len(zsteps):
                self.sums = (self.keep, self.brought[0])
            return [sent], self.brought

        def result(self):
            while self.sums is None:
                self.step()
            return [*self.sums, *[lax.ppermute(v, "rep", swap) for v in self.sums]]

    flight = []

    def turn(values, last, *steps):
        nonlocal flight
        waits = flight
        flight = []
        for red in steps:
            if red.sums is None:
                red.settle(last)
                moved = red.step()
                waits = waits + moved[0]
                flight = flight + moved[1]
        return after(values, *waits) if waits else list(values)

    inv_freq = jnp.power(F32(10000.0), -jnp.arange(0, ROT, 2, dtype=F32) / ROT)
    angles = inv_freq[:, None] * jnp.arange(T, dtype=F32)[None, :]
    cos, sin = jnp.cos(angles), jnp.sin(angles)
    qkv, dot_ = proj(piece_off, n, dy, cos, sin, weights, apieces)
    half = HEADS // 2
    heads = attend(length, qkv, dot_, cos, sin, 0, half, None)
    if cube:
        *two, qkv = after([*two, qkv], heads[0])
        three = gather_second(two)
        across = [lax.ppermute(v, "rep", swap) for v in two[:2]]
    ot, dq, dk, dv = attend(length, qkv, dot_, cos, sin, half, half, heads)
    dyg = dy
    if cube:
        (dyg,) = after([dy], ot, *three, *across)
        rest = after(two[2:] + three, ot)
        across += [lax.ppermute(v, "rep", swap) for v in rest]
        fpieces = two + three + across
    else:
        fpieces = two
    reds = [Reduce(attn_grads(stack(*y_off), nt, dyg, ot, dq, dk, dv, hr, shards))]
    places = [(0, 2 * D)]
    acc = None
    dbs = []
    nk = n
    for at, size in zip(offsets, SIZES):
        (nk,) = turn([nk], dbs[-1] if dbs else dv, *reds)
        *grads, db_in, acc_o, acc_g = mlp(
            piece_off, nk, nt, dy, dyt, b_in, weights, fpieces, at, size, acc
        )
        acc = (acc_o, acc_g)
        dbs.append(db_in)
        reds.append(Reduce(grads))
        places.append((4 * D + at, 4 * D + FF + at))

    (ot,) = turn([ot], dbs[-1], *reds)
    out, grad_in, vsum = final(
        len_piece_off, hidden_in, dy, gain, b_out, ot, dq, dk, dv, *acc, weights, apieces
    )
    core = stack(c, own)
    def push(last, *steps):
        waits = []
        for red in steps:
            if red.sums is None:
                red.settle(last)
                waits = waits + red.step()[0]
        return after([core], *waits)[0] if waits else core

    args = moment_m, moment_v, weights
    vec = jnp.concatenate([vsum[0], vsum[1], db_out[0], *[d[0] for d in dbs]])
    if cube:
        vec = vec.reshape(-1, 128)
        hops = [("rep", swap), ("shard", xn), ("shard", yn)]
        hops += [("rep", zn(bit)) for bit in [1] + zsteps]
    else:
        vec = lax.psum(vec, ("rep", "shard"))
        hops = []

    def hop(last, count=1):
        nonlocal vec
        for _ in range(count):
            if hops:
                (vec,) = after([vec], last)
                vec = vec + lax.ppermute(vec, *hops.pop(0))

    hop(vsum)
    ids = push(vsum, *reds)
    done = reds[0].result()
    *big, end = adam(ids, done, places[0], *args, None, 0, 1)
    hop(end)
    ids = push(end, *reds[1:])
    *big, end = adam(ids, done, places[0], *args, big, 1, 1)
    hop(end)
    ids = push(end, *reds[2:])
    done = reds[1].result()
    *big, end = adam(ids, done, places[1], *args, big, 0, 1)
    hop(end)
    ids = push(end, *reds[2:])
    *big, end = adam(ids, done, places[1], *args, big, 1, 1)
    hop(end, len(hops))
    for red, place_ in zip(reds[2:], places[2:]):
        *big, end = adam(core, red.result(), place_, *args, big)
    vec = vec.reshape(-1)
    vm, vv, vu = adam_math(vec, vector_m, vector_v, vectors, 0.0)
    return (out, grad_in, *big, vec, vm, vv, vu)


def solution(mesh):
    tok = P(("rep", "shard"), None)
    w = P("shard", None)
    return jax.shard_map(
        functools.partial(on_device, mesh.shape["shard"], mesh.shape["rep"]),
        mesh=mesh,
        in_specs=(tok, tok, P(("rep", "shard")), w, w, w, P(), P(), P()),
        out_specs=(tok, tok, w, w, w, w, P(), P(), P(), P()),
        check_vma=False,
    )
```

```python
import functools

import jax
import jax.numpy as jnp
import numpy as np
from jax import lax
from jax.experimental import pallas as pl
from jax.experimental.pallas import tpu as pltpu
from jax.sharding import PartitionSpec as P

D = 1024
HEADS = 16
HEAD_DIM = 64
ROT = 32
FF = 4096
T = 1024
STEP = 10

B1 = 0.9
B2 = 0.95
LR = 0.02
DECAY = 0.1
ADAM_EPS = 1e-08
NORM_EPS = 1e-05
GC = 0.7978845608028654
GA = 0.044715
LOG2E = 1.4426950408889634
LN2 = 0.6931471805599453

BF = jnp.bfloat16
F32 = jnp.float32
VLIM = 58 * 1024 * 1024
NN = (((1,), (0,)), ((), ()))
NT = (((1,), (1,)), ((), ()))
TN = (((0,), (0,)), ((), ()))
TT = (((0,), (1,)), ((), ()))
TILE = 512
SIZES = (2048, 1024, 1024)
MB = 1024
MT = 512
TB = 256
PT = 512
FT = 256


def mm(a, b, dims=NN):
    return lax.dot_general(a, b, dims, preferred_element_type=F32)


def params():
    return pltpu.CompilerParams(
        dimension_semantics=("arbitrary",), vmem_limit_bytes=VLIM
    )


def once(shape):
    return pl.BlockSpec(shape, lambda *_: (0,) * len(shape), pipeline_mode=pl.Buffered(1))


def cost(us):
    return pl.CostEstimate(flops=int(us * 1.15e9), bytes_accessed=1024, transcendentals=0)


def prep_kernel(hr, blocks, ids, x_ref, c_ref, g_ref, b_ref, n_ref, nt_ref, d_ref, dt_ref, db_ref, s_ref):
    i = pl.program_id(0)
    x = x_ref[...].astype(F32)
    mean = jnp.mean(x, -1, keepdims=True)
    xc = x - mean
    var = jnp.mean(xc * xc, -1, keepdims=True)
    n = xc * lax.rsqrt(var + NORM_EPS) * g_ref[...] + b_ref[...]
    n_ref[...] = n.astype(BF)
    row = i * TB + lax.broadcasted_iota(jnp.int32, (TB, 1), 0)
    dy = jnp.where(row < ids[0], c_ref[...].astype(F32), 0.0)
    d_ref[...] = dy.astype(BF)

    @pl.when(i == 0)
    def _():
        db_ref[...] = jnp.zeros_like(db_ref)

    db_ref[...] += jnp.sum(dy, 0, keepdims=True)
    for val, out in ((n, nt_ref), (dy, dt_ref)):
        s_ref[...] = val.T.astype(BF)
        for b in range(2 * blocks):
            off = pl.multiple_of(ids[1 + b], hr)
            out[b * hr : (b + 1) * hr, :] = s_ref[pl.ds(off, hr), :]


def prep(ids, x, cot, gain, shift, hr, blocks):
    row = lambda i, *_: (i, 0)
    col = lambda i, *_: (0, i)
    fix = lambda i, *_: (0, 0)
    return pl.pallas_call(
        functools.partial(prep_kernel, hr, blocks),
        grid_spec=pltpu.PrefetchScalarGridSpec(
            num_scalar_prefetch=1,
            grid=(T // TB,),
            in_specs=[
                pl.BlockSpec((TB, D), row),
                pl.BlockSpec((TB, D), row),
                pl.BlockSpec((1, D), fix),
                pl.BlockSpec((1, D), fix),
            ],
            out_specs=[
                pl.BlockSpec((TB, D), row),
                pl.BlockSpec((D, TB), col),
                pl.BlockSpec((TB, D), row),
                pl.BlockSpec((D, TB), col),
                pl.BlockSpec((1, D), fix),
            ],
            scratch_shapes=[pltpu.VMEM((D, TB), BF)],
        ),
        out_shape=[
            jax.ShapeDtypeStruct((T, D), BF),
            jax.ShapeDtypeStruct((D, T), BF),
            jax.ShapeDtypeStruct((T, D), BF),
            jax.ShapeDtypeStruct((D, T), BF),
            jax.ShapeDtypeStruct((1, D), F32),
        ],
        compiler_params=params(),
        cost_estimate=cost(8),
    )(ids, x, cot, gain, shift)


def place(dst, srcs, ids, base):
    for k, src in enumerate(srcs):
        rows = src.shape[0]
        dst[pl.ds(pl.multiple_of(ids[base + k], rows), rows), :] = src[...]


def spread(g, e, mine, near, far):
    a, b = D // 2, 3 * D // 4
    mine[e] = g[:a, :]
    near[...] = g[a:b, :]
    far[e] = g[b:, :]


def grad_shapes(n):
    return [
        jax.ShapeDtypeStruct(v, BF)
        for v in ((2, D // 2, n), (D // 4, n), (D // 4, n), (2, D // 4, n))
    ]


def mlp_kernel(np_, first, ids, n_ref, nt_ref, d_ref, dt_ref, b_ref, *refs):
    win = refs[:np_]
    wout = refs[np_ : 2 * np_]
    refs = refs[2 * np_ :]
    if not first:
        oin, gin = refs[:2]
        refs = refs[2:]
    gm, g0, g1, gf = refs[:4]
    db_ref, o_out, g_out, wi, wo, h_s, p_s, o_ref, g_ref = refs[4:]
    j = pl.program_id(0)
    place(wi, win, ids, 0)
    place(wo, wout, ids, 0)
    bias = b_ref[...]
    wi_v = wi[...]
    wo_v = wo[...]
    db = jnp.zeros((1, MT), F32)
    for t in range(T // MB):
        rows = slice(t * MB, (t + 1) * MB)
        pre = mm(n_ref[rows, :], wi_v) + bias
        dh = mm(d_ref[rows, :], wo_v)
        sq = pre * pre
        th = jnp.tanh(GC * pre * (1.0 + GA * sq))
        half = 0.5 * (1.0 + th)
        h = (pre * half).astype(BF)
        slope = half + 0.5 * pre * (1.0 - th * th) * (GC + (3.0 * GA * GC) * sq)
        dp = (dh * slope).astype(BF)
        h_s[rows, :] = h
        p_s[rows, :] = dp
        db = db + jnp.sum(dp.astype(F32), 0, keepdims=True)
        ov = mm(h, wo_v, NT)
        gv = mm(wi_v, dp, NT)

        if first:

            @pl.when(j == 0)
            def _():
                o_ref[rows, :] = ov
                g_ref[:, rows] = gv

        else:

            @pl.when(j == 0)
            def _():
                o_ref[rows, :] = oin[rows, :].astype(F32) + ov
                g_ref[:, rows] = gin[:, rows].astype(F32) + gv

        @pl.when(j > 0)
        def _():
            o_ref[rows, :] += ov
            g_ref[:, rows] += gv

    @pl.when(j == pl.num_programs(0) - 1)
    def _():
        o_out[...] = o_ref[...].astype(BF)
        g_out[...] = g_ref[...].astype(BF)

    db_ref[...] = db
    hv = h_s[...]
    pv = p_s[...]
    for e, (left, right) in enumerate(((nt_ref, pv), (dt_ref, hv))):
        spread(mm(left[...], right).astype(BF), e, gm, (g0, g1)[e], gf)


def mlp(ids, n, nt, dy, dyt, bias, weights, pieces, offset, size, acc):
    first = acc is None
    nt_cols = size // MT
    tall = lambda cols: pl.BlockSpec((T, cols), lambda j, *_: (0, 0))
    own_rows = weights.shape[0]
    in_base = (4 * D + offset) // MT
    out_base = (4 * D + FF + offset) // MT
    wspecs = []
    for base_own, base in ((in_base, offset // MT), (out_base, (FF + offset) // MT)):
        if own_rows:
            wspecs.append(pl.BlockSpec((own_rows, MT), lambda j, *_, b=base_own: (0, b + j)))
        for p in pieces:
            wspecs.append(pl.BlockSpec((p.shape[0], MT), lambda j, *_, b=base: (0, b + j)))
    wargs = [weights, *pieces]
    bb = offset // MT
    flat = pl.BlockSpec((D // 4, MT), lambda j, *_: (0, j))
    deep = lambda r: pl.BlockSpec((2, r, MT), lambda j, *_: (0, 0, j))
    gspecs = [deep(D // 2), flat, flat, deep(D // 4)]
    return pl.pallas_call(
        functools.partial(mlp_kernel, len(wargs), first),
        grid_spec=pltpu.PrefetchScalarGridSpec(
            num_scalar_prefetch=1,
            grid=(nt_cols,),
            in_specs=[
                once((T, D)),
                once((D, T)),
                once((T, D)),
                once((D, T)),
                pl.BlockSpec((1, MT), lambda j, *_: (0, bb + j)),
                *wspecs,
                *([] if first else [once((T, D)), once((D, T))]),
            ],
            out_specs=[
                *gspecs,
                pl.BlockSpec((1, MT), lambda j, *_: (0, j)),
                once((T, D)),
                once((D, T)),
            ],
            scratch_shapes=[
                pltpu.VMEM((D, MT), BF),
                pltpu.VMEM((D, MT), BF),
                pltpu.VMEM((T, MT), BF),
                pltpu.VMEM((T, MT), BF),
                pltpu.VMEM((T, D), F32),
                pltpu.VMEM((D, T), F32),
            ],
        ),
        out_shape=[
            *grad_shapes(size),
            jax.ShapeDtypeStruct((1, size), F32),
            jax.ShapeDtypeStruct((T, D), BF),
            jax.ShapeDtypeStruct((D, T), BF),
        ],
        compiler_params=params(),
        cost_estimate=cost(41 * size / 2048),
    )(ids, n, nt, dy, dyt, bias, *wargs, *wargs, *([] if first else acc))


def proj_kernel(np_, ids, n_ref, d_ref, cos_ref, sin_ref, *refs):
    wq = refs[:np_]
    wo = refs[np_ : 2 * np_]
    out_ref, dout_ref, w_s, wo_s = refs[2 * np_ :]
    j = pl.program_id(0)
    place(w_s, wq, ids, 0)
    r = mm(w_s[...], n_ref[...], TT)

    def rotated(scale):
        for h in range(PT // HEAD_DIM):
            b = h * HEAD_DIM
            u = r[b : b + 16, :]
            w = r[b + 16 : b + 32, :]
            cs = cos_ref[...]
            sn = sin_ref[...]
            turned = [u * cs - w * sn, w * cs + u * sn, r[b + 32 : b + 64, :]]
            out_ref[b : b + 64, :] = (jnp.concatenate(turned, 0) * scale).astype(BF)

    @pl.when(j < D // PT)
    def _():
        rotated(LOG2E * HEAD_DIM ** (-0.5))

    @pl.when((j >= D // PT) & (j < 2 * D // PT))
    def _():
        rotated(1.0)

    @pl.when(j >= 2 * D // PT)
    def _():
        out_ref[...] = r.astype(BF)

    @pl.when(j == 0)
    def _():
        place(wo_s, wo, ids, 0)
        dout_ref[...] = mm(wo_s[...], d_ref[...], NT).astype(BF)


def proj(ids, n, dy, cos, sin, weights, pieces):
    wargs = [weights, *pieces]
    return pl.pallas_call(
        functools.partial(proj_kernel, len(wargs)),
        grid_spec=pltpu.PrefetchScalarGridSpec(
            num_scalar_prefetch=1,
            grid=(3 * D // PT,),
            in_specs=[
                once((T, D)),
                once((T, D)),
                once((16, T)),
                once((16, T)),
                *[pl.BlockSpec((w.shape[0], PT), lambda j, *_: (0, j)) for w in wargs],
                *[
                    pl.BlockSpec((w.shape[0], D), lambda j, *_: (0, 3), pipeline_mode=pl.Buffered(1))
                    for w in wargs
                ],
            ],
            out_specs=[
                pl.BlockSpec((PT, T), lambda j, *_: (j, 0)),
                once((D, T)),
            ],
            scratch_shapes=[pltpu.VMEM((D, PT), BF), pltpu.VMEM((D, D), BF)],
        ),
        out_shape=[
            jax.ShapeDtypeStruct((3 * D, T), BF),
            jax.ShapeDtypeStruct((D, T), BF),
        ],
        compiler_params=params(),
        cost_estimate=cost(20),
    )(ids, n, dy, cos, sin, *wargs, *wargs)


QB = 512
HPS = 2


def attn_kernel(n_alias, len_ref, q_ref, k_ref, v_ref, do_ref, cos_ref, sin_ref, *refs):
    o_ref, dq_ref, dk_ref, dv_ref = refs[n_alias:]
    sub = lax.broadcasted_iota(jnp.int32, (HEAD_DIM, T), 0)
    lane = lax.broadcasted_iota(jnp.int32, (HEAD_DIM, T), 1)
    bias = jnp.where((sub == 0) & (lane >= len_ref[0]), -1e30, 0.0)
    ones = jnp.where(sub == 0, 1.0, 0.0).astype(BF)
    none = jnp.zeros((HEAD_DIM, T), F32)
    ki = lax.broadcasted_iota(jnp.int32, (QB, QB), 0)
    qi = lax.broadcasted_iota(jnp.int32, (QB, QB), 1)

    def unrot(val, cs, sn, out, base, cols):
        a = val[0:16, :]
        b = val[16:32, :]
        turned = [a * cs + b * sn, b * cs - a * sn, val[32:64, :]]
        out[base : base + 64, cols] = jnp.concatenate(turned, 0).astype(BF)

    for h in range(HPS):
        b = h * HEAD_DIM
        hs = slice(b, b + HEAD_DIM)
        q = q_ref[hs, :]
        k = k_ref[hs, :]
        v = v_ref[hs, :]
        qa = jnp.concatenate([q, ones], 0)
        ka = jnp.concatenate([k.astype(F32), bias], 0).T.astype(BF)
        vt = jnp.concatenate([v.astype(F32), none], 0).T.astype(BF)
        dk = [jnp.zeros((HEAD_DIM, QB), F32) for _ in range(T // QB)]
        dv = [jnp.zeros((HEAD_DIM, QB), F32) for _ in range(T // QB)]
        for i in range(T // QB):
            qs = slice(i * QB, (i + 1) * QB)
            kk = (i + 1) * QB
            st = mm(ka[:kk, :], qa[:, qs])
            diag = jnp.where(ki <= qi, st[kk - QB :, :], -1e30)
            st = diag if i == 0 else jnp.concatenate([st[: kk - QB, :], diag], 0)
            e = jnp.exp2(st - jnp.max(st, 0, keepdims=True))
            rl = 1.0 / jnp.sum(e, 0, keepdims=True)
            eb = e.astype(BF)
            ot = mm(v[:, :kk], eb) * rl
            o_ref[hs, qs] = ot.astype(BF)
            dn = (do_ref[hs, qs].astype(F32) * rl).astype(BF)
            delta = jnp.sum(dn.astype(F32) * ot, 0, keepdims=True)
            da = jnp.concatenate([dn, none[:, qs].astype(BF)], 0)
            ds = (e * (mm(vt[:kk, :], da) - delta)).astype(BF)
            dq = mm(k[:, :kk], ds) * (HEAD_DIM ** (-0.5))
            unrot(dq, cos_ref[:, qs], sin_ref[:, qs], dq_ref, b, qs)
            dvi = mm(dn, eb, NT)
            dki = mm(q[:, qs], ds, NT)
            for t in range(i + 1):
                ts = slice(t * QB, (t + 1) * QB)
                dv[t] = dv[t] + dvi[:, ts]
                dk[t] = dk[t] + dki[:, ts]
        for t in range(T // QB):
            ts = slice(t * QB, (t + 1) * QB)
            dv_ref[hs, ts] = dv[t].astype(BF)
            unrot(dk[t] * LN2, cos_ref[:, ts], sin_ref[:, ts], dk_ref, b, ts)


def attend(length, qkv, dot_, cos, sin, first, heads, before):
    rows = HPS * HEAD_DIM
    steps = HEADS // HPS
    at = first // HPS
    spec = lambda base: pl.BlockSpec((rows, T), lambda h, *_: (base + at + h, 0))
    shape = jax.ShapeDtypeStruct((D, T), BF)
    alias = [] if before is None else list(before)
    return pl.pallas_call(
        functools.partial(attn_kernel, len(alias)),
        grid_spec=pltpu.PrefetchScalarGridSpec(
            num_scalar_prefetch=1,
            grid=(heads // HPS,),
            in_specs=[
                spec(0),
                spec(steps),
                spec(2 * steps),
                spec(0),
                once((16, T)),
                once((16, T)),
            ]
            + [pl.BlockSpec(memory_space=pl.ANY)] * len(alias),
            out_specs=[spec(0)] * 4,
        ),
        out_shape=[shape] * 4,
        input_output_aliases={7 + i: i for i in range(len(alias))},
        compiler_params=params(),
        cost_estimate=cost(46 * heads / HEADS),
    )(length, qkv, qkv, qkv, dot_, cos, sin, *alias)


def agrad_kernel(hr, blocks, ids, nt_ref, dy_ref, o_ref, dq_ref, dk_ref, dv_ref, gm, g0, g1, gf, g_s):
    j = pl.program_id(0)
    for at, (src, near) in enumerate(((dq_ref, g0), (dk_ref, g0), (dv_ref, g1))):

        @pl.when((j >= 2 * at) & (j < 2 * at + 2))
        def _(src=src, near=near):
            spread(mm(nt_ref[...], src[...], NT).astype(BF), 0, gm, near, gf)

    @pl.when(j >= 6)
    def _():
        g_s[...] = mm(o_ref[...], dy_ref[...]).astype(BF)
        rows = [pl.multiple_of(ids[b], hr) for b in range(2 * blocks)]
        spread(jnp.concatenate([g_s[pl.ds(k, hr), :] for k in rows], 0), 0, gm, g1, gf)


def attn_grads(ids, nt, dy, ot, dq, dk, dv, hr, blocks):
    def grab(at):
        return pl.BlockSpec((TILE, T), lambda j, *_: (jnp.clip(j - 2 * at, 0, 1), 0))

    deep = lambda r: pl.BlockSpec((1, r, TILE), lambda j, *_: (j // 4, 0, j % 4))
    gspecs = [
        deep(D // 2),
        pl.BlockSpec((D // 4, TILE), lambda j, *_: (0, jnp.minimum(j, 3))),
        pl.BlockSpec((D // 4, TILE), lambda j, *_: (0, jnp.maximum(j - 4, 0))),
        deep(D // 4),
    ]
    return pl.pallas_call(
        functools.partial(agrad_kernel, hr, blocks),
        grid_spec=pltpu.PrefetchScalarGridSpec(
            num_scalar_prefetch=1,
            grid=(4 * D // TILE,),
            in_specs=[
                once((D, T)),
                pl.BlockSpec((T, TILE), lambda j, *_: (0, jnp.clip(j - 6, 0, 1))),
                once((D, T)),
                grab(0),
                grab(1),
                grab(2),
            ],
            out_specs=gspecs,
            scratch_shapes=[pltpu.VMEM((D, TILE), BF)],
        ),
        out_shape=grad_shapes(2 * D),
        compiler_params=params(),
        cost_estimate=cost(17),
    )(ids, nt, dy, ot, dq, dk, dv)


def final_kernel(np_, ids, x_ref, dy_ref, g_ref, bo_ref, o_ref, dq_ref, dk_ref, dv_ref, ao_ref, ag_ref, *refs):
    wq = refs[:np_]
    out_ref, gin_ref, v_ref, w_s = refs[np_:]
    i = pl.program_id(0)

    @pl.when(i == 0)
    def _():
        place(w_s, wq, ids, 1)

    x = x_ref[...].astype(F32)
    row = i * FT + lax.broadcasted_iota(jnp.int32, (FT, 1), 0)
    attn = mm(o_ref[...], w_s[:, 3 * D :], TN)
    out = x + attn + ao_ref[...].astype(F32) + bo_ref[...]
    out_ref[...] = jnp.where(row < ids[0], out, 0.0).astype(BF)
    dn = (
        ag_ref[...].astype(F32)
        + mm(w_s[:, :D], dq_ref[...])
        + mm(w_s[:, D : 2 * D], dk_ref[...])
        + mm(w_s[:, 2 * D : 3 * D], dv_ref[...])
    ).T
    mean = jnp.mean(x, -1, keepdims=True)
    xc = x - mean
    inv = lax.rsqrt(jnp.mean(xc * xc, -1, keepdims=True) + NORM_EPS)
    xh = xc * inv
    g = dn * g_ref[...]
    gx = dn * xh
    ln = inv * (
        g - jnp.mean(g, -1, keepdims=True) - xh * jnp.mean(g * xh, -1, keepdims=True)
    )
    gin_ref[...] = (dy_ref[...].astype(F32) + ln).astype(BF)

    @pl.when(i == 0)
    def _():
        v_ref[...] = jnp.zeros_like(v_ref)

    v_ref[0:1, :] += jnp.sum(gx, 0, keepdims=True)
    v_ref[1:2, :] += jnp.sum(dn, 0, keepdims=True)


def final(ids, x, dy, gain, b_out, ot, dq, dk, dv, acc_o, acc_g, weights, pieces):
    row = pl.BlockSpec((FT, D), lambda i, *_: (i, 0))
    col = pl.BlockSpec((D, FT), lambda i, *_: (0, i))
    vec = pl.BlockSpec((1, D), lambda i, *_: (0, 0))
    wargs = [weights, *pieces]
    return pl.pallas_call(
        functools.partial(final_kernel, len(wargs)),
        grid_spec=pltpu.PrefetchScalarGridSpec(
            num_scalar_prefetch=1,
            grid=(T // FT,),
            in_specs=[
                row,
                row,
                vec,
                vec,
                col,
                col,
                col,
                col,
                row,
                col,
                *[once((w.shape[0], 4 * D)) for w in wargs],
            ],
            out_specs=[row, row, pl.BlockSpec((8, D), lambda i, *_: (0, 0))],
            scratch_shapes=[pltpu.VMEM((D, 4 * D), BF)],
        ),
        out_shape=[
            jax.ShapeDtypeStruct((T, D), BF),
            jax.ShapeDtypeStruct((T, D), BF),
            jax.ShapeDtypeStruct((8, D), F32),
        ],
        compiler_params=params(),
        cost_estimate=cost(20),
    )(ids, x, dy, gain, b_out, ot, dq, dk, dv, acc_o, acc_g, *wargs)


C1 = float(1.0 - np.float32(B1) ** np.float32(STEP))
C2 = float(1.0 - np.float32(B2) ** np.float32(STEP))


def adam_math(g, m, v, w, decay):
    nm = B1 * m + (1.0 - B1) * g
    nv = B2 * v + (1.0 - B2) * g * g
    up = -LR * (nm / C1 / (jnp.sqrt(nv / C2) + ADAM_EPS) + decay * w)
    return nm, nv, up


def adam_kernel(n_alias, first, ids, sm, rm, so, ro, m_ref, v_ref, w_ref, *refs):
    wg_ref, nm_ref, nv_ref, up_ref, end_ref = refs[n_alias:]
    end_ref[...] = jnp.zeros_like(end_ref)
    summed = pl.program_id(0) + first == ids[1]
    hr = sm.shape[0]
    mine = jnp.where(summed, sm[...].astype(F32), rm[...].astype(F32))
    other = jnp.where(summed, so[...].astype(F32), ro[...].astype(F32))
    lead = ids[0] == 0
    for h, g in enumerate((jnp.where(lead, mine, other), jnp.where(lead, other, mine))):
        rows = slice(h * hr, (h + 1) * hr)
        nm, nv, up = adam_math(g, m_ref[rows, :], v_ref[rows, :], w_ref[rows, :].astype(F32), DECAY)
        wg_ref[rows, :] = g
        nm_ref[rows, :] = nm
        nv_ref[rows, :] = nv
        up_ref[rows, :] = up


def adam(ids, grads, cols, m, v, w, outs, first=0, count=2):
    rows, width = m.shape
    hr = rows // 2
    n = grads[0].shape[1]
    AC = 1024 if n % 1024 == 0 else 512
    pick = lambda hit: pl.BlockSpec(
        (hr, AC), lambda p, j, ids: (0, jnp.where((p + first == ids[1]) == hit, j, 0))
    )
    b0, b1 = cols[0] // AC, cols[1] // AC
    big = pl.BlockSpec((rows, AC), lambda p, j, ids: (0, jnp.where(p + first == 0, b0, b1) + j))
    alias = [] if outs is None else list(outs)
    return pl.pallas_call(
        functools.partial(adam_kernel, len(alias), first),
        grid_spec=pltpu.PrefetchScalarGridSpec(
            num_scalar_prefetch=1,
            grid=(count, n // AC),
            in_specs=[pick(True), pick(False), pick(True), pick(False), big, big, big]
            + [pl.BlockSpec(memory_space=pl.ANY)] * len(alias),
            out_specs=[big] * 4 + [pl.BlockSpec((8, 128), lambda p, j, ids: (0, 0))],
        ),
        out_shape=[jax.ShapeDtypeStruct((rows, width), F32)] * 4
        + [jax.ShapeDtypeStruct((8, 128), F32)],
        input_output_aliases={8 + i: i for i in range(len(alias))},
        compiler_params=pltpu.CompilerParams(
            dimension_semantics=("arbitrary", "arbitrary"), vmem_limit_bytes=VLIM
        ),
        cost_estimate=cost(6 * count * n / 2048),
    )(ids, *grads, m, v, w, *alias)


def after(values, *waits):
    flat = lax.optimization_barrier((*values, *waits))
    return list(flat[: len(values)])


def on_device(shards, reps, hidden_in, cotangent, lengths, weights, moment_m, moment_v, vectors, vector_m, vector_v):
    s = lax.axis_index("shard")
    rep = lax.axis_index("rep")
    c = rep % 2
    z = rep // 2
    zs = reps // 2
    swap = [(i, i ^ 1) for i in range(reps)]
    rows = weights.shape[0]
    hr = rows // 2
    i32 = jnp.int32
    cube = shards == 4 and zs & (zs - 1) == 0 and zs >= 4
    xn = [(i, i ^ 1) for i in range(shards)]
    yn = [(i, i ^ 2) for i in range(shards)]
    zsteps = [3] + [1 << k for k in range(2, 16) if 1 << k < zs]
    zn = lambda bit: [(i, i ^ (2 * bit)) for i in range(reps)]
    own = ((z ^ (z // 2)) % 2) if cube else jnp.int32(0)

    if cube:
        y_rows = [(s ^ r) * rows for r in (2, 3, 0, 1)]
    else:
        y_rows = [r * rows for r in range(shards)]
    cut = lambda at: [b + c * hr for b in at] + [b + (1 - c) * hr for b in at]
    y_off = cut(y_rows)
    stack = lambda *v: jnp.stack([jnp.asarray(x, i32) for x in v])
    length = lengths.astype(i32)
    gain = vectors[:D].reshape(1, D)
    shift = vectors[D : 2 * D].reshape(1, D)
    b_out = vectors[2 * D : 3 * D].reshape(1, D)
    b_in = vectors[3 * D :].reshape(1, FF)
    half_w = lax.dynamic_slice_in_dim(weights, c * hr, hr, 0)

    n, nt, dy, dyt, db_out = prep(
        stack(length[0], *y_off), hidden_in, cotangent, gain, shift, hr, shards
    )

    def part_of(cols):
        return jnp.concatenate([half_w[:, a:b] for a, b in cols], 1)

    q = hr // 2

    def gather_first(part):
        a, b = part[:q], part[q:]
        return [
            lax.ppermute(p, "shard", way) for p, way in ((a, xn), (b, yn), (b, xn), (a, yn))
        ]

    def gather_second(first):
        return [lax.ppermute(first[0], "shard", yn), lax.ppermute(first[1], "shard", xn)]

    def swapped(mine):
        return mine + [lax.ppermute(p, "rep", swap) for p in mine]

    def gather_whole(part):
        full = lax.all_gather(part, "shard", axis=0, tiled=True)
        other = lax.ppermute(full, "rep", swap)
        return [p[b * hr : (b + 1) * hr] for p in (full, other) for b in range(shards)]

    offsets = [0]
    for size in SIZES:
        offsets.append(offsets[-1] + size)
    apart, fpart = part_of([(0, 4 * D)]), part_of([(4 * D, 4 * D + 2 * FF)])
    if cube:
        base = [(s ^ r) * rows + e * q for r, e in ((1, 0), (2, 1), (1, 1), (2, 0), (3, 0), (3, 1))]
        offs = [b + c * hr for b in base] + [b + (1 - c) * hr for b in base]
        one = gather_first(apart)
        one[:2] = after(one[:2], n)
        one = one + gather_second(one)
        (fpart,) = after([fpart], *one)
        apieces = swapped(one)
        two = gather_first(fpart)
    else:
        offs = cut([b * rows for b in range(shards)])
        apieces = gather_whole(apart)
        two = gather_whole(fpart)
    piece_off = stack(s * rows, *offs)
    len_piece_off = stack(length[0], s * rows, *offs)

    add = lambda *v: sum(x.astype(F32) for x in v).astype(BF)

    class Reduce:
        def __init__(self, grads):
            self.mine = grads[0]
            self.got = [lax.ppermute(g, "rep", swap) for g in grads[1:]]
            self.at = 0
            self.sums = None
            self.brought = []

        def settle(self, last):
            if self.brought:
                self.brought = after(self.brought, last)

        def step(self):
            self.at += 1
            k = self.at
            m, far, old = self.mine, self.got[2], self.brought
            if not cube:
                groups = [[2 * j + e for j in range(zs)] for e in range(2)]
                both = add(m, jnp.concatenate([jnp.stack(self.got[:2]), far], 1))
                both = lax.psum_scatter(both, "shard", scatter_dimension=1, tiled=True)
                both = lax.psum(both, "rep", axis_index_groups=groups)
                self.sums = (both[0], both[1])
                return [], []
            if k == 1:
                sent = add(m[:, : 2 * hr], jnp.stack(self.got[:2]))
                way = ("shard", yn)
            elif k == 2:
                self.first = old[0]
                sent = add(m[:, 3 * hr :], far[:, hr:], old[0][:, hr:])
                way = ("shard", xn)
            elif k == 3:
                total = add(m[:, 2 * hr : 3 * hr], far[:, :hr], self.first[:, :hr], old[0])
                lead = own == 0
                sent = jnp.where(lead, total[1], total[0])
                self.keep = jnp.where(lead, total[0], total[1])
                way = ("rep", zn(1))
            else:
                sent = self.keep = add(self.keep, old[0])
                last = k == 4 + len(zsteps)
                way = ("rep", zn(1 if last else zsteps[k - 4]))
            self.brought = [lax.ppermute(sent, *way)]
            if k == 4 + len(zsteps):
                self.sums = (self.keep, self.brought[0])
            return [sent], self.brought

        def result(self):
            while self.sums is None:
                self.step()
            return [*self.sums, *[lax.ppermute(v, "rep", swap) for v in self.sums]]

    flight = []

    def turn(values, last, *steps):
        nonlocal flight
        waits = flight
        flight = []
        for red in steps:
            if red.sums is None:
                red.settle(last)
                moved = red.step()
                waits = waits + moved[0]
                flight = flight + moved[1]
        return after(values, *waits) if waits else list(values)

    inv_freq = jnp.power(F32(10000.0), -jnp.arange(0, ROT, 2, dtype=F32) / ROT)
    angles = inv_freq[:, None] * jnp.arange(T, dtype=F32)[None, :]
    cos, sin = jnp.cos(angles), jnp.sin(angles)
    qkv, dot_ = proj(piece_off, n, dy, cos, sin, weights, apieces)
    half = HEADS // 2
    heads = attend(length, qkv, dot_, cos, sin, 0, half, None)
    if cube:
        *two, qkv = after([*two, qkv], heads[0])
        three = gather_second(two)
        across = [lax.ppermute(v, "rep", swap) for v in two[:2]]
    ot, dq, dk, dv = attend(length, qkv, dot_, cos, sin, half, half, heads)
    dyg = dy
    if cube:
        (dyg,) = after([dy], ot, *three, *across)
        rest = after(two[2:] + three, ot)
        across += [lax.ppermute(v, "rep", swap) for v in rest]
        fpieces = two + three + across
    else:
        fpieces = two
    reds = [Reduce(attn_grads(stack(*y_off), nt, dyg, ot, dq, dk, dv, hr, shards))]
    places = [(0, 2 * D)]
    acc = None
    dbs = []
    nk = n
    for at, size in zip(offsets, SIZES):
        (nk,) = turn([nk], dbs[-1] if dbs else dv, *reds)
        *grads, db_in, acc_o, acc_g = mlp(
            piece_off, nk, nt, dy, dyt, b_in, weights, fpieces, at, size, acc
        )
        acc = (acc_o, acc_g)
        dbs.append(db_in)
        reds.append(Reduce(grads))
        places.append((4 * D + at, 4 * D + FF + at))

    (ot,) = turn([ot], dbs[-1], *reds)
    out, grad_in, vsum = final(
        len_piece_off, hidden_in, dy, gain, b_out, ot, dq, dk, dv, *acc, weights, apieces
    )
    core = stack(c, own)
    def push(last, *steps):
        waits = []
        for red in steps:
            if red.sums is None:
                red.settle(last)
                waits = waits + red.step()[0]
        return after([core], *waits)[0] if waits else core

    args = moment_m, moment_v, weights
    vec = jnp.concatenate([vsum[0], vsum[1], db_out[0], *[d[0] for d in dbs]])
    if cube:
        vec = vec.reshape(-1, 128)
        hops = [("rep", swap), ("shard", xn), ("shard", yn)]
        hops += [("rep", zn(bit)) for bit in [1] + zsteps]
    else:
        vec = lax.psum(vec, ("rep", "shard"))
        hops = []

    def hop(last, count=1):
        nonlocal vec
        for _ in range(count):
            if hops:
                (vec,) = after([vec], last)
                vec = vec + lax.ppermute(vec, *hops.pop(0))

    hop(vsum)
    ids = push(vsum, *reds)
    done = reds[0].result()
    *big, end = adam(ids, done, places[0], *args, None)
    hop(end)
    ids = push(end, *reds[1:])
    done = reds[1].result()
    *big, end = adam(ids, done, places[1], *args, big, 0, 1)
    hop(end)
    ids = push(end, *reds[2:])
    *big, end = adam(ids, done, places[1], *args, big, 1, 1)
    hop(end, len(hops))
    for red, place_ in zip(reds[2:], places[2:]):
        *big, end = adam(core, red.result(), place_, *args, big)
    vec = vec.reshape(-1)
    vm, vv, vu = adam_math(vec, vector_m, vector_v, vectors, 0.0)
    return (out, grad_in, *big, vec, vm, vv, vu)


def solution(mesh):
    tok = P(("rep", "shard"), None)
    w = P("shard", None)
    return jax.shard_map(
        functools.partial(on_device, mesh.shape["shard"], mesh.shape["rep"]),
        mesh=mesh,
        in_specs=(tok, tok, P(("rep", "shard")), w, w, w, P(), P(), P()),
        out_specs=(tok, tok, w, w, w, w, P(), P(), P(), P()),
        check_vma=False,
    )
```

```python
import functools

import jax
import jax.numpy as jnp
import numpy as np
from jax import lax
from jax.experimental import pallas as pl
from jax.experimental.pallas import tpu as pltpu
from jax.sharding import PartitionSpec as P

D = 1024
HEADS = 16
HEAD_DIM = 64
ROT = 32
FF = 4096
T = 1024
STEP = 10

B1 = 0.9
B2 = 0.95
LR = 0.02
DECAY = 0.1
ADAM_EPS = 1e-08
NORM_EPS = 1e-05
GC = 0.7978845608028654
GA = 0.044715
LOG2E = 1.4426950408889634
LN2 = 0.6931471805599453

BF = jnp.bfloat16
F32 = jnp.float32
VLIM = 58 * 1024 * 1024
NN = (((1,), (0,)), ((), ()))
NT = (((1,), (1,)), ((), ()))
TN = (((0,), (0,)), ((), ()))
TT = (((0,), (1,)), ((), ()))
TILE = 512
SIZES = (1024, 1024, 1024, 1024)
MB = 1024
MT = 512
TB = 256
PT = 512
FT = 256


def mm(a, b, dims=NN):
    return lax.dot_general(a, b, dims, preferred_element_type=F32)


def params():
    return pltpu.CompilerParams(
        dimension_semantics=("arbitrary",), vmem_limit_bytes=VLIM
    )


def once(shape):
    return pl.BlockSpec(shape, lambda *_: (0,) * len(shape), pipeline_mode=pl.Buffered(1))


def cost(us):
    return pl.CostEstimate(flops=int(us * 1.15e9), bytes_accessed=1024, transcendentals=0)


def prep_kernel(hr, blocks, ids, x_ref, c_ref, g_ref, b_ref, n_ref, nt_ref, d_ref, dt_ref, db_ref, s_ref):
    i = pl.program_id(0)
    x = x_ref[...].astype(F32)
    mean = jnp.mean(x, -1, keepdims=True)
    xc = x - mean
    var = jnp.mean(xc * xc, -1, keepdims=True)
    n = xc * lax.rsqrt(var + NORM_EPS) * g_ref[...] + b_ref[...]
    n_ref[...] = n.astype(BF)
    row = i * TB + lax.broadcasted_iota(jnp.int32, (TB, 1), 0)
    dy = jnp.where(row < ids[0], c_ref[...].astype(F32), 0.0)
    d_ref[...] = dy.astype(BF)

    @pl.when(i == 0)
    def _():
        db_ref[...] = jnp.zeros_like(db_ref)

    db_ref[...] += jnp.sum(dy, 0, keepdims=True)
    for val, out in ((n, nt_ref), (dy, dt_ref)):
        s_ref[...] = val.T.astype(BF)
        for b in range(2 * blocks):
            off = pl.multiple_of(ids[1 + b], hr)
            out[b * hr : (b + 1) * hr, :] = s_ref[pl.ds(off, hr), :]


def prep(ids, x, cot, gain, shift, hr, blocks):
    row = lambda i, *_: (i, 0)
    col = lambda i, *_: (0, i)
    fix = lambda i, *_: (0, 0)
    return pl.pallas_call(
        functools.partial(prep_kernel, hr, blocks),
        grid_spec=pltpu.PrefetchScalarGridSpec(
            num_scalar_prefetch=1,
            grid=(T // TB,),
            in_specs=[
                pl.BlockSpec((TB, D), row),
                pl.BlockSpec((TB, D), row),
                pl.BlockSpec((1, D), fix),
                pl.BlockSpec((1, D), fix),
            ],
            out_specs=[
                pl.BlockSpec((TB, D), row),
                pl.BlockSpec((D, TB), col),
                pl.BlockSpec((TB, D), row),
                pl.BlockSpec((D, TB), col),
                pl.BlockSpec((1, D), fix),
            ],
            scratch_shapes=[pltpu.VMEM((D, TB), BF)],
        ),
        out_shape=[
            jax.ShapeDtypeStruct((T, D), BF),
            jax.ShapeDtypeStruct((D, T), BF),
            jax.ShapeDtypeStruct((T, D), BF),
            jax.ShapeDtypeStruct((D, T), BF),
            jax.ShapeDtypeStruct((1, D), F32),
        ],
        compiler_params=params(),
        cost_estimate=cost(8),
    )(ids, x, cot, gain, shift)


def place(dst, srcs, ids, base):
    for k, src in enumerate(srcs):
        rows = src.shape[0]
        dst[pl.ds(pl.multiple_of(ids[base + k], rows), rows), :] = src[...]


def spread(g, e, mine, near, far):
    a, b = D // 2, 3 * D // 4
    mine[e] = g[:a, :]
    near[...] = g[a:b, :]
    far[e] = g[b:, :]


def grad_shapes(n):
    return [
        jax.ShapeDtypeStruct(v, BF)
        for v in ((2, D // 2, n), (D // 4, n), (D // 4, n), (2, D // 4, n))
    ]


def mlp_kernel(np_, first, ids, n_ref, nt_ref, d_ref, dt_ref, b_ref, *refs):
    win = refs[:np_]
    wout = refs[np_ : 2 * np_]
    refs = refs[2 * np_ :]
    if not first:
        oin, gin = refs[:2]
        refs = refs[2:]
    gm, g0, g1, gf = refs[:4]
    db_ref, o_out, g_out, wi, wo, h_s, p_s, o_ref, g_ref = refs[4:]
    j = pl.program_id(0)
    place(wi, win, ids, 0)
    place(wo, wout, ids, 0)
    bias = b_ref[...]
    wi_v = wi[...]
    wo_v = wo[...]
    db = jnp.zeros((1, MT), F32)
    for t in range(T // MB):
        rows = slice(t * MB, (t + 1) * MB)
        pre = mm(n_ref[rows, :], wi_v) + bias
        dh = mm(d_ref[rows, :], wo_v)
        sq = pre * pre
        th = jnp.tanh(GC * pre * (1.0 + GA * sq))
        half = 0.5 * (1.0 + th)
        h = (pre * half).astype(BF)
        slope = half + 0.5 * pre * (1.0 - th * th) * (GC + (3.0 * GA * GC) * sq)
        dp = (dh * slope).astype(BF)
        h_s[rows, :] = h
        p_s[rows, :] = dp
        db = db + jnp.sum(dp.astype(F32), 0, keepdims=True)
        ov = mm(h, wo_v, NT)
        gv = mm(wi_v, dp, NT)

        if first:

            @pl.when(j == 0)
            def _():
                o_ref[rows, :] = ov
                g_ref[:, rows] = gv

        else:

            @pl.when(j == 0)
            def _():
                o_ref[rows, :] = oin[rows, :].astype(F32) + ov
                g_ref[:, rows] = gin[:, rows].astype(F32) + gv

        @pl.when(j > 0)
        def _():
            o_ref[rows, :] += ov
            g_ref[:, rows] += gv

    @pl.when(j == pl.num_programs(0) - 1)
    def _():
        o_out[...] = o_ref[...].astype(BF)
        g_out[...] = g_ref[...].astype(BF)

    db_ref[...] = db
    hv = h_s[...]
    pv = p_s[...]
    for e, (left, right) in enumerate(((nt_ref, pv), (dt_ref, hv))):
        spread(mm(left[...], right).astype(BF), e, gm, (g0, g1)[e], gf)


def mlp(ids, n, nt, dy, dyt, bias, weights, pieces, offset, size, acc):
    first = acc is None
    nt_cols = size // MT
    tall = lambda cols: pl.BlockSpec((T, cols), lambda j, *_: (0, 0))
    own_rows = weights.shape[0]
    in_base = (4 * D + offset) // MT
    out_base = (4 * D + FF + offset) // MT
    wspecs = []
    for base_own, base in ((in_base, offset // MT), (out_base, (FF + offset) // MT)):
        if own_rows:
            wspecs.append(pl.BlockSpec((own_rows, MT), lambda j, *_, b=base_own: (0, b + j)))
        for p in pieces:
            wspecs.append(pl.BlockSpec((p.shape[0], MT), lambda j, *_, b=base: (0, b + j)))
    wargs = [weights, *pieces]
    bb = offset // MT
    flat = pl.BlockSpec((D // 4, MT), lambda j, *_: (0, j))
    deep = lambda r: pl.BlockSpec((2, r, MT), lambda j, *_: (0, 0, j))
    gspecs = [deep(D // 2), flat, flat, deep(D // 4)]
    return pl.pallas_call(
        functools.partial(mlp_kernel, len(wargs), first),
        grid_spec=pltpu.PrefetchScalarGridSpec(
            num_scalar_prefetch=1,
            grid=(nt_cols,),
            in_specs=[
                once((T, D)),
                once((D, T)),
                once((T, D)),
                once((D, T)),
                pl.BlockSpec((1, MT), lambda j, *_: (0, bb + j)),
                *wspecs,
                *([] if first else [once((T, D)), once((D, T))]),
            ],
            out_specs=[
                *gspecs,
                pl.BlockSpec((1, MT), lambda j, *_: (0, j)),
                once((T, D)),
                once((D, T)),
            ],
            scratch_shapes=[
                pltpu.VMEM((D, MT), BF),
                pltpu.VMEM((D, MT), BF),
                pltpu.VMEM((T, MT), BF),
                pltpu.VMEM((T, MT), BF),
                pltpu.VMEM((T, D), F32),
                pltpu.VMEM((D, T), F32),
            ],
        ),
        out_shape=[
            *grad_shapes(size),
            jax.ShapeDtypeStruct((1, size), F32),
            jax.ShapeDtypeStruct((T, D), BF),
            jax.ShapeDtypeStruct((D, T), BF),
        ],
        compiler_params=params(),
        cost_estimate=cost(41 * size / 2048),
    )(ids, n, nt, dy, dyt, bias, *wargs, *wargs, *([] if first else acc))


def proj_kernel(np_, ids, n_ref, d_ref, cos_ref, sin_ref, *refs):
    wq = refs[:np_]
    wo = refs[np_ : 2 * np_]
    out_ref, dout_ref, w_s, wo_s = refs[2 * np_ :]
    j = pl.program_id(0)
    place(w_s, wq, ids, 0)
    r = mm(w_s[...], n_ref[...], TT)

    def rotated(scale):
        for h in range(PT // HEAD_DIM):
            b = h * HEAD_DIM
            u = r[b : b + 16, :]
            w = r[b + 16 : b + 32, :]
            cs = cos_ref[...]
            sn = sin_ref[...]
            turned = [u * cs - w * sn, w * cs + u * sn, r[b + 32 : b + 64, :]]
            out_ref[b : b + 64, :] = (jnp.concatenate(turned, 0) * scale).astype(BF)

    @pl.when(j < D // PT)
    def _():
        rotated(LOG2E * HEAD_DIM ** (-0.5))

    @pl.when((j >= D // PT) & (j < 2 * D // PT))
    def _():
        rotated(1.0)

    @pl.when(j >= 2 * D // PT)
    def _():
        out_ref[...] = r.astype(BF)

    @pl.when(j == 0)
    def _():
        place(wo_s, wo, ids, 0)
        dout_ref[...] = mm(wo_s[...], d_ref[...], NT).astype(BF)


def proj(ids, n, dy, cos, sin, weights, pieces):
    wargs = [weights, *pieces]
    return pl.pallas_call(
        functools.partial(proj_kernel, len(wargs)),
        grid_spec=pltpu.PrefetchScalarGridSpec(
            num_scalar_prefetch=1,
            grid=(3 * D // PT,),
            in_specs=[
                once((T, D)),
                once((T, D)),
                once((16, T)),
                once((16, T)),
                *[pl.BlockSpec((w.shape[0], PT), lambda j, *_: (0, j)) for w in wargs],
                *[
                    pl.BlockSpec((w.shape[0], D), lambda j, *_: (0, 3), pipeline_mode=pl.Buffered(1))
                    for w in wargs
                ],
            ],
            out_specs=[
                pl.BlockSpec((PT, T), lambda j, *_: (j, 0)),
                once((D, T)),
            ],
            scratch_shapes=[pltpu.VMEM((D, PT), BF), pltpu.VMEM((D, D), BF)],
        ),
        out_shape=[
            jax.ShapeDtypeStruct((3 * D, T), BF),
            jax.ShapeDtypeStruct((D, T), BF),
        ],
        compiler_params=params(),
        cost_estimate=cost(20),
    )(ids, n, dy, cos, sin, *wargs, *wargs)


QB = 512
HPS = 2


def attn_kernel(n_alias, len_ref, q_ref, k_ref, v_ref, do_ref, cos_ref, sin_ref, *refs):
    o_ref, dq_ref, dk_ref, dv_ref = refs[n_alias:]
    sub = lax.broadcasted_iota(jnp.int32, (HEAD_DIM, T), 0)
    lane = lax.broadcasted_iota(jnp.int32, (HEAD_DIM, T), 1)
    bias = jnp.where((sub == 0) & (lane >= len_ref[0]), -1e30, 0.0)
    ones = jnp.where(sub == 0, 1.0, 0.0).astype(BF)
    none = jnp.zeros((HEAD_DIM, T), F32)
    ki = lax.broadcasted_iota(jnp.int32, (QB, QB), 0)
    qi = lax.broadcasted_iota(jnp.int32, (QB, QB), 1)

    def unrot(val, cs, sn, out, base, cols):
        a = val[0:16, :]
        b = val[16:32, :]
        turned = [a * cs + b * sn, b * cs - a * sn, val[32:64, :]]
        out[base : base + 64, cols] = jnp.concatenate(turned, 0).astype(BF)

    for h in range(HPS):
        b = h * HEAD_DIM
        hs = slice(b, b + HEAD_DIM)
        q = q_ref[hs, :]
        k = k_ref[hs, :]
        v = v_ref[hs, :]
        qa = jnp.concatenate([q, ones], 0)
        ka = jnp.concatenate([k.astype(F32), bias], 0).T.astype(BF)
        vt = jnp.concatenate([v.astype(F32), none], 0).T.astype(BF)
        dk = [jnp.zeros((HEAD_DIM, QB), F32) for _ in range(T // QB)]
        dv = [jnp.zeros((HEAD_DIM, QB), F32) for _ in range(T // QB)]
        for i in range(T // QB):
            qs = slice(i * QB, (i + 1) * QB)
            kk = (i + 1) * QB
            st = mm(ka[:kk, :], qa[:, qs])
            diag = jnp.where(ki <= qi, st[kk - QB :, :], -1e30)
            st = diag if i == 0 else jnp.concatenate([st[: kk - QB, :], diag], 0)
            e = jnp.exp2(st - jnp.max(st, 0, keepdims=True))
            rl = 1.0 / jnp.sum(e, 0, keepdims=True)
            eb = e.astype(BF)
            ot = mm(v[:, :kk], eb) * rl
            o_ref[hs, qs] = ot.astype(BF)
            dn = (do_ref[hs, qs].astype(F32) * rl).astype(BF)
            delta = jnp.sum(dn.astype(F32) * ot, 0, keepdims=True)
            da = jnp.concatenate([dn, none[:, qs].astype(BF)], 0)
            ds = (e * (mm(vt[:kk, :], da) - delta)).astype(BF)
            dq = mm(k[:, :kk], ds) * (HEAD_DIM ** (-0.5))
            unrot(dq, cos_ref[:, qs], sin_ref[:, qs], dq_ref, b, qs)
            dvi = mm(dn, eb, NT)
            dki = mm(q[:, qs], ds, NT)
            for t in range(i + 1):
                ts = slice(t * QB, (t + 1) * QB)
                dv[t] = dv[t] + dvi[:, ts]
                dk[t] = dk[t] + dki[:, ts]
        for t in range(T // QB):
            ts = slice(t * QB, (t + 1) * QB)
            dv_ref[hs, ts] = dv[t].astype(BF)
            unrot(dk[t] * LN2, cos_ref[:, ts], sin_ref[:, ts], dk_ref, b, ts)


def attend(length, qkv, dot_, cos, sin, first, heads, before):
    rows = HPS * HEAD_DIM
    steps = HEADS // HPS
    at = first // HPS
    spec = lambda base: pl.BlockSpec((rows, T), lambda h, *_: (base + at + h, 0))
    shape = jax.ShapeDtypeStruct((D, T), BF)
    alias = [] if before is None else list(before)
    return pl.pallas_call(
        functools.partial(attn_kernel, len(alias)),
        grid_spec=pltpu.PrefetchScalarGridSpec(
            num_scalar_prefetch=1,
            grid=(heads // HPS,),
            in_specs=[
                spec(0),
                spec(steps),
                spec(2 * steps),
                spec(0),
                once((16, T)),
                once((16, T)),
            ]
            + [pl.BlockSpec(memory_space=pl.ANY)] * len(alias),
            out_specs=[spec(0)] * 4,
        ),
        out_shape=[shape] * 4,
        input_output_aliases={7 + i: i for i in range(len(alias))},
        compiler_params=params(),
        cost_estimate=cost(46 * heads / HEADS),
    )(length, qkv, qkv, qkv, dot_, cos, sin, *alias)


def agrad_kernel(hr, blocks, ids, nt_ref, dy_ref, o_ref, dq_ref, dk_ref, dv_ref, gm, g0, g1, gf, g_s):
    j = pl.program_id(0)
    for at, (src, near) in enumerate(((dq_ref, g0), (dk_ref, g0), (dv_ref, g1))):

        @pl.when((j >= 2 * at) & (j < 2 * at + 2))
        def _(src=src, near=near):
            spread(mm(nt_ref[...], src[...], NT).astype(BF), 0, gm, near, gf)

    @pl.when(j >= 6)
    def _():
        g_s[...] = mm(o_ref[...], dy_ref[...]).astype(BF)
        rows = [pl.multiple_of(ids[b], hr) for b in range(2 * blocks)]
        spread(jnp.concatenate([g_s[pl.ds(k, hr), :] for k in rows], 0), 0, gm, g1, gf)


def attn_grads(ids, nt, dy, ot, dq, dk, dv, hr, blocks):
    def grab(at):
        return pl.BlockSpec((TILE, T), lambda j, *_: (jnp.clip(j - 2 * at, 0, 1), 0))

    deep = lambda r: pl.BlockSpec((1, r, TILE), lambda j, *_: (j // 4, 0, j % 4))
    gspecs = [
        deep(D // 2),
        pl.BlockSpec((D // 4, TILE), lambda j, *_: (0, jnp.minimum(j, 3))),
        pl.BlockSpec((D // 4, TILE), lambda j, *_: (0, jnp.maximum(j - 4, 0))),
        deep(D // 4),
    ]
    return pl.pallas_call(
        functools.partial(agrad_kernel, hr, blocks),
        grid_spec=pltpu.PrefetchScalarGridSpec(
            num_scalar_prefetch=1,
            grid=(4 * D // TILE,),
            in_specs=[
                once((D, T)),
                pl.BlockSpec((T, TILE), lambda j, *_: (0, jnp.clip(j - 6, 0, 1))),
                once((D, T)),
                grab(0),
                grab(1),
                grab(2),
            ],
            out_specs=gspecs,
            scratch_shapes=[pltpu.VMEM((D, TILE), BF)],
        ),
        out_shape=grad_shapes(2 * D),
        compiler_params=params(),
        cost_estimate=cost(17),
    )(ids, nt, dy, ot, dq, dk, dv)


def final_kernel(np_, ids, x_ref, dy_ref, g_ref, bo_ref, o_ref, dq_ref, dk_ref, dv_ref, ao_ref, ag_ref, *refs):
    wq = refs[:np_]
    out_ref, gin_ref, v_ref, w_s = refs[np_:]
    i = pl.program_id(0)

    @pl.when(i == 0)
    def _():
        place(w_s, wq, ids, 1)

    x = x_ref[...].astype(F32)
    row = i * FT + lax.broadcasted_iota(jnp.int32, (FT, 1), 0)
    attn = mm(o_ref[...], w_s[:, 3 * D :], TN)
    out = x + attn + ao_ref[...].astype(F32) + bo_ref[...]
    out_ref[...] = jnp.where(row < ids[0], out, 0.0).astype(BF)
    dn = (
        ag_ref[...].astype(F32)
        + mm(w_s[:, :D], dq_ref[...])
        + mm(w_s[:, D : 2 * D], dk_ref[...])
        + mm(w_s[:, 2 * D : 3 * D], dv_ref[...])
    ).T
    mean = jnp.mean(x, -1, keepdims=True)
    xc = x - mean
    inv = lax.rsqrt(jnp.mean(xc * xc, -1, keepdims=True) + NORM_EPS)
    xh = xc * inv
    g = dn * g_ref[...]
    gx = dn * xh
    ln = inv * (
        g - jnp.mean(g, -1, keepdims=True) - xh * jnp.mean(g * xh, -1, keepdims=True)
    )
    gin_ref[...] = (dy_ref[...].astype(F32) + ln).astype(BF)

    @pl.when(i == 0)
    def _():
        v_ref[...] = jnp.zeros_like(v_ref)

    v_ref[0:1, :] += jnp.sum(gx, 0, keepdims=True)
    v_ref[1:2, :] += jnp.sum(dn, 0, keepdims=True)


def final(ids, x, dy, gain, b_out, ot, dq, dk, dv, acc_o, acc_g, weights, pieces):
    row = pl.BlockSpec((FT, D), lambda i, *_: (i, 0))
    col = pl.BlockSpec((D, FT), lambda i, *_: (0, i))
    vec = pl.BlockSpec((1, D), lambda i, *_: (0, 0))
    wargs = [weights, *pieces]
    return pl.pallas_call(
        functools.partial(final_kernel, len(wargs)),
        grid_spec=pltpu.PrefetchScalarGridSpec(
            num_scalar_prefetch=1,
            grid=(T // FT,),
            in_specs=[
                row,
                row,
                vec,
                vec,
                col,
                col,
                col,
                col,
                row,
                col,
                *[once((w.shape[0], 4 * D)) for w in wargs],
            ],
            out_specs=[row, row, pl.BlockSpec((8, D), lambda i, *_: (0, 0))],
            scratch_shapes=[pltpu.VMEM((D, 4 * D), BF)],
        ),
        out_shape=[
            jax.ShapeDtypeStruct((T, D), BF),
            jax.ShapeDtypeStruct((T, D), BF),
            jax.ShapeDtypeStruct((8, D), F32),
        ],
        compiler_params=params(),
        cost_estimate=cost(20),
    )(ids, x, dy, gain, b_out, ot, dq, dk, dv, acc_o, acc_g, *wargs)


C1 = float(1.0 - np.float32(B1) ** np.float32(STEP))
C2 = float(1.0 - np.float32(B2) ** np.float32(STEP))


def adam_math(g, m, v, w, decay):
    nm = B1 * m + (1.0 - B1) * g
    nv = B2 * v + (1.0 - B2) * g * g
    up = -LR * (nm / C1 / (jnp.sqrt(nv / C2) + ADAM_EPS) + decay * w)
    return nm, nv, up


def adam_kernel(n_alias, first, ids, sm, rm, so, ro, m_ref, v_ref, w_ref, *refs):
    wg_ref, nm_ref, nv_ref, up_ref, end_ref = refs[n_alias:]
    end_ref[...] = jnp.zeros_like(end_ref)
    summed = pl.program_id(0) + first == ids[1]
    hr = sm.shape[0]
    mine = jnp.where(summed, sm[...].astype(F32), rm[...].astype(F32))
    other = jnp.where(summed, so[...].astype(F32), ro[...].astype(F32))
    lead = ids[0] == 0
    for h, g in enumerate((jnp.where(lead, mine, other), jnp.where(lead, other, mine))):
        rows = slice(h * hr, (h + 1) * hr)
        nm, nv, up = adam_math(g, m_ref[rows, :], v_ref[rows, :], w_ref[rows, :].astype(F32), DECAY)
        wg_ref[rows, :] = g
        nm_ref[rows, :] = nm
        nv_ref[rows, :] = nv
        up_ref[rows, :] = up


def adam(ids, grads, cols, m, v, w, outs, first=0, count=2):
    rows, width = m.shape
    hr = rows // 2
    n = grads[0].shape[1]
    AC = 1024 if n % 1024 == 0 else 512
    pick = lambda hit: pl.BlockSpec(
        (hr, AC), lambda p, j, ids: (0, jnp.where((p + first == ids[1]) == hit, j, 0))
    )
    b0, b1 = cols[0] // AC, cols[1] // AC
    big = pl.BlockSpec((rows, AC), lambda p, j, ids: (0, jnp.where(p + first == 0, b0, b1) + j))
    alias = [] if outs is None else list(outs)
    return pl.pallas_call(
        functools.partial(adam_kernel, len(alias), first),
        grid_spec=pltpu.PrefetchScalarGridSpec(
            num_scalar_prefetch=1,
            grid=(count, n // AC),
            in_specs=[pick(True), pick(False), pick(True), pick(False), big, big, big]
            + [pl.BlockSpec(memory_space=pl.ANY)] * len(alias),
            out_specs=[big] * 4 + [pl.BlockSpec((8, 128), lambda p, j, ids: (0, 0))],
        ),
        out_shape=[jax.ShapeDtypeStruct((rows, width), F32)] * 4
        + [jax.ShapeDtypeStruct((8, 128), F32)],
        input_output_aliases={8 + i: i for i in range(len(alias))},
        compiler_params=pltpu.CompilerParams(
            dimension_semantics=("arbitrary", "arbitrary"), vmem_limit_bytes=VLIM
        ),
        cost_estimate=cost(6 * count * n / 2048),
    )(ids, *grads, m, v, w, *alias)


def after(values, *waits):
    flat = lax.optimization_barrier((*values, *waits))
    return list(flat[: len(values)])


def on_device(shards, reps, hidden_in, cotangent, lengths, weights, moment_m, moment_v, vectors, vector_m, vector_v):
    s = lax.axis_index("shard")
    rep = lax.axis_index("rep")
    c = rep % 2
    z = rep // 2
    zs = reps // 2
    swap = [(i, i ^ 1) for i in range(reps)]
    rows = weights.shape[0]
    hr = rows // 2
    i32 = jnp.int32
    cube = shards == 4 and zs & (zs - 1) == 0 and zs >= 4
    xn = [(i, i ^ 1) for i in range(shards)]
    yn = [(i, i ^ 2) for i in range(shards)]
    zsteps = [3] + [1 << k for k in range(2, 16) if 1 << k < zs]
    zn = lambda bit: [(i, i ^ (2 * bit)) for i in range(reps)]
    own = ((z ^ (z // 2)) % 2) if cube else jnp.int32(0)

    if cube:
        y_rows = [(s ^ r) * rows for r in (2, 3, 0, 1)]
    else:
        y_rows = [r * rows for r in range(shards)]
    cut = lambda at: [b + c * hr for b in at] + [b + (1 - c) * hr for b in at]
    y_off = cut(y_rows)
    stack = lambda *v: jnp.stack([jnp.asarray(x, i32) for x in v])
    length = lengths.astype(i32)
    gain = vectors[:D].reshape(1, D)
    shift = vectors[D : 2 * D].reshape(1, D)
    b_out = vectors[2 * D : 3 * D].reshape(1, D)
    b_in = vectors[3 * D :].reshape(1, FF)
    half_w = lax.dynamic_slice_in_dim(weights, c * hr, hr, 0)

    n, nt, dy, dyt, db_out = prep(
        stack(length[0], *y_off), hidden_in, cotangent, gain, shift, hr, shards
    )

    def part_of(cols):
        return jnp.concatenate([half_w[:, a:b] for a, b in cols], 1)

    q = hr // 2

    def gather_first(part):
        a, b = part[:q], part[q:]
        return [
            lax.ppermute(p, "shard", way) for p, way in ((a, xn), (b, yn), (b, xn), (a, yn))
        ]

    def gather_second(first):
        return [lax.ppermute(first[0], "shard", yn), lax.ppermute(first[1], "shard", xn)]

    def swapped(mine):
        return mine + [lax.ppermute(p, "rep", swap) for p in mine]

    def gather_whole(part):
        full = lax.all_gather(part, "shard", axis=0, tiled=True)
        other = lax.ppermute(full, "rep", swap)
        return [p[b * hr : (b + 1) * hr] for p in (full, other) for b in range(shards)]

    offsets = [0]
    for size in SIZES:
        offsets.append(offsets[-1] + size)
    apart, fpart = part_of([(0, 4 * D)]), part_of([(4 * D, 4 * D + 2 * FF)])
    if cube:
        base = [(s ^ r) * rows + e * q for r, e in ((1, 0), (2, 1), (1, 1), (2, 0), (3, 0), (3, 1))]
        offs = [b + c * hr for b in base] + [b + (1 - c) * hr for b in base]
        one = gather_first(apart)
        one[:2] = after(one[:2], n)
        one = one + gather_second(one)
        (fpart,) = after([fpart], *one)
        apieces = swapped(one)
        two = gather_first(fpart)
    else:
        offs = cut([b * rows for b in range(shards)])
        apieces = gather_whole(apart)
        two = gather_whole(fpart)
    piece_off = stack(s * rows, *offs)
    len_piece_off = stack(length[0], s * rows, *offs)

    add = lambda *v: sum(x.astype(F32) for x in v).astype(BF)

    class Reduce:
        def __init__(self, grads, split=False):
            self.split = split
            self.mine = grads[0]
            self.got = [lax.ppermute(g, "rep", swap) for g in grads[1:]]
            self.at = 0
            self.sums = None
            self.brought = []

        def settle(self, last):
            if self.brought:
                self.brought = after(self.brought, last)

        def step(self):
            self.at += 1
            k = self.at
            m, far, old = self.mine, self.got[2], self.brought
            if not cube:
                groups = [[2 * j + e for j in range(zs)] for e in range(2)]
                both = add(m, jnp.concatenate([jnp.stack(self.got[:2]), far], 1))
                both = lax.psum_scatter(both, "shard", scatter_dimension=1, tiled=True)
                both = lax.psum(both, "rep", axis_index_groups=groups)
                self.sums = (both[0], both[1])
                return [], []
            if self.split and k <= 3:
                return self.step_split(k)
            if k == 1:
                sent = add(m[:, : 2 * hr], jnp.stack(self.got[:2]))
                way = ("shard", yn)
            elif k == 2:
                self.first = old[0]
                sent = add(m[:, 3 * hr :], far[:, hr:], old[0][:, hr:])
                way = ("shard", xn)
            elif k == 3:
                total = add(m[:, 2 * hr : 3 * hr], far[:, :hr], self.first[:, :hr], old[0])
                lead = own == 0
                sent = jnp.where(lead, total[1], total[0])
                self.keep = jnp.where(lead, total[0], total[1])
                way = ("rep", zn(1))
            else:
                sent = self.keep = add(self.keep, old[0])
                last = k == 4 + len(zsteps)
                way = ("rep", zn(1 if last else zsteps[k - 4]))
            self.brought = [lax.ppermute(sent, *way)]
            if k == 4 + len(zsteps):
                self.sums = (self.keep, self.brought[0])
            return [sent], self.brought

        def step_split(self, k):
            m, old = self.mine, self.brought
            near, far = self.got[:2], self.got[2]
            b = [slice(i * hr, (i + 1) * hr) for i in range(4)]
            if k == 1:
                low = [add(m[0, b[3]], far[0, b[1]]), add(m[0, b[1]], near[0][b[1]])]
                sent = [jnp.concatenate(low, 0), add(m[1, : 2 * hr], near[1])]
                ways = xn, yn
            elif k == 2:
                self.first = old
                sent = [
                    add(m[0, b[0]], near[0][b[0]], old[0][b[1]]),
                    add(m[1, b[3]], far[1, b[1]], old[1][b[1]]),
                ]
                ways = yn, xn
            else:
                total = [
                    add(m[e, b[2]], far[e, b[0]], self.first[e][b[0]], old[e]) for e in range(2)
                ]
                lead = own == 0
                sent = [jnp.where(lead, total[1], total[0])]
                self.keep = jnp.where(lead, total[0], total[1])
                self.brought = [lax.ppermute(sent[0], "rep", zn(1))]
                return sent, self.brought
            self.brought = [lax.ppermute(v, "shard", w) for v, w in zip(sent, ways)]
            return sent, self.brought

        def result(self):
            while self.sums is None:
                self.step()
            return [*self.sums, *[lax.ppermute(v, "rep", swap) for v in self.sums]]

    flight = []

    def turn(values, last, *steps):
        nonlocal flight
        waits = flight
        flight = []
        for red in steps:
            if red.sums is None:
                red.settle(last)
                moved = red.step()
                waits = waits + moved[0]
                flight = flight + moved[1]
        return after(values, *waits) if waits else list(values)

    inv_freq = jnp.power(F32(10000.0), -jnp.arange(0, ROT, 2, dtype=F32) / ROT)
    angles = inv_freq[:, None] * jnp.arange(T, dtype=F32)[None, :]
    cos, sin = jnp.cos(angles), jnp.sin(angles)
    qkv, dot_ = proj(piece_off, n, dy, cos, sin, weights, apieces)
    half = HEADS // 2
    heads = attend(length, qkv, dot_, cos, sin, 0, half, None)
    if cube:
        *two, qkv = after([*two, qkv], heads[0])
        three = gather_second(two)
        across = [lax.ppermute(v, "rep", swap) for v in two[:2]]
    ot, dq, dk, dv = attend(length, qkv, dot_, cos, sin, half, half, heads)
    dyg = dy
    if cube:
        (dyg,) = after([dy], ot, *three, *across)
        rest = after(two[2:] + three, ot)
        across += [lax.ppermute(v, "rep", swap) for v in rest]
        fpieces = two + three + across
    else:
        fpieces = two
    reds = [Reduce(attn_grads(stack(*y_off), nt, dyg, ot, dq, dk, dv, hr, shards), True)]
    places = [(0, 2 * D)]
    acc = None
    dbs = []
    nk = n
    for at, size in zip(offsets, SIZES):
        (nk,) = turn([nk], dbs[-1] if dbs else dv, *reds)
        *grads, db_in, acc_o, acc_g = mlp(
            piece_off, nk, nt, dy, dyt, b_in, weights, fpieces, at, size, acc
        )
        acc = (acc_o, acc_g)
        dbs.append(db_in)
        reds.append(Reduce(grads))
        places.append((4 * D + at, 4 * D + FF + at))

    (ot,) = turn([ot], dbs[-1], *reds)
    out, grad_in, vsum = final(
        len_piece_off, hidden_in, dy, gain, b_out, ot, dq, dk, dv, *acc, weights, apieces
    )
    core = stack(c, own)
    def push(last, *steps):
        waits = []
        for red in steps:
            if red.sums is None:
                red.settle(last)
                waits = waits + red.step()[0]
        return after([core], *waits)[0] if waits else core

    args = moment_m, moment_v, weights
    vec = jnp.concatenate([vsum[0], vsum[1], db_out[0], *[d[0] for d in dbs]])
    if cube:
        vec = vec.reshape(-1, 128)
        hops = [("rep", swap), ("shard", xn), ("shard", yn)]
        hops += [("rep", zn(bit)) for bit in [1] + zsteps]
    else:
        vec = lax.psum(vec, ("rep", "shard"))
        hops = []

    def hop(last, count=1):
        nonlocal vec
        for _ in range(count):
            if hops:
                (vec,) = after([vec], last)
                vec = vec + lax.ppermute(vec, *hops.pop(0))

    big, end = None, vsum
    for i, (red, place_) in enumerate(zip(reds, places)):
        hop(end)
        ids = push(end, *reds[i:])
        *big, end = adam(ids, red.result(), place_, *args, big)
    while hops:
        hop(end)
    vec = vec.reshape(-1)
    vm, vv, vu = adam_math(vec, vector_m, vector_v, vectors, 0.0)
    return (out, grad_in, *big, vec, vm, vv, vu)


def solution(mesh):
    tok = P(("rep", "shard"), None)
    w = P("shard", None)
    return jax.shard_map(
        functools.partial(on_device, mesh.shape["shard"], mesh.shape["rep"]),
        mesh=mesh,
        in_specs=(tok, tok, P(("rep", "shard")), w, w, w, P(), P(), P()),
        out_specs=(tok, tok, w, w, w, w, P(), P(), P(), P()),
        check_vma=False,
    )
```

```python
import functools

import jax
import jax.numpy as jnp
import numpy as np
from jax import lax
from jax.experimental import pallas as pl
from jax.experimental.pallas import tpu as pltpu
from jax.sharding import PartitionSpec as P

D = 1024
HEADS = 16
HEAD_DIM = 64
ROT = 32
FF = 4096
T = 1024
STEP = 10

B1 = 0.9
B2 = 0.95
LR = 0.02
DECAY = 0.1
ADAM_EPS = 1e-08
NORM_EPS = 1e-05
GC = 0.7978845608028654
GA = 0.044715
LOG2E = 1.4426950408889634
LN2 = 0.6931471805599453

BF = jnp.bfloat16
F32 = jnp.float32
VLIM = 58 * 1024 * 1024
NN = (((1,), (0,)), ((), ()))
NT = (((1,), (1,)), ((), ()))
TN = (((0,), (0,)), ((), ()))
TT = (((0,), (1,)), ((), ()))
TILE = 512
SIZES = (1024, 1024, 1024, 1024)
MB = 1024
MT = 1024
TB = 256
PT = 512
FT = 256


def mm(a, b, dims=NN):
    return lax.dot_general(a, b, dims, preferred_element_type=F32)


def params():
    return pltpu.CompilerParams(
        dimension_semantics=("arbitrary",), vmem_limit_bytes=VLIM
    )


def once(shape):
    return pl.BlockSpec(shape, lambda *_: (0,) * len(shape), pipeline_mode=pl.Buffered(1))


def cost(us):
    return pl.CostEstimate(flops=int(us * 1.15e9), bytes_accessed=1024, transcendentals=0)


def prep_kernel(hr, blocks, ids, x_ref, c_ref, g_ref, b_ref, n_ref, nt_ref, d_ref, dt_ref, db_ref, s_ref):
    i = pl.program_id(0)
    x = x_ref[...].astype(F32)
    mean = jnp.mean(x, -1, keepdims=True)
    xc = x - mean
    var = jnp.mean(xc * xc, -1, keepdims=True)
    n = xc * lax.rsqrt(var + NORM_EPS) * g_ref[...] + b_ref[...]
    n_ref[...] = n.astype(BF)
    row = i * TB + lax.broadcasted_iota(jnp.int32, (TB, 1), 0)
    dy = jnp.where(row < ids[0], c_ref[...].astype(F32), 0.0)
    d_ref[...] = dy.astype(BF)

    @pl.when(i == 0)
    def _():
        db_ref[...] = jnp.zeros_like(db_ref)

    db_ref[...] += jnp.sum(dy, 0, keepdims=True)
    for val, out in ((n, nt_ref), (dy, dt_ref)):
        s_ref[...] = val.T.astype(BF)
        for b in range(2 * blocks):
            off = pl.multiple_of(ids[1 + b], hr)
            out[b * hr : (b + 1) * hr, :] = s_ref[pl.ds(off, hr), :]


def prep(ids, x, cot, gain, shift, hr, blocks):
    row = lambda i, *_: (i, 0)
    col = lambda i, *_: (0, i)
    fix = lambda i, *_: (0, 0)
    return pl.pallas_call(
        functools.partial(prep_kernel, hr, blocks),
        grid_spec=pltpu.PrefetchScalarGridSpec(
            num_scalar_prefetch=1,
            grid=(T // TB,),
            in_specs=[
                pl.BlockSpec((TB, D), row),
                pl.BlockSpec((TB, D), row),
                pl.BlockSpec((1, D), fix),
                pl.BlockSpec((1, D), fix),
            ],
            out_specs=[
                pl.BlockSpec((TB, D), row),
                pl.BlockSpec((D, TB), col),
                pl.BlockSpec((TB, D), row),
                pl.BlockSpec((D, TB), col),
                pl.BlockSpec((1, D), fix),
            ],
            scratch_shapes=[pltpu.VMEM((D, TB), BF)],
        ),
        out_shape=[
            jax.ShapeDtypeStruct((T, D), BF),
            jax.ShapeDtypeStruct((D, T), BF),
            jax.ShapeDtypeStruct((T, D), BF),
            jax.ShapeDtypeStruct((D, T), BF),
            jax.ShapeDtypeStruct((1, D), F32),
        ],
        compiler_params=params(),
        cost_estimate=cost(8),
    )(ids, x, cot, gain, shift)


def place(dst, srcs, ids, base):
    for k, src in enumerate(srcs):
        rows = src.shape[0]
        dst[pl.ds(pl.multiple_of(ids[base + k], rows), rows), :] = src[...]


def spread(g, e, mine, near, far):
    a, b = D // 2, 3 * D // 4
    mine[e] = g[:a, :]
    near[...] = g[a:b, :]
    far[e] = g[b:, :]


def grad_shapes(n):
    return [
        jax.ShapeDtypeStruct(v, BF)
        for v in ((2, D // 2, n), (D // 4, n), (D // 4, n), (2, D // 4, n))
    ]


def mlp_kernel(np_, first, ids, n_ref, nt_ref, d_ref, dt_ref, b_ref, *refs):
    win = refs[:np_]
    wout = refs[np_ : 2 * np_]
    refs = refs[2 * np_ :]
    if not first:
        oin, gin = refs[:2]
        refs = refs[2:]
    gm, g0, g1, gf = refs[:4]
    db_ref, o_out, g_out, wi, wo, h_s, p_s, o_ref, g_ref = refs[4:]
    j = pl.program_id(0)
    place(wi, win, ids, 0)
    place(wo, wout, ids, 0)
    bias = b_ref[...]
    wi_v = wi[...]
    wo_v = wo[...]
    db = jnp.zeros((1, MT), F32)
    for t in range(T // MB):
        rows = slice(t * MB, (t + 1) * MB)
        pre = mm(n_ref[rows, :], wi_v) + bias
        dh = mm(d_ref[rows, :], wo_v)
        sq = pre * pre
        th = jnp.tanh(GC * pre * (1.0 + GA * sq))
        half = 0.5 * (1.0 + th)
        h = (pre * half).astype(BF)
        slope = half + 0.5 * pre * (1.0 - th * th) * (GC + (3.0 * GA * GC) * sq)
        dp = (dh * slope).astype(BF)
        h_s[rows, :] = h
        p_s[rows, :] = dp
        db = db + jnp.sum(dp.astype(F32), 0, keepdims=True)
        ov = mm(h, wo_v, NT)
        gv = mm(wi_v, dp, NT)

        if first:

            @pl.when(j == 0)
            def _():
                o_ref[rows, :] = ov
                g_ref[:, rows] = gv

        else:

            @pl.when(j == 0)
            def _():
                o_ref[rows, :] = oin[rows, :].astype(F32) + ov
                g_ref[:, rows] = gin[:, rows].astype(F32) + gv

        @pl.when(j > 0)
        def _():
            o_ref[rows, :] += ov
            g_ref[:, rows] += gv

    @pl.when(j == pl.num_programs(0) - 1)
    def _():
        o_out[...] = o_ref[...].astype(BF)
        g_out[...] = g_ref[...].astype(BF)

    db_ref[...] = db
    hv = h_s[...]
    pv = p_s[...]
    for e, (left, right) in enumerate(((nt_ref, pv), (dt_ref, hv))):
        spread(mm(left[...], right).astype(BF), e, gm, (g0, g1)[e], gf)


def mlp(ids, n, nt, dy, dyt, bias, weights, pieces, offset, size, acc):
    first = acc is None
    nt_cols = size // MT
    tall = lambda cols: pl.BlockSpec((T, cols), lambda j, *_: (0, 0))
    own_rows = weights.shape[0]
    in_base = (4 * D + offset) // MT
    out_base = (4 * D + FF + offset) // MT
    wspecs = []
    for base_own, base in ((in_base, offset // MT), (out_base, (FF + offset) // MT)):
        if own_rows:
            wspecs.append(pl.BlockSpec((own_rows, MT), lambda j, *_, b=base_own: (0, b + j)))
        for p in pieces:
            wspecs.append(pl.BlockSpec((p.shape[0], MT), lambda j, *_, b=base: (0, b + j)))
    wargs = [weights, *pieces]
    bb = offset // MT
    flat = pl.BlockSpec((D // 4, MT), lambda j, *_: (0, j))
    deep = lambda r: pl.BlockSpec((2, r, MT), lambda j, *_: (0, 0, j))
    gspecs = [deep(D // 2), flat, flat, deep(D // 4)]
    return pl.pallas_call(
        functools.partial(mlp_kernel, len(wargs), first),
        grid_spec=pltpu.PrefetchScalarGridSpec(
            num_scalar_prefetch=1,
            grid=(nt_cols,),
            in_specs=[
                once((T, D)),
                once((D, T)),
                once((T, D)),
                once((D, T)),
                pl.BlockSpec((1, MT), lambda j, *_: (0, bb + j)),
                *wspecs,
                *([] if first else [once((T, D)), once((D, T))]),
            ],
            out_specs=[
                *gspecs,
                pl.BlockSpec((1, MT), lambda j, *_: (0, j)),
                once((T, D)),
                once((D, T)),
            ],
            scratch_shapes=[
                pltpu.VMEM((D, MT), BF),
                pltpu.VMEM((D, MT), BF),
                pltpu.VMEM((T, MT), BF),
                pltpu.VMEM((T, MT), BF),
                pltpu.VMEM((T, D), F32),
                pltpu.VMEM((D, T), F32),
            ],
        ),
        out_shape=[
            *grad_shapes(size),
            jax.ShapeDtypeStruct((1, size), F32),
            jax.ShapeDtypeStruct((T, D), BF),
            jax.ShapeDtypeStruct((D, T), BF),
        ],
        compiler_params=params(),
        cost_estimate=cost(41 * size / 2048),
    )(ids, n, nt, dy, dyt, bias, *wargs, *wargs, *([] if first else acc))


def proj_kernel(np_, ids, n_ref, d_ref, cos_ref, sin_ref, *refs):
    wq = refs[:np_]
    wo = refs[np_ : 2 * np_]
    out_ref, dout_ref, w_s, wo_s = refs[2 * np_ :]
    j = pl.program_id(0)
    place(w_s, wq, ids, 0)
    r = mm(w_s[...], n_ref[...], TT)

    def rotated(scale):
        for h in range(PT // HEAD_DIM):
            b = h * HEAD_DIM
            u = r[b : b + 16, :]
            w = r[b + 16 : b + 32, :]
            cs = cos_ref[...]
            sn = sin_ref[...]
            turned = [u * cs - w * sn, w * cs + u * sn, r[b + 32 : b + 64, :]]
            out_ref[b : b + 64, :] = (jnp.concatenate(turned, 0) * scale).astype(BF)

    @pl.when(j < D // PT)
    def _():
        rotated(LOG2E * HEAD_DIM ** (-0.5))

    @pl.when((j >= D // PT) & (j < 2 * D // PT))
    def _():
        rotated(1.0)

    @pl.when(j >= 2 * D // PT)
    def _():
        out_ref[...] = r.astype(BF)

    @pl.when(j == 0)
    def _():
        place(wo_s, wo, ids, 0)
        dout_ref[...] = mm(wo_s[...], d_ref[...], NT).astype(BF)


def proj(ids, n, dy, cos, sin, weights, pieces):
    wargs = [weights, *pieces]
    return pl.pallas_call(
        functools.partial(proj_kernel, len(wargs)),
        grid_spec=pltpu.PrefetchScalarGridSpec(
            num_scalar_prefetch=1,
            grid=(3 * D // PT,),
            in_specs=[
                once((T, D)),
                once((T, D)),
                once((16, T)),
                once((16, T)),
                *[pl.BlockSpec((w.shape[0], PT), lambda j, *_: (0, j)) for w in wargs],
                *[
                    pl.BlockSpec((w.shape[0], D), lambda j, *_: (0, 3), pipeline_mode=pl.Buffered(1))
                    for w in wargs
                ],
            ],
            out_specs=[
                pl.BlockSpec((PT, T), lambda j, *_: (j, 0)),
                once((D, T)),
            ],
            scratch_shapes=[pltpu.VMEM((D, PT), BF), pltpu.VMEM((D, D), BF)],
        ),
        out_shape=[
            jax.ShapeDtypeStruct((3 * D, T), BF),
            jax.ShapeDtypeStruct((D, T), BF),
        ],
        compiler_params=params(),
        cost_estimate=cost(20),
    )(ids, n, dy, cos, sin, *wargs, *wargs)


QB = 512
HPS = 2


def attn_kernel(n_alias, len_ref, q_ref, k_ref, v_ref, do_ref, cos_ref, sin_ref, *refs):
    o_ref, dq_ref, dk_ref, dv_ref = refs[n_alias:]
    sub = lax.broadcasted_iota(jnp.int32, (HEAD_DIM, T), 0)
    lane = lax.broadcasted_iota(jnp.int32, (HEAD_DIM, T), 1)
    bias = jnp.where((sub == 0) & (lane >= len_ref[0]), -1e30, 0.0)
    ones = jnp.where(sub == 0, 1.0, 0.0).astype(BF)
    none = jnp.zeros((HEAD_DIM, T), F32)
    ki = lax.broadcasted_iota(jnp.int32, (QB, QB), 0)
    qi = lax.broadcasted_iota(jnp.int32, (QB, QB), 1)

    def unrot(val, cs, sn, out, base, cols):
        a = val[0:16, :]
        b = val[16:32, :]
        turned = [a * cs + b * sn, b * cs - a * sn, val[32:64, :]]
        out[base : base + 64, cols] = jnp.concatenate(turned, 0).astype(BF)

    for h in range(HPS):
        b = h * HEAD_DIM
        hs = slice(b, b + HEAD_DIM)
        q = q_ref[hs, :]
        k = k_ref[hs, :]
        v = v_ref[hs, :]
        qa = jnp.concatenate([q, ones], 0)
        ka = jnp.concatenate([k.astype(F32), bias], 0).T.astype(BF)
        vt = jnp.concatenate([v.astype(F32), none], 0).T.astype(BF)
        dk = [jnp.zeros((HEAD_DIM, QB), F32) for _ in range(T // QB)]
        dv = [jnp.zeros((HEAD_DIM, QB), F32) for _ in range(T // QB)]
        for i in range(T // QB):
            qs = slice(i * QB, (i + 1) * QB)
            kk = (i + 1) * QB
            st = mm(ka[:kk, :], qa[:, qs])
            diag = jnp.where(ki <= qi, st[kk - QB :, :], -1e30)
            st = diag if i == 0 else jnp.concatenate([st[: kk - QB, :], diag], 0)
            e = jnp.exp2(st - jnp.max(st, 0, keepdims=True))
            rl = 1.0 / jnp.sum(e, 0, keepdims=True)
            eb = e.astype(BF)
            ot = mm(v[:, :kk], eb) * rl
            o_ref[hs, qs] = ot.astype(BF)
            dn = (do_ref[hs, qs].astype(F32) * rl).astype(BF)
            delta = jnp.sum(dn.astype(F32) * ot, 0, keepdims=True)
            da = jnp.concatenate([dn, none[:, qs].astype(BF)], 0)
            ds = (e * (mm(vt[:kk, :], da) - delta)).astype(BF)
            dq = mm(k[:, :kk], ds) * (HEAD_DIM ** (-0.5))
            unrot(dq, cos_ref[:, qs], sin_ref[:, qs], dq_ref, b, qs)
            dvi = mm(dn, eb, NT)
            dki = mm(q[:, qs], ds, NT)
            for t in range(i + 1):
                ts = slice(t * QB, (t + 1) * QB)
                dv[t] = dv[t] + dvi[:, ts]
                dk[t] = dk[t] + dki[:, ts]
        for t in range(T // QB):
            ts = slice(t * QB, (t + 1) * QB)
            dv_ref[hs, ts] = dv[t].astype(BF)
            unrot(dk[t] * LN2, cos_ref[:, ts], sin_ref[:, ts], dk_ref, b, ts)


def attend(length, qkv, dot_, cos, sin, first, heads, before):
    rows = HPS * HEAD_DIM
    steps = HEADS // HPS
    at = first // HPS
    spec = lambda base: pl.BlockSpec((rows, T), lambda h, *_: (base + at + h, 0))
    shape = jax.ShapeDtypeStruct((D, T), BF)
    alias = [] if before is None else list(before)
    return pl.pallas_call(
        functools.partial(attn_kernel, len(alias)),
        grid_spec=pltpu.PrefetchScalarGridSpec(
            num_scalar_prefetch=1,
            grid=(heads // HPS,),
            in_specs=[
                spec(0),
                spec(steps),
                spec(2 * steps),
                spec(0),
                once((16, T)),
                once((16, T)),
            ]
            + [pl.BlockSpec(memory_space=pl.ANY)] * len(alias),
            out_specs=[spec(0)] * 4,
        ),
        out_shape=[shape] * 4,
        input_output_aliases={7 + i: i for i in range(len(alias))},
        compiler_params=params(),
        cost_estimate=cost(46 * heads / HEADS),
    )(length, qkv, qkv, qkv, dot_, cos, sin, *alias)


def agrad_kernel(hr, blocks, ids, nt_ref, dy_ref, o_ref, dq_ref, dk_ref, dv_ref, gm, g0, g1, gf, g_s):
    j = pl.program_id(0)
    for at, (src, near) in enumerate(((dq_ref, g0), (dk_ref, g0), (dv_ref, g1))):

        @pl.when((j >= 2 * at) & (j < 2 * at + 2))
        def _(src=src, near=near):
            spread(mm(nt_ref[...], src[...], NT).astype(BF), 0, gm, near, gf)

    @pl.when(j >= 6)
    def _():
        g_s[...] = mm(o_ref[...], dy_ref[...]).astype(BF)
        rows = [pl.multiple_of(ids[b], hr) for b in range(2 * blocks)]
        spread(jnp.concatenate([g_s[pl.ds(k, hr), :] for k in rows], 0), 0, gm, g1, gf)


def attn_grads(ids, nt, dy, ot, dq, dk, dv, hr, blocks):
    def grab(at):
        return pl.BlockSpec((TILE, T), lambda j, *_: (jnp.clip(j - 2 * at, 0, 1), 0))

    deep = lambda r: pl.BlockSpec((1, r, TILE), lambda j, *_: (j // 4, 0, j % 4))
    gspecs = [
        deep(D // 2),
        pl.BlockSpec((D // 4, TILE), lambda j, *_: (0, jnp.minimum(j, 3))),
        pl.BlockSpec((D // 4, TILE), lambda j, *_: (0, jnp.maximum(j - 4, 0))),
        deep(D // 4),
    ]
    return pl.pallas_call(
        functools.partial(agrad_kernel, hr, blocks),
        grid_spec=pltpu.PrefetchScalarGridSpec(
            num_scalar_prefetch=1,
            grid=(4 * D // TILE,),
            in_specs=[
                once((D, T)),
                pl.BlockSpec((T, TILE), lambda j, *_: (0, jnp.clip(j - 6, 0, 1))),
                once((D, T)),
                grab(0),
                grab(1),
                grab(2),
            ],
            out_specs=gspecs,
            scratch_shapes=[pltpu.VMEM((D, TILE), BF)],
        ),
        out_shape=grad_shapes(2 * D),
        compiler_params=params(),
        cost_estimate=cost(17),
    )(ids, nt, dy, ot, dq, dk, dv)


def final_kernel(np_, ids, x_ref, dy_ref, g_ref, bo_ref, o_ref, dq_ref, dk_ref, dv_ref, ao_ref, ag_ref, *refs):
    wq = refs[:np_]
    out_ref, gin_ref, v_ref, w_s = refs[np_:]
    i = pl.program_id(0)

    @pl.when(i == 0)
    def _():
        place(w_s, wq, ids, 1)

    x = x_ref[...].astype(F32)
    row = i * FT + lax.broadcasted_iota(jnp.int32, (FT, 1), 0)
    attn = mm(o_ref[...], w_s[:, 3 * D :], TN)
    out = x + attn + ao_ref[...].astype(F32) + bo_ref[...]
    out_ref[...] = jnp.where(row < ids[0], out, 0.0).astype(BF)
    dn = (
        ag_ref[...].astype(F32)
        + mm(w_s[:, :D], dq_ref[...])
        + mm(w_s[:, D : 2 * D], dk_ref[...])
        + mm(w_s[:, 2 * D : 3 * D], dv_ref[...])
    ).T
    mean = jnp.mean(x, -1, keepdims=True)
    xc = x - mean
    inv = lax.rsqrt(jnp.mean(xc * xc, -1, keepdims=True) + NORM_EPS)
    xh = xc * inv
    g = dn * g_ref[...]
    gx = dn * xh
    ln = inv * (
        g - jnp.mean(g, -1, keepdims=True) - xh * jnp.mean(g * xh, -1, keepdims=True)
    )
    gin_ref[...] = (dy_ref[...].astype(F32) + ln).astype(BF)

    @pl.when(i == 0)
    def _():
        v_ref[...] = jnp.zeros_like(v_ref)

    v_ref[0:1, :] += jnp.sum(gx, 0, keepdims=True)
    v_ref[1:2, :] += jnp.sum(dn, 0, keepdims=True)


def final(ids, x, dy, gain, b_out, ot, dq, dk, dv, acc_o, acc_g, weights, pieces):
    row = pl.BlockSpec((FT, D), lambda i, *_: (i, 0))
    col = pl.BlockSpec((D, FT), lambda i, *_: (0, i))
    vec = pl.BlockSpec((1, D), lambda i, *_: (0, 0))
    wargs = [weights, *pieces]
    return pl.pallas_call(
        functools.partial(final_kernel, len(wargs)),
        grid_spec=pltpu.PrefetchScalarGridSpec(
            num_scalar_prefetch=1,
            grid=(T // FT,),
            in_specs=[
                row,
                row,
                vec,
                vec,
                col,
                col,
                col,
                col,
                row,
                col,
                *[once((w.shape[0], 4 * D)) for w in wargs],
            ],
            out_specs=[row, row, pl.BlockSpec((8, D), lambda i, *_: (0, 0))],
            scratch_shapes=[pltpu.VMEM((D, 4 * D), BF)],
        ),
        out_shape=[
            jax.ShapeDtypeStruct((T, D), BF),
            jax.ShapeDtypeStruct((T, D), BF),
            jax.ShapeDtypeStruct((8, D), F32),
        ],
        compiler_params=params(),
        cost_estimate=cost(20),
    )(ids, x, dy, gain, b_out, ot, dq, dk, dv, acc_o, acc_g, *wargs)


C1 = float(1.0 - np.float32(B1) ** np.float32(STEP))
C2 = float(1.0 - np.float32(B2) ** np.float32(STEP))


def adam_math(g, m, v, w, decay):
    nm = B1 * m + (1.0 - B1) * g
    nv = B2 * v + (1.0 - B2) * g * g
    up = -LR * (nm / C1 / (jnp.sqrt(nv / C2) + ADAM_EPS) + decay * w)
    return nm, nv, up


def adam_kernel(n_alias, first, ids, sm, rm, so, ro, m_ref, v_ref, w_ref, *refs):
    wg_ref, nm_ref, nv_ref, up_ref, end_ref = refs[n_alias:]
    end_ref[...] = jnp.zeros_like(end_ref)
    summed = pl.program_id(0) + first == ids[1]
    hr = sm.shape[0]
    mine = jnp.where(summed, sm[...].astype(F32), rm[...].astype(F32))
    other = jnp.where(summed, so[...].astype(F32), ro[...].astype(F32))
    lead = ids[0] == 0
    for h, g in enumerate((jnp.where(lead, mine, other), jnp.where(lead, other, mine))):
        rows = slice(h * hr, (h + 1) * hr)
        nm, nv, up = adam_math(g, m_ref[rows, :], v_ref[rows, :], w_ref[rows, :].astype(F32), DECAY)
        wg_ref[rows, :] = g
        nm_ref[rows, :] = nm
        nv_ref[rows, :] = nv
        up_ref[rows, :] = up


def adam(ids, grads, cols, m, v, w, outs, first=0, count=2):
    rows, width = m.shape
    hr = rows // 2
    n = grads[0].shape[1]
    AC = 1024 if n % 1024 == 0 else 512
    pick = lambda hit: pl.BlockSpec(
        (hr, AC), lambda p, j, ids: (0, jnp.where((p + first == ids[1]) == hit, j, 0))
    )
    b0, b1 = cols[0] // AC, cols[1] // AC
    big = pl.BlockSpec((rows, AC), lambda p, j, ids: (0, jnp.where(p + first == 0, b0, b1) + j))
    alias = [] if outs is None else list(outs)
    return pl.pallas_call(
        functools.partial(adam_kernel, len(alias), first),
        grid_spec=pltpu.PrefetchScalarGridSpec(
            num_scalar_prefetch=1,
            grid=(count, n // AC),
            in_specs=[pick(True), pick(False), pick(True), pick(False), big, big, big]
            + [pl.BlockSpec(memory_space=pl.ANY)] * len(alias),
            out_specs=[big] * 4 + [pl.BlockSpec((8, 128), lambda p, j, ids: (0, 0))],
        ),
        out_shape=[jax.ShapeDtypeStruct((rows, width), F32)] * 4
        + [jax.ShapeDtypeStruct((8, 128), F32)],
        input_output_aliases={8 + i: i for i in range(len(alias))},
        compiler_params=pltpu.CompilerParams(
            dimension_semantics=("arbitrary", "arbitrary"), vmem_limit_bytes=VLIM
        ),
        cost_estimate=cost(6 * count * n / 2048),
    )(ids, *grads, m, v, w, *alias)


def after(values, *waits):
    flat = lax.optimization_barrier((*values, *waits))
    return list(flat[: len(values)])


def on_device(shards, reps, hidden_in, cotangent, lengths, weights, moment_m, moment_v, vectors, vector_m, vector_v):
    s = lax.axis_index("shard")
    rep = lax.axis_index("rep")
    c = rep % 2
    z = rep // 2
    zs = reps // 2
    swap = [(i, i ^ 1) for i in range(reps)]
    rows = weights.shape[0]
    hr = rows // 2
    i32 = jnp.int32
    cube = shards == 4 and zs & (zs - 1) == 0 and zs >= 4
    xn = [(i, i ^ 1) for i in range(shards)]
    yn = [(i, i ^ 2) for i in range(shards)]
    zsteps = [3] + [1 << k for k in range(2, 16) if 1 << k < zs]
    zn = lambda bit: [(i, i ^ (2 * bit)) for i in range(reps)]
    own = ((z ^ (z // 2)) % 2) if cube else jnp.int32(0)

    if cube:
        y_rows = [(s ^ r) * rows for r in (2, 3, 0, 1)]
    else:
        y_rows = [r * rows for r in range(shards)]
    cut = lambda at: [b + c * hr for b in at] + [b + (1 - c) * hr for b in at]
    y_off = cut(y_rows)
    stack = lambda *v: jnp.stack([jnp.asarray(x, i32) for x in v])
    length = lengths.astype(i32)
    gain = vectors[:D].reshape(1, D)
    shift = vectors[D : 2 * D].reshape(1, D)
    b_out = vectors[2 * D : 3 * D].reshape(1, D)
    b_in = vectors[3 * D :].reshape(1, FF)
    half_w = lax.dynamic_slice_in_dim(weights, c * hr, hr, 0)

    n, nt, dy, dyt, db_out = prep(
        stack(length[0], *y_off), hidden_in, cotangent, gain, shift, hr, shards
    )

    def part_of(cols):
        return jnp.concatenate([half_w[:, a:b] for a, b in cols], 1)

    q = hr // 2

    def gather_first(part):
        a, b = part[:q], part[q:]
        return [
            lax.ppermute(p, "shard", way) for p, way in ((a, xn), (b, yn), (b, xn), (a, yn))
        ]

    def gather_second(first):
        return [lax.ppermute(first[0], "shard", yn), lax.ppermute(first[1], "shard", xn)]

    def swapped(mine):
        return mine + [lax.ppermute(p, "rep", swap) for p in mine]

    def gather_whole(part):
        full = lax.all_gather(part, "shard", axis=0, tiled=True)
        other = lax.ppermute(full, "rep", swap)
        return [p[b * hr : (b + 1) * hr] for p in (full, other) for b in range(shards)]

    offsets = [0]
    for size in SIZES:
        offsets.append(offsets[-1] + size)
    apart, fpart = part_of([(0, 4 * D)]), part_of([(4 * D, 4 * D + 2 * FF)])
    if cube:
        base = [(s ^ r) * rows + e * q for r, e in ((1, 0), (2, 1), (1, 1), (2, 0), (3, 0), (3, 1))]
        offs = [b + c * hr for b in base] + [b + (1 - c) * hr for b in base]
        one = gather_first(apart)
        one[:2] = after(one[:2], n)
        one = one + gather_second(one)
        (fpart,) = after([fpart], *one)
        apieces = swapped(one)
        two = gather_first(fpart)
    else:
        offs = cut([b * rows for b in range(shards)])
        apieces = gather_whole(apart)
        two = gather_whole(fpart)
    piece_off = stack(s * rows, *offs)
    len_piece_off = stack(length[0], s * rows, *offs)

    add = lambda *v: sum(x.astype(F32) for x in v).astype(BF)

    class Reduce:
        def __init__(self, grads, split=False):
            self.split = split
            self.mine = grads[0]
            self.got = [lax.ppermute(g, "rep", swap) for g in grads[1:]]
            self.at = 0
            self.sums = None
            self.brought = []

        def settle(self, last):
            if self.brought:
                self.brought = after(self.brought, last)

        def step(self):
            self.at += 1
            k = self.at
            m, far, old = self.mine, self.got[2], self.brought
            if not cube:
                groups = [[2 * j + e for j in range(zs)] for e in range(2)]
                both = add(m, jnp.concatenate([jnp.stack(self.got[:2]), far], 1))
                both = lax.psum_scatter(both, "shard", scatter_dimension=1, tiled=True)
                both = lax.psum(both, "rep", axis_index_groups=groups)
                self.sums = (both[0], both[1])
                return [], []
            if self.split and k <= 3:
                return self.step_split(k)
            if k == 1:
                sent = add(m[:, : 2 * hr], jnp.stack(self.got[:2]))
                way = ("shard", yn)
            elif k == 2:
                self.first = old[0]
                sent = add(m[:, 3 * hr :], far[:, hr:], old[0][:, hr:])
                way = ("shard", xn)
            elif k == 3:
                total = add(m[:, 2 * hr : 3 * hr], far[:, :hr], self.first[:, :hr], old[0])
                lead = own == 0
                sent = jnp.where(lead, total[1], total[0])
                self.keep = jnp.where(lead, total[0], total[1])
                way = ("rep", zn(1))
            else:
                sent = self.keep = add(self.keep, old[0])
                last = k == 4 + len(zsteps)
                way = ("rep", zn(1 if last else zsteps[k - 4]))
            self.brought = [lax.ppermute(sent, *way)]
            if k == 4 + len(zsteps):
                self.sums = (self.keep, self.brought[0])
            return [sent], self.brought

        def step_split(self, k):
            m, old = self.mine, self.brought
            near, far = self.got[:2], self.got[2]
            b = [slice(i * hr, (i + 1) * hr) for i in range(4)]
            if k == 1:
                low = [add(m[0, b[3]], far[0, b[1]]), add(m[0, b[1]], near[0][b[1]])]
                sent = [jnp.concatenate(low, 0), add(m[1, : 2 * hr], near[1])]
                ways = xn, yn
            elif k == 2:
                self.first = old
                sent = [
                    add(m[0, b[0]], near[0][b[0]], old[0][b[1]]),
                    add(m[1, b[3]], far[1, b[1]], old[1][b[1]]),
                ]
                ways = yn, xn
            else:
                total = [
                    add(m[e, b[2]], far[e, b[0]], self.first[e][b[0]], old[e]) for e in range(2)
                ]
                lead = own == 0
                sent = [jnp.where(lead, total[1], total[0])]
                self.keep = jnp.where(lead, total[0], total[1])
                self.brought = [lax.ppermute(sent[0], "rep", zn(1))]
                return sent, self.brought
            self.brought = [lax.ppermute(v, "shard", w) for v, w in zip(sent, ways)]
            return sent, self.brought

        def result(self):
            while self.sums is None:
                self.step()
            sums = after(list(self.sums))
            return [*sums, *[lax.ppermute(v, "rep", swap) for v in sums]]

    flight = []

    def turn(values, last, *steps):
        nonlocal flight
        waits = flight
        flight = []
        for red in steps:
            if red.sums is None:
                red.settle(last)
                moved = red.step()
                waits = waits + moved[0]
                flight = flight + moved[1]
        return after(values, *waits) if waits else list(values)

    inv_freq = jnp.power(F32(10000.0), -jnp.arange(0, ROT, 2, dtype=F32) / ROT)
    angles = inv_freq[:, None] * jnp.arange(T, dtype=F32)[None, :]
    cos, sin = jnp.cos(angles), jnp.sin(angles)
    qkv, dot_ = proj(piece_off, n, dy, cos, sin, weights, apieces)
    half = HEADS // 2
    heads = attend(length, qkv, dot_, cos, sin, 0, half, None)
    if cube:
        *two, qkv = after([*two, qkv], heads[0])
        three = gather_second(two)
        across = [lax.ppermute(v, "rep", swap) for v in two[:2]]
    ot, dq, dk, dv = attend(length, qkv, dot_, cos, sin, half, half, heads)
    dyg = dy
    if cube:
        (dyg,) = after([dy], ot, *three, *across)
        rest = after(two[2:] + three, ot)
        across += [lax.ppermute(v, "rep", swap) for v in rest]
        fpieces = two + three + across
    else:
        fpieces = two
    grads = attn_grads(stack(*y_off), nt, dyg, ot, dq, dk, dv, hr, shards)
    if cube:
        grads = after(grads, *across[2:])
    reds = [Reduce(grads, True)]
    places = [(0, 2 * D)]
    acc = None
    dbs = []
    nk = n
    for at, size in zip(offsets, SIZES):
        (nk,) = turn([nk], dbs[-1] if dbs else dv, *reds)
        *grads, db_in, acc_o, acc_g = mlp(
            piece_off, nk, nt, dy, dyt, b_in, weights, fpieces, at, size, acc
        )
        acc = (acc_o, acc_g)
        dbs.append(db_in)
        reds.append(Reduce(grads))
        places.append((4 * D + at, 4 * D + FF + at))

    (ot,) = turn([ot], dbs[-1], *reds)
    (ot,) = after([ot], reds[-1].got[2])
    out, grad_in, vsum = final(
        len_piece_off, hidden_in, dy, gain, b_out, ot, dq, dk, dv, *acc, weights, apieces
    )
    core = stack(c, own)
    def push(last, steps, loose):
        waits = []
        for red in steps + loose:
            if red.sums is None:
                red.settle(last)
                sent = red.step()[0]
                waits = waits + (sent if red in steps else [])
        return after([core], *waits)[0] if waits else core

    args = moment_m, moment_v, weights
    vec = jnp.concatenate([vsum[0], vsum[1], db_out[0], *[d[0] for d in dbs]])
    if cube:
        vec = vec.reshape(-1, 128)
        hops = [("rep", swap), ("shard", xn), ("shard", yn)]
        hops += [("rep", zn(bit)) for bit in [1] + zsteps]
    else:
        vec = lax.psum(vec, ("rep", "shard"))
        hops = []

    def hop(last, count=1):
        nonlocal vec
        for _ in range(count):
            if hops:
                (vec,) = after([vec], last)
                vec = vec + lax.ppermute(vec, *hops.pop(0))

    big, end = None, vsum
    for i, (red, place_) in enumerate(zip(reds, places)):
        hop(end)
        near = i + 3
        ids = push(end, reds[i:near], reds[near:])
        *big, end = adam(ids, red.result(), place_, *args, big)
    while hops:
        hop(end)
    vec = vec.reshape(-1)
    vm, vv, vu = adam_math(vec, vector_m, vector_v, vectors, 0.0)
    return (out, grad_in, *big, vec, vm, vv, vu)


def solution(mesh):
    tok = P(("rep", "shard"), None)
    w = P("shard", None)
    return jax.shard_map(
        functools.partial(on_device, mesh.shape["shard"], mesh.shape["rep"]),
        mesh=mesh,
        in_specs=(tok, tok, P(("rep", "shard")), w, w, w, P(), P(), P()),
        out_specs=(tok, tok, w, w, w, w, P(), P(), P(), P()),
        check_vma=False,
    )
```

```python
import functools

import jax
import jax.numpy as jnp
import numpy as np
from jax import lax
from jax.experimental import pallas as pl
from jax.experimental.pallas import tpu as pltpu
from jax.sharding import PartitionSpec as P

D = 1024
HEADS = 16
HEAD_DIM = 64
ROT = 32
FF = 4096
T = 1024
STEP = 10

B1 = 0.9
B2 = 0.95
LR = 0.02
DECAY = 0.1
ADAM_EPS = 1e-08
NORM_EPS = 1e-05
GC = 0.7978845608028654
GA = 0.044715
LOG2E = 1.4426950408889634
LN2 = 0.6931471805599453

BF = jnp.bfloat16
F32 = jnp.float32
VLIM = 58 * 1024 * 1024
NN = (((1,), (0,)), ((), ()))
NT = (((1,), (1,)), ((), ()))
TN = (((0,), (0,)), ((), ()))
TT = (((0,), (1,)), ((), ()))
TILE = 512
SIZES = (1024, 1024, 1024, 1024)
MB = 1024
MT = 1024
TB = 256
PT = 512
FT = 256


def mm(a, b, dims=NN):
    return lax.dot_general(a, b, dims, preferred_element_type=F32)


def params():
    return pltpu.CompilerParams(
        dimension_semantics=("arbitrary",), vmem_limit_bytes=VLIM
    )


def once(shape):
    return pl.BlockSpec(shape, lambda *_: (0,) * len(shape), pipeline_mode=pl.Buffered(1))


def cost(us):
    return pl.CostEstimate(flops=int(us * 1.15e9), bytes_accessed=1024, transcendentals=0)


def prep_kernel(hr, blocks, ids, x_ref, c_ref, g_ref, b_ref, n_ref, nt_ref, d_ref, dt_ref, db_ref, s_ref):
    i = pl.program_id(0)
    x = x_ref[...].astype(F32)
    mean = jnp.mean(x, -1, keepdims=True)
    xc = x - mean
    var = jnp.mean(xc * xc, -1, keepdims=True)
    n = xc * lax.rsqrt(var + NORM_EPS) * g_ref[...] + b_ref[...]
    n_ref[...] = n.astype(BF)
    row = i * TB + lax.broadcasted_iota(jnp.int32, (TB, 1), 0)
    dy = jnp.where(row < ids[0], c_ref[...].astype(F32), 0.0)
    d_ref[...] = dy.astype(BF)

    @pl.when(i == 0)
    def _():
        db_ref[...] = jnp.zeros_like(db_ref)

    db_ref[...] += jnp.sum(dy, 0, keepdims=True)
    for val, out in ((n, nt_ref), (dy, dt_ref)):
        s_ref[...] = val.T.astype(BF)
        for b in range(2 * blocks):
            off = pl.multiple_of(ids[1 + b], hr)
            out[b * hr : (b + 1) * hr, :] = s_ref[pl.ds(off, hr), :]


def prep(ids, x, cot, gain, shift, hr, blocks):
    row = lambda i, *_: (i, 0)
    col = lambda i, *_: (0, i)
    fix = lambda i, *_: (0, 0)
    return pl.pallas_call(
        functools.partial(prep_kernel, hr, blocks),
        grid_spec=pltpu.PrefetchScalarGridSpec(
            num_scalar_prefetch=1,
            grid=(T // TB,),
            in_specs=[
                pl.BlockSpec((TB, D), row),
                pl.BlockSpec((TB, D), row),
                pl.BlockSpec((1, D), fix),
                pl.BlockSpec((1, D), fix),
            ],
            out_specs=[
                pl.BlockSpec((TB, D), row),
                pl.BlockSpec((D, TB), col),
                pl.BlockSpec((TB, D), row),
                pl.BlockSpec((D, TB), col),
                pl.BlockSpec((1, D), fix),
            ],
            scratch_shapes=[pltpu.VMEM((D, TB), BF)],
        ),
        out_shape=[
            jax.ShapeDtypeStruct((T, D), BF),
            jax.ShapeDtypeStruct((D, T), BF),
            jax.ShapeDtypeStruct((T, D), BF),
            jax.ShapeDtypeStruct((D, T), BF),
            jax.ShapeDtypeStruct((1, D), F32),
        ],
        compiler_params=params(),
        cost_estimate=cost(8),
    )(ids, x, cot, gain, shift)


def place(dst, srcs, ids, base):
    for k, src in enumerate(srcs):
        rows = src.shape[0]
        dst[pl.ds(pl.multiple_of(ids[base + k], rows), rows), :] = src[...]


def spread(g, e, mine, near, far):
    a, b = D // 2, 3 * D // 4
    mine[e] = g[:a, :]
    near[...] = g[a:b, :]
    far[e] = g[b:, :]


def grad_shapes(n):
    return [
        jax.ShapeDtypeStruct(v, BF)
        for v in ((2, D // 2, n), (D // 4, n), (D // 4, n), (2, D // 4, n))
    ]


def mlp_kernel(np_, first, ids, n_ref, nt_ref, d_ref, dt_ref, b_ref, *refs):
    win = refs[:np_]
    wout = refs[np_ : 2 * np_]
    refs = refs[2 * np_ :]
    if not first:
        oin, gin = refs[:2]
        refs = refs[2:]
    gm, g0, g1, gf = refs[:4]
    db_ref, o_out, g_out, wi, wo, h_s, p_s, o_ref, g_ref = refs[4:]
    j = pl.program_id(0)
    place(wi, win, ids, 0)
    place(wo, wout, ids, 0)
    bias = b_ref[...]
    wi_v = wi[...]
    wo_v = wo[...]
    db = jnp.zeros((1, MT), F32)
    for t in range(T // MB):
        rows = slice(t * MB, (t + 1) * MB)
        pre = mm(n_ref[rows, :], wi_v) + bias
        dh = mm(d_ref[rows, :], wo_v)
        sq = pre * pre
        th = jnp.tanh(GC * pre * (1.0 + GA * sq))
        half = 0.5 * (1.0 + th)
        h = (pre * half).astype(BF)
        slope = half + 0.5 * pre * (1.0 - th * th) * (GC + (3.0 * GA * GC) * sq)
        dp = (dh * slope).astype(BF)
        h_s[rows, :] = h
        p_s[rows, :] = dp
        db = db + jnp.sum(dp.astype(F32), 0, keepdims=True)
        ov = mm(h, wo_v, NT)
        gv = mm(wi_v, dp, NT)

        if first:

            @pl.when(j == 0)
            def _():
                o_ref[rows, :] = ov
                g_ref[:, rows] = gv

        else:

            @pl.when(j == 0)
            def _():
                o_ref[rows, :] = oin[rows, :].astype(F32) + ov
                g_ref[:, rows] = gin[:, rows].astype(F32) + gv

        @pl.when(j > 0)
        def _():
            o_ref[rows, :] += ov
            g_ref[:, rows] += gv

    @pl.when(j == pl.num_programs(0) - 1)
    def _():
        o_out[...] = o_ref[...].astype(BF)
        g_out[...] = g_ref[...].astype(BF)

    db_ref[...] = db
    hv = h_s[...]
    pv = p_s[...]
    for e, (left, right) in enumerate(((nt_ref, pv), (dt_ref, hv))):
        spread(mm(left[...], right).astype(BF), e, gm, (g0, g1)[e], gf)


def mlp(ids, n, nt, dy, dyt, bias, weights, pieces, offset, size, acc):
    first = acc is None
    nt_cols = size // MT
    tall = lambda cols: pl.BlockSpec((T, cols), lambda j, *_: (0, 0))
    own_rows = weights.shape[0]
    in_base = (4 * D + offset) // MT
    out_base = (4 * D + FF + offset) // MT
    wspecs = []
    for base_own, base in ((in_base, offset // MT), (out_base, (FF + offset) // MT)):
        if own_rows:
            wspecs.append(pl.BlockSpec((own_rows, MT), lambda j, *_, b=base_own: (0, b + j)))
        for p in pieces:
            wspecs.append(pl.BlockSpec((p.shape[0], MT), lambda j, *_, b=base: (0, b + j)))
    wargs = [weights, *pieces]
    bb = offset // MT
    flat = pl.BlockSpec((D // 4, MT), lambda j, *_: (0, j))
    deep = lambda r: pl.BlockSpec((2, r, MT), lambda j, *_: (0, 0, j))
    gspecs = [deep(D // 2), flat, flat, deep(D // 4)]
    return pl.pallas_call(
        functools.partial(mlp_kernel, len(wargs), first),
        grid_spec=pltpu.PrefetchScalarGridSpec(
            num_scalar_prefetch=1,
            grid=(nt_cols,),
            in_specs=[
                once((T, D)),
                once((D, T)),
                once((T, D)),
                once((D, T)),
                pl.BlockSpec((1, MT), lambda j, *_: (0, bb + j)),
                *wspecs,
                *([] if first else [once((T, D)), once((D, T))]),
            ],
            out_specs=[
                *gspecs,
                pl.BlockSpec((1, MT), lambda j, *_: (0, j)),
                once((T, D)),
                once((D, T)),
            ],
            scratch_shapes=[
                pltpu.VMEM((D, MT), BF),
                pltpu.VMEM((D, MT), BF),
                pltpu.VMEM((T, MT), BF),
                pltpu.VMEM((T, MT), BF),
                pltpu.VMEM((T, D), F32),
                pltpu.VMEM((D, T), F32),
            ],
        ),
        out_shape=[
            *grad_shapes(size),
            jax.ShapeDtypeStruct((1, size), F32),
            jax.ShapeDtypeStruct((T, D), BF),
            jax.ShapeDtypeStruct((D, T), BF),
        ],
        compiler_params=params(),
        cost_estimate=cost(41 * size / 2048),
    )(ids, n, nt, dy, dyt, bias, *wargs, *wargs, *([] if first else acc))


def proj_kernel(np_, ids, n_ref, d_ref, cos_ref, sin_ref, *refs):
    wq = refs[:np_]
    wo = refs[np_ : 2 * np_]
    out_ref, dout_ref, w_s, wo_s = refs[2 * np_ :]
    j = pl.program_id(0)
    place(w_s, wq, ids, 0)
    r = mm(w_s[...], n_ref[...], TT)

    def rotated(scale):
        for h in range(PT // HEAD_DIM):
            b = h * HEAD_DIM
            u = r[b : b + 16, :]
            w = r[b + 16 : b + 32, :]
            cs = cos_ref[...]
            sn = sin_ref[...]
            turned = [u * cs - w * sn, w * cs + u * sn, r[b + 32 : b + 64, :]]
            out_ref[b : b + 64, :] = (jnp.concatenate(turned, 0) * scale).astype(BF)

    @pl.when(j < D // PT)
    def _():
        rotated(LOG2E * HEAD_DIM ** (-0.5))

    @pl.when((j >= D // PT) & (j < 2 * D // PT))
    def _():
        rotated(1.0)

    @pl.when(j >= 2 * D // PT)
    def _():
        out_ref[...] = r.astype(BF)

    @pl.when(j == 0)
    def _():
        place(wo_s, wo, ids, 0)
        dout_ref[...] = mm(wo_s[...], d_ref[...], NT).astype(BF)


def proj(ids, n, dy, cos, sin, weights, pieces):
    wargs = [weights, *pieces]
    return pl.pallas_call(
        functools.partial(proj_kernel, len(wargs)),
        grid_spec=pltpu.PrefetchScalarGridSpec(
            num_scalar_prefetch=1,
            grid=(3 * D // PT,),
            in_specs=[
                once((T, D)),
                once((T, D)),
                once((16, T)),
                once((16, T)),
                *[pl.BlockSpec((w.shape[0], PT), lambda j, *_: (0, j)) for w in wargs],
                *[
                    pl.BlockSpec((w.shape[0], D), lambda j, *_: (0, 3), pipeline_mode=pl.Buffered(1))
                    for w in wargs
                ],
            ],
            out_specs=[
                pl.BlockSpec((PT, T), lambda j, *_: (j, 0)),
                once((D, T)),
            ],
            scratch_shapes=[pltpu.VMEM((D, PT), BF), pltpu.VMEM((D, D), BF)],
        ),
        out_shape=[
            jax.ShapeDtypeStruct((3 * D, T), BF),
            jax.ShapeDtypeStruct((D, T), BF),
        ],
        compiler_params=params(),
        cost_estimate=cost(20),
    )(ids, n, dy, cos, sin, *wargs, *wargs)


QB = 512
HPS = 2


def attn_kernel(n_alias, len_ref, q_ref, k_ref, v_ref, do_ref, cos_ref, sin_ref, *refs):
    o_ref, dq_ref, dk_ref, dv_ref = refs[n_alias:]
    sub = lax.broadcasted_iota(jnp.int32, (HEAD_DIM, T), 0)
    lane = lax.broadcasted_iota(jnp.int32, (HEAD_DIM, T), 1)
    bias = jnp.where((sub == 0) & (lane >= len_ref[0]), -1e30, 0.0)
    ones = jnp.where(sub == 0, 1.0, 0.0).astype(BF)
    none = jnp.zeros((HEAD_DIM, T), F32)
    ki = lax.broadcasted_iota(jnp.int32, (QB, QB), 0)
    qi = lax.broadcasted_iota(jnp.int32, (QB, QB), 1)

    def unrot(val, cs, sn, out, base, cols):
        a = val[0:16, :]
        b = val[16:32, :]
        turned = [a * cs + b * sn, b * cs - a * sn, val[32:64, :]]
        out[base : base + 64, cols] = jnp.concatenate(turned, 0).astype(BF)

    for h in range(HPS):
        b = h * HEAD_DIM
        hs = slice(b, b + HEAD_DIM)
        q = q_ref[hs, :]
        k = k_ref[hs, :]
        v = v_ref[hs, :]
        qa = jnp.concatenate([q, ones], 0)
        ka = jnp.concatenate([k.astype(F32), bias], 0).T.astype(BF)
        vt = jnp.concatenate([v.astype(F32), none], 0).T.astype(BF)
        dk = [jnp.zeros((HEAD_DIM, QB), F32) for _ in range(T // QB)]
        dv = [jnp.zeros((HEAD_DIM, QB), F32) for _ in range(T // QB)]
        for i in range(T // QB):
            qs = slice(i * QB, (i + 1) * QB)
            kk = (i + 1) * QB
            st = mm(ka[:kk, :], qa[:, qs])
            diag = jnp.where(ki <= qi, st[kk - QB :, :], -1e30)
            st = diag if i == 0 else jnp.concatenate([st[: kk - QB, :], diag], 0)
            e = jnp.exp2(st - jnp.max(st, 0, keepdims=True))
            rl = 1.0 / jnp.sum(e, 0, keepdims=True)
            eb = e.astype(BF)
            ot = mm(v[:, :kk], eb) * rl
            o_ref[hs, qs] = ot.astype(BF)
            dn = (do_ref[hs, qs].astype(F32) * rl).astype(BF)
            delta = jnp.sum(dn.astype(F32) * ot, 0, keepdims=True)
            da = jnp.concatenate([dn, none[:, qs].astype(BF)], 0)
            ds = (e * (mm(vt[:kk, :], da) - delta)).astype(BF)
            dq = mm(k[:, :kk], ds) * (HEAD_DIM ** (-0.5))
            unrot(dq, cos_ref[:, qs], sin_ref[:, qs], dq_ref, b, qs)
            dvi = mm(dn, eb, NT)
            dki = mm(q[:, qs], ds, NT)
            for t in range(i + 1):
                ts = slice(t * QB, (t + 1) * QB)
                dv[t] = dv[t] + dvi[:, ts]
                dk[t] = dk[t] + dki[:, ts]
        for t in range(T // QB):
            ts = slice(t * QB, (t + 1) * QB)
            dv_ref[hs, ts] = dv[t].astype(BF)
            unrot(dk[t] * LN2, cos_ref[:, ts], sin_ref[:, ts], dk_ref, b, ts)


def attend(length, qkv, dot_, cos, sin, first, heads, before):
    rows = HPS * HEAD_DIM
    steps = HEADS // HPS
    at = first // HPS
    spec = lambda base: pl.BlockSpec((rows, T), lambda h, *_: (base + at + h, 0))
    shape = jax.ShapeDtypeStruct((D, T), BF)
    alias = [] if before is None else list(before)
    return pl.pallas_call(
        functools.partial(attn_kernel, len(alias)),
        grid_spec=pltpu.PrefetchScalarGridSpec(
            num_scalar_prefetch=1,
            grid=(heads // HPS,),
            in_specs=[
                spec(0),
                spec(steps),
                spec(2 * steps),
                spec(0),
                once((16, T)),
                once((16, T)),
            ]
            + [pl.BlockSpec(memory_space=pl.ANY)] * len(alias),
            out_specs=[spec(0)] * 4,
        ),
        out_shape=[shape] * 4,
        input_output_aliases={7 + i: i for i in range(len(alias))},
        compiler_params=params(),
        cost_estimate=cost(46 * heads / HEADS),
    )(length, qkv, qkv, qkv, dot_, cos, sin, *alias)


def agrad_kernel(hr, blocks, ids, nt_ref, dy_ref, o_ref, dq_ref, dk_ref, dv_ref, gm, g0, g1, gf, g_s):
    j = pl.program_id(0)
    for at, (src, near) in enumerate(((dq_ref, g0), (dk_ref, g0), (dv_ref, g1))):

        @pl.when((j >= 2 * at) & (j < 2 * at + 2))
        def _(src=src, near=near):
            spread(mm(nt_ref[...], src[...], NT).astype(BF), 0, gm, near, gf)

    @pl.when(j >= 6)
    def _():
        g_s[...] = mm(o_ref[...], dy_ref[...]).astype(BF)
        rows = [pl.multiple_of(ids[b], hr) for b in range(2 * blocks)]
        spread(jnp.concatenate([g_s[pl.ds(k, hr), :] for k in rows], 0), 0, gm, g1, gf)


def attn_grads(ids, nt, dy, ot, dq, dk, dv, hr, blocks):
    def grab(at):
        return pl.BlockSpec((TILE, T), lambda j, *_: (jnp.clip(j - 2 * at, 0, 1), 0))

    deep = lambda r: pl.BlockSpec((1, r, TILE), lambda j, *_: (j // 4, 0, j % 4))
    gspecs = [
        deep(D // 2),
        pl.BlockSpec((D // 4, TILE), lambda j, *_: (0, jnp.minimum(j, 3))),
        pl.BlockSpec((D // 4, TILE), lambda j, *_: (0, jnp.maximum(j - 4, 0))),
        deep(D // 4),
    ]
    return pl.pallas_call(
        functools.partial(agrad_kernel, hr, blocks),
        grid_spec=pltpu.PrefetchScalarGridSpec(
            num_scalar_prefetch=1,
            grid=(4 * D // TILE,),
            in_specs=[
                once((D, T)),
                pl.BlockSpec((T, TILE), lambda j, *_: (0, jnp.clip(j - 6, 0, 1))),
                once((D, T)),
                grab(0),
                grab(1),
                grab(2),
            ],
            out_specs=gspecs,
            scratch_shapes=[pltpu.VMEM((D, TILE), BF)],
        ),
        out_shape=grad_shapes(2 * D),
        compiler_params=params(),
        cost_estimate=cost(17),
    )(ids, nt, dy, ot, dq, dk, dv)


def final_kernel(np_, ids, x_ref, dy_ref, g_ref, bo_ref, o_ref, dq_ref, dk_ref, dv_ref, ao_ref, ag_ref, *refs):
    wq = refs[:np_]
    out_ref, gin_ref, v_ref, w_s = refs[np_:]
    i = pl.program_id(0)

    @pl.when(i == 0)
    def _():
        place(w_s, wq, ids, 1)

    x = x_ref[...].astype(F32)
    row = i * FT + lax.broadcasted_iota(jnp.int32, (FT, 1), 0)
    attn = mm(o_ref[...], w_s[:, 3 * D :], TN)
    out = x + attn + ao_ref[...].astype(F32) + bo_ref[...]
    out_ref[...] = jnp.where(row < ids[0], out, 0.0).astype(BF)
    dn = (
        ag_ref[...].astype(F32)
        + mm(w_s[:, :D], dq_ref[...])
        + mm(w_s[:, D : 2 * D], dk_ref[...])
        + mm(w_s[:, 2 * D : 3 * D], dv_ref[...])
    ).T
    mean = jnp.mean(x, -1, keepdims=True)
    xc = x - mean
    inv = lax.rsqrt(jnp.mean(xc * xc, -1, keepdims=True) + NORM_EPS)
    xh = xc * inv
    g = dn * g_ref[...]
    gx = dn * xh
    ln = inv * (
        g - jnp.mean(g, -1, keepdims=True) - xh * jnp.mean(g * xh, -1, keepdims=True)
    )
    gin_ref[...] = (dy_ref[...].astype(F32) + ln).astype(BF)

    @pl.when(i == 0)
    def _():
        v_ref[...] = jnp.zeros_like(v_ref)

    v_ref[0:1, :] += jnp.sum(gx, 0, keepdims=True)
    v_ref[1:2, :] += jnp.sum(dn, 0, keepdims=True)


def final(ids, x, dy, gain, b_out, ot, dq, dk, dv, acc_o, acc_g, weights, pieces):
    row = pl.BlockSpec((FT, D), lambda i, *_: (i, 0))
    col = pl.BlockSpec((D, FT), lambda i, *_: (0, i))
    vec = pl.BlockSpec((1, D), lambda i, *_: (0, 0))
    wargs = [weights, *pieces]
    return pl.pallas_call(
        functools.partial(final_kernel, len(wargs)),
        grid_spec=pltpu.PrefetchScalarGridSpec(
            num_scalar_prefetch=1,
            grid=(T // FT,),
            in_specs=[
                row,
                row,
                vec,
                vec,
                col,
                col,
                col,
                col,
                row,
                col,
                *[once((w.shape[0], 4 * D)) for w in wargs],
            ],
            out_specs=[row, row, pl.BlockSpec((8, D), lambda i, *_: (0, 0))],
            scratch_shapes=[pltpu.VMEM((D, 4 * D), BF)],
        ),
        out_shape=[
            jax.ShapeDtypeStruct((T, D), BF),
            jax.ShapeDtypeStruct((T, D), BF),
            jax.ShapeDtypeStruct((8, D), F32),
        ],
        compiler_params=params(),
        cost_estimate=cost(20),
    )(ids, x, dy, gain, b_out, ot, dq, dk, dv, acc_o, acc_g, *wargs)


C1 = float(1.0 - np.float32(B1) ** np.float32(STEP))
C2 = float(1.0 - np.float32(B2) ** np.float32(STEP))


def adam_math(g, m, v, w, decay):
    nm = B1 * m + (1.0 - B1) * g
    nv = B2 * v + (1.0 - B2) * g * g
    up = -LR * (nm / C1 / (jnp.sqrt(nv / C2) + ADAM_EPS) + decay * w)
    return nm, nv, up


def adam_kernel(n_alias, first, ids, sm, rm, so, ro, m_ref, v_ref, w_ref, *refs):
    wg_ref, nm_ref, nv_ref, up_ref, end_ref = refs[n_alias:]
    end_ref[...] = jnp.zeros_like(end_ref)
    summed = pl.program_id(0) + first == ids[1]
    hr = sm.shape[0]
    mine = jnp.where(summed, sm[...].astype(F32), rm[...].astype(F32))
    other = jnp.where(summed, so[...].astype(F32), ro[...].astype(F32))
    lead = ids[0] == 0
    for h, g in enumerate((jnp.where(lead, mine, other), jnp.where(lead, other, mine))):
        rows = slice(h * hr, (h + 1) * hr)
        nm, nv, up = adam_math(g, m_ref[rows, :], v_ref[rows, :], w_ref[rows, :].astype(F32), DECAY)
        wg_ref[rows, :] = g
        nm_ref[rows, :] = nm
        nv_ref[rows, :] = nv
        up_ref[rows, :] = up


def adam(ids, grads, cols, m, v, w, outs, first=0, count=2):
    rows, width = m.shape
    hr = rows // 2
    n = grads[0].shape[1]
    AC = 1024 if n % 1024 == 0 else 512
    pick = lambda hit: pl.BlockSpec(
        (hr, AC), lambda p, j, ids: (0, jnp.where((p + first == ids[1]) == hit, j, 0))
    )
    b0, b1 = cols[0] // AC, cols[1] // AC
    big = pl.BlockSpec((rows, AC), lambda p, j, ids: (0, jnp.where(p + first == 0, b0, b1) + j))
    alias = [] if outs is None else list(outs)
    return pl.pallas_call(
        functools.partial(adam_kernel, len(alias), first),
        grid_spec=pltpu.PrefetchScalarGridSpec(
            num_scalar_prefetch=1,
            grid=(count, n // AC),
            in_specs=[pick(True), pick(False), pick(True), pick(False), big, big, big]
            + [pl.BlockSpec(memory_space=pl.ANY)] * len(alias),
            out_specs=[big] * 4 + [pl.BlockSpec((8, 128), lambda p, j, ids: (0, 0))],
        ),
        out_shape=[jax.ShapeDtypeStruct((rows, width), F32)] * 4
        + [jax.ShapeDtypeStruct((8, 128), F32)],
        input_output_aliases={8 + i: i for i in range(len(alias))},
        compiler_params=pltpu.CompilerParams(
            dimension_semantics=("arbitrary", "arbitrary"), vmem_limit_bytes=VLIM
        ),
        cost_estimate=cost(6 * count * n / 2048),
    )(ids, *grads, m, v, w, *alias)


def after(values, *waits):
    flat = lax.optimization_barrier((*values, *waits))
    return list(flat[: len(values)])


def on_device(shards, reps, hidden_in, cotangent, lengths, weights, moment_m, moment_v, vectors, vector_m, vector_v):
    s = lax.axis_index("shard")
    rep = lax.axis_index("rep")
    c = rep % 2
    z = rep // 2
    zs = reps // 2
    swap = [(i, i ^ 1) for i in range(reps)]
    rows = weights.shape[0]
    hr = rows // 2
    i32 = jnp.int32
    cube = shards == 4 and zs & (zs - 1) == 0 and zs >= 4
    xn = [(i, i ^ 1) for i in range(shards)]
    yn = [(i, i ^ 2) for i in range(shards)]
    zsteps = [3] + [1 << k for k in range(2, 16) if 1 << k < zs]
    zn = lambda bit: [(i, i ^ (2 * bit)) for i in range(reps)]
    own = ((z ^ (z // 2)) % 2) if cube else jnp.int32(0)

    if cube:
        y_rows = [(s ^ r) * rows for r in (2, 3, 0, 1)]
    else:
        y_rows = [r * rows for r in range(shards)]
    cut = lambda at: [b + c * hr for b in at] + [b + (1 - c) * hr for b in at]
    y_off = cut(y_rows)
    stack = lambda *v: jnp.stack([jnp.asarray(x, i32) for x in v])
    length = lengths.astype(i32)
    gain = vectors[:D].reshape(1, D)
    shift = vectors[D : 2 * D].reshape(1, D)
    b_out = vectors[2 * D : 3 * D].reshape(1, D)
    b_in = vectors[3 * D :].reshape(1, FF)
    half_w = lax.dynamic_slice_in_dim(weights, c * hr, hr, 0)

    n, nt, dy, dyt, db_out = prep(
        stack(length[0], *y_off), hidden_in, cotangent, gain, shift, hr, shards
    )

    def part_of(cols):
        return jnp.concatenate([half_w[:, a:b] for a, b in cols], 1)

    q = hr // 2

    def gather_first(part):
        a, b = part[:q], part[q:]
        return [
            lax.ppermute(p, "shard", way) for p, way in ((a, xn), (b, yn), (b, xn), (a, yn))
        ]

    def gather_second(first):
        return [lax.ppermute(first[0], "shard", yn), lax.ppermute(first[1], "shard", xn)]

    def swapped(mine):
        return mine + [lax.ppermute(p, "rep", swap) for p in mine]

    def gather_whole(part):
        full = lax.all_gather(part, "shard", axis=0, tiled=True)
        other = lax.ppermute(full, "rep", swap)
        return [p[b * hr : (b + 1) * hr] for p in (full, other) for b in range(shards)]

    offsets = [0]
    for size in SIZES:
        offsets.append(offsets[-1] + size)
    apart, fpart = part_of([(0, 4 * D)]), part_of([(4 * D, 4 * D + 2 * FF)])
    if cube:
        base = [(s ^ r) * rows + e * q for r, e in ((1, 0), (2, 1), (1, 1), (2, 0), (3, 0), (3, 1))]
        offs = [b + c * hr for b in base] + [b + (1 - c) * hr for b in base]
        one = gather_first(apart)
        one[:2] = after(one[:2], n)
        one = one + gather_second(one)
        (fpart,) = after([fpart], *one)
        apieces = swapped(one)
        two = gather_first(fpart)
    else:
        offs = cut([b * rows for b in range(shards)])
        apieces = gather_whole(apart)
        two = gather_whole(fpart)
    piece_off = stack(s * rows, *offs)
    len_piece_off = stack(length[0], s * rows, *offs)

    add = lambda *v: sum(x.astype(F32) for x in v).astype(BF)

    class Reduce:
        def __init__(self, grads, split=False):
            self.split = split
            self.mine = grads[0]
            self.got = [lax.ppermute(g, "rep", swap) for g in grads[1:]]
            self.at = 0
            self.sums = None
            self.brought = []

        def settle(self, last):
            if self.brought:
                self.brought = after(self.brought, last)

        def step(self):
            self.at += 1
            k = self.at
            m, far, old = self.mine, self.got[2], self.brought
            if not cube:
                groups = [[2 * j + e for j in range(zs)] for e in range(2)]
                both = add(m, jnp.concatenate([jnp.stack(self.got[:2]), far], 1))
                both = lax.psum_scatter(both, "shard", scatter_dimension=1, tiled=True)
                both = lax.psum(both, "rep", axis_index_groups=groups)
                self.sums = (both[0], both[1])
                return [], []
            if self.split and k <= 3:
                return self.step_split(k)
            if k == 1:
                sent = add(m[:, : 2 * hr], jnp.stack(self.got[:2]))
                way = ("shard", yn)
            elif k == 2:
                self.first = old[0]
                sent = add(m[:, 3 * hr :], far[:, hr:], old[0][:, hr:])
                way = ("shard", xn)
            elif k == 3:
                total = add(m[:, 2 * hr : 3 * hr], far[:, :hr], self.first[:, :hr], old[0])
                lead = own == 0
                sent = jnp.where(lead, total[1], total[0])
                self.keep = jnp.where(lead, total[0], total[1])
                way = ("rep", zn(1))
            else:
                sent = self.keep = add(self.keep, old[0])
                last = k == 4 + len(zsteps)
                way = ("rep", zn(1 if last else zsteps[k - 4]))
            self.brought = [lax.ppermute(sent, *way)]
            if k == 4 + len(zsteps):
                self.sums = (self.keep, self.brought[0])
            return [sent], self.brought

        def step_split(self, k):
            m, old = self.mine, self.brought
            near, far = self.got[:2], self.got[2]
            b = [slice(i * hr, (i + 1) * hr) for i in range(4)]
            if k == 1:
                low = [add(m[0, b[3]], far[0, b[1]]), add(m[0, b[1]], near[0][b[1]])]
                sent = [jnp.concatenate(low, 0), add(m[1, : 2 * hr], near[1])]
                ways = xn, yn
            elif k == 2:
                self.first = old
                sent = [
                    add(m[0, b[0]], near[0][b[0]], old[0][b[1]]),
                    add(m[1, b[3]], far[1, b[1]], old[1][b[1]]),
                ]
                ways = yn, xn
            else:
                total = [
                    add(m[e, b[2]], far[e, b[0]], self.first[e][b[0]], old[e]) for e in range(2)
                ]
                lead = own == 0
                sent = [jnp.where(lead, total[1], total[0])]
                self.keep = jnp.where(lead, total[0], total[1])
                self.brought = [lax.ppermute(sent[0], "rep", zn(1))]
                return sent, self.brought
            self.brought = [lax.ppermute(v, "shard", w) for v, w in zip(sent, ways)]
            return sent, self.brought

        def result(self, *waits):
            while self.sums is None:
                self.step()
            sums = after(list(self.sums), *waits)
            return [*sums, *[lax.ppermute(v, "rep", swap) for v in sums]]

    flight = []

    def turn(values, last, *steps):
        nonlocal flight
        waits = flight
        flight = []
        for red in steps:
            if red.sums is None:
                red.settle(last)
                moved = red.step()
                waits = waits + moved[0]
                flight = flight + moved[1]
        return after(values, *waits) if waits else list(values)

    inv_freq = jnp.power(F32(10000.0), -jnp.arange(0, ROT, 2, dtype=F32) / ROT)
    angles = inv_freq[:, None] * jnp.arange(T, dtype=F32)[None, :]
    cos, sin = jnp.cos(angles), jnp.sin(angles)
    qkv, dot_ = proj(piece_off, n, dy, cos, sin, weights, apieces)
    half = HEADS // 2
    heads = attend(length, qkv, dot_, cos, sin, 0, half, None)
    if cube:
        *two, qkv = after([*two, qkv], heads[0])
        three = gather_second(two)
        across = [lax.ppermute(v, "rep", swap) for v in two[:2]]
    ot, dq, dk, dv = attend(length, qkv, dot_, cos, sin, half, half, heads)
    dyg = dy
    if cube:
        (dyg,) = after([dy], ot, *three, *across)
        rest = after(two[2:] + three, ot)
        across += [lax.ppermute(v, "rep", swap) for v in rest]
        fpieces = two + three + across
    else:
        fpieces = two
    grads = attn_grads(stack(*y_off), nt, dyg, ot, dq, dk, dv, hr, shards)
    if cube:
        grads = after(grads, *across[2:])
    reds = [Reduce(grads, True)]
    places = [(0, 2 * D)]
    acc = None
    dbs = []
    nk = n
    for at, size in zip(offsets, SIZES):
        (nk,) = turn([nk], dbs[-1] if dbs else dv, *reds)
        *grads, db_in, acc_o, acc_g = mlp(
            piece_off, nk, nt, dy, dyt, b_in, weights, fpieces, at, size, acc
        )
        acc = (acc_o, acc_g)
        dbs.append(db_in)
        reds.append(Reduce(grads))
        places.append((4 * D + at, 4 * D + FF + at))

    (ot,) = turn([ot], dbs[-1], *reds)
    (ot,) = after([ot], reds[-1].got[2])
    out, grad_in, vsum = final(
        len_piece_off, hidden_in, dy, gain, b_out, ot, dq, dk, dv, *acc, weights, apieces
    )
    core = stack(c, own)
    def push(last, steps, loose):
        waits = []
        for red in steps + loose:
            if red.sums is None:
                red.settle(last)
                sent = red.step()[0]
                waits = waits + (sent if red in steps else [])
        return after([core], *waits)[0] if waits else core

    args = moment_m, moment_v, weights
    vec = jnp.concatenate([vsum[0], vsum[1], db_out[0], *[d[0] for d in dbs]])
    if cube:
        vec = vec.reshape(-1, 128)
        hops = [("rep", swap), ("shard", xn), ("shard", yn)]
        hops += [("rep", zn(bit)) for bit in [1] + zsteps]
    else:
        vec = lax.psum(vec, ("rep", "shard"))
        hops = []

    def hop(last, count=1):
        nonlocal vec
        for _ in range(count):
            if hops:
                (vec,) = after([vec], last)
                vec = vec + lax.ppermute(vec, *hops.pop(0))

    big, end = None, vsum
    for i, (red, place_) in enumerate(zip(reds, places)):
        hop(end)
        near = i + 3
        ids = push(end, reds[i:near], reds[near:])
        *big, end = adam(ids, red.result(*([] if i else [vsum])), place_, *args, big)
    while hops:
        hop(end)
    vec = vec.reshape(-1)
    vm, vv, vu = adam_math(vec, vector_m, vector_v, vectors, 0.0)
    return (out, grad_in, *big, vec, vm, vv, vu)


def solution(mesh):
    tok = P(("rep", "shard"), None)
    w = P("shard", None)
    return jax.shard_map(
        functools.partial(on_device, mesh.shape["shard"], mesh.shape["rep"]),
        mesh=mesh,
        in_specs=(tok, tok, P(("rep", "shard")), w, w, w, P(), P(), P()),
        out_specs=(tok, tok, w, w, w, w, P(), P(), P(), P()),
        check_vma=False,
    )
```

```python
import functools

import jax
import jax.numpy as jnp
import numpy as np
from jax import lax
from jax.experimental import pallas as pl
from jax.experimental.pallas import tpu as pltpu
from jax.sharding import PartitionSpec as P

D = 1024
HEADS = 16
HEAD_DIM = 64
ROT = 32
FF = 4096
T = 1024
STEP = 10

B1 = 0.9
B2 = 0.95
LR = 0.02
DECAY = 0.1
ADAM_EPS = 1e-08
NORM_EPS = 1e-05
GC = 0.7978845608028654
GA = 0.044715
LOG2E = 1.4426950408889634
LN2 = 0.6931471805599453

BF = jnp.bfloat16
F32 = jnp.float32
VLIM = 58 * 1024 * 1024
NN = (((1,), (0,)), ((), ()))
NT = (((1,), (1,)), ((), ()))
TN = (((0,), (0,)), ((), ()))
TT = (((0,), (1,)), ((), ()))
TILE = 512
SIZES = (1024, 1024, 1024, 1024)
MB = 1024
MT = 1024
TB = 256
PT = 512
FT = 256


def mm(a, b, dims=NN):
    return lax.dot_general(a, b, dims, preferred_element_type=F32)


def params():
    return pltpu.CompilerParams(
        dimension_semantics=("arbitrary",), vmem_limit_bytes=VLIM
    )


def once(shape):
    return pl.BlockSpec(shape, lambda *_: (0,) * len(shape), pipeline_mode=pl.Buffered(1))


def cost(us):
    return pl.CostEstimate(flops=int(us * 1.15e9), bytes_accessed=1024, transcendentals=0)


def prep_kernel(hr, blocks, ids, x_ref, c_ref, g_ref, b_ref, n_ref, nt_ref, d_ref, dt_ref, db_ref, s_ref):
    i = pl.program_id(0)
    x = x_ref[...].astype(F32)
    mean = jnp.mean(x, -1, keepdims=True)
    xc = x - mean
    var = jnp.mean(xc * xc, -1, keepdims=True)
    n = xc * lax.rsqrt(var + NORM_EPS) * g_ref[...] + b_ref[...]
    n_ref[...] = n.astype(BF)
    row = i * TB + lax.broadcasted_iota(jnp.int32, (TB, 1), 0)
    dy = jnp.where(row < ids[0], c_ref[...].astype(F32), 0.0)
    d_ref[...] = dy.astype(BF)

    @pl.when(i == 0)
    def _():
        db_ref[...] = jnp.zeros_like(db_ref)

    db_ref[...] += jnp.sum(dy, 0, keepdims=True)
    for val, out in ((n, nt_ref), (dy, dt_ref)):
        s_ref[...] = val.T.astype(BF)
        for b in range(2 * blocks):
            off = pl.multiple_of(ids[1 + b], hr)
            out[b * hr : (b + 1) * hr, :] = s_ref[pl.ds(off, hr), :]


def prep(ids, x, cot, gain, shift, hr, blocks):
    row = lambda i, *_: (i, 0)
    col = lambda i, *_: (0, i)
    fix = lambda i, *_: (0, 0)
    return pl.pallas_call(
        functools.partial(prep_kernel, hr, blocks),
        grid_spec=pltpu.PrefetchScalarGridSpec(
            num_scalar_prefetch=1,
            grid=(T // TB,),
            in_specs=[
                pl.BlockSpec((TB, D), row),
                pl.BlockSpec((TB, D), row),
                pl.BlockSpec((1, D), fix),
                pl.BlockSpec((1, D), fix),
            ],
            out_specs=[
                pl.BlockSpec((TB, D), row),
                pl.BlockSpec((D, TB), col),
                pl.BlockSpec((TB, D), row),
                pl.BlockSpec((D, TB), col),
                pl.BlockSpec((1, D), fix),
            ],
            scratch_shapes=[pltpu.VMEM((D, TB), BF)],
        ),
        out_shape=[
            jax.ShapeDtypeStruct((T, D), BF),
            jax.ShapeDtypeStruct((D, T), BF),
            jax.ShapeDtypeStruct((T, D), BF),
            jax.ShapeDtypeStruct((D, T), BF),
            jax.ShapeDtypeStruct((1, D), F32),
        ],
        compiler_params=params(),
        cost_estimate=cost(8),
    )(ids, x, cot, gain, shift)


def place(dst, srcs, ids, base):
    for k, src in enumerate(srcs):
        rows = src.shape[0]
        dst[pl.ds(pl.multiple_of(ids[base + k], rows), rows), :] = src[...]


def spread(g, e, mine, near, far):
    a, b = D // 2, 3 * D // 4
    mine[e] = g[:a, :]
    near[...] = g[a:b, :]
    far[e] = g[b:, :]


def grad_shapes(n):
    return [
        jax.ShapeDtypeStruct(v, BF)
        for v in ((2, D // 2, n), (D // 4, n), (D // 4, n), (2, D // 4, n))
    ]


def mlp_kernel(np_, first, ids, n_ref, nt_ref, d_ref, dt_ref, b_ref, *refs):
    win = refs[:np_]
    wout = refs[np_ : 2 * np_]
    refs = refs[2 * np_ :]
    if not first:
        oin, gin = refs[:2]
        refs = refs[2:]
    gm, g0, g1, gf = refs[:4]
    db_ref, o_out, g_out, wi, wo, h_s, p_s, o_ref, g_ref = refs[4:]
    j = pl.program_id(0)
    place(wi, win, ids, 0)
    place(wo, wout, ids, 0)
    bias = b_ref[...]
    wi_v = wi[...]
    wo_v = wo[...]
    db = jnp.zeros((1, MT), F32)
    for t in range(T // MB):
        rows = slice(t * MB, (t + 1) * MB)
        pre = mm(n_ref[rows, :], wi_v) + bias
        dh = mm(d_ref[rows, :], wo_v)
        sq = pre * pre
        th = jnp.tanh(GC * pre * (1.0 + GA * sq))
        half = 0.5 * (1.0 + th)
        h = (pre * half).astype(BF)
        slope = half + 0.5 * pre * (1.0 - th * th) * (GC + (3.0 * GA * GC) * sq)
        dp = (dh * slope).astype(BF)
        h_s[rows, :] = h
        p_s[rows, :] = dp
        db = db + jnp.sum(dp.astype(F32), 0, keepdims=True)
        ov = mm(h, wo_v, NT)
        gv = mm(wi_v, dp, NT)

        if first:

            @pl.when(j == 0)
            def _():
                o_ref[rows, :] = ov
                g_ref[:, rows] = gv

        else:

            @pl.when(j == 0)
            def _():
                o_ref[rows, :] = oin[rows, :].astype(F32) + ov
                g_ref[:, rows] = gin[:, rows].astype(F32) + gv

        @pl.when(j > 0)
        def _():
            o_ref[rows, :] += ov
            g_ref[:, rows] += gv

    @pl.when(j == pl.num_programs(0) - 1)
    def _():
        o_out[...] = o_ref[...].astype(BF)
        g_out[...] = g_ref[...].astype(BF)

    db_ref[...] = db
    hv = h_s[...]
    pv = p_s[...]
    for e, (left, right) in enumerate(((nt_ref, pv), (dt_ref, hv))):
        spread(mm(left[...], right).astype(BF), e, gm, (g0, g1)[e], gf)


def mlp(ids, n, nt, dy, dyt, bias, weights, pieces, offset, size, acc):
    first = acc is None
    nt_cols = size // MT
    tall = lambda cols: pl.BlockSpec((T, cols), lambda j, *_: (0, 0))
    own_rows = weights.shape[0]
    in_base = (4 * D + offset) // MT
    out_base = (4 * D + FF + offset) // MT
    wspecs = []
    for base_own, base in ((in_base, offset // MT), (out_base, (FF + offset) // MT)):
        if own_rows:
            wspecs.append(pl.BlockSpec((own_rows, MT), lambda j, *_, b=base_own: (0, b + j)))
        for p in pieces:
            wspecs.append(pl.BlockSpec((p.shape[0], MT), lambda j, *_, b=base: (0, b + j)))
    wargs = [weights, *pieces]
    bb = offset // MT
    flat = pl.BlockSpec((D // 4, MT), lambda j, *_: (0, j))
    deep = lambda r: pl.BlockSpec((2, r, MT), lambda j, *_: (0, 0, j))
    gspecs = [deep(D // 2), flat, flat, deep(D // 4)]
    return pl.pallas_call(
        functools.partial(mlp_kernel, len(wargs), first),
        grid_spec=pltpu.PrefetchScalarGridSpec(
            num_scalar_prefetch=1,
            grid=(nt_cols,),
            in_specs=[
                once((T, D)),
                once((D, T)),
                once((T, D)),
                once((D, T)),
                pl.BlockSpec((1, MT), lambda j, *_: (0, bb + j)),
                *wspecs,
                *([] if first else [once((T, D)), once((D, T))]),
            ],
            out_specs=[
                *gspecs,
                pl.BlockSpec((1, MT), lambda j, *_: (0, j)),
                once((T, D)),
                once((D, T)),
            ],
            scratch_shapes=[
                pltpu.VMEM((D, MT), BF),
                pltpu.VMEM((D, MT), BF),
                pltpu.VMEM((T, MT), BF),
                pltpu.VMEM((T, MT), BF),
                pltpu.VMEM((T, D), F32),
                pltpu.VMEM((D, T), F32),
            ],
        ),
        out_shape=[
            *grad_shapes(size),
            jax.ShapeDtypeStruct((1, size), F32),
            jax.ShapeDtypeStruct((T, D), BF),
            jax.ShapeDtypeStruct((D, T), BF),
        ],
        compiler_params=params(),
        cost_estimate=cost(41 * size / 2048),
    )(ids, n, nt, dy, dyt, bias, *wargs, *wargs, *([] if first else acc))


def proj_kernel(np_, ids, n_ref, d_ref, cos_ref, sin_ref, *refs):
    wq = refs[:np_]
    wo = refs[np_ : 2 * np_]
    out_ref, dout_ref, w_s, wo_s = refs[2 * np_ :]
    j = pl.program_id(0)
    place(w_s, wq, ids, 0)
    r = mm(w_s[...], n_ref[...], TT)

    def rotated(scale):
        for h in range(PT // HEAD_DIM):
            b = h * HEAD_DIM
            u = r[b : b + 16, :]
            w = r[b + 16 : b + 32, :]
            cs = cos_ref[...]
            sn = sin_ref[...]
            turned = [u * cs - w * sn, w * cs + u * sn, r[b + 32 : b + 64, :]]
            out_ref[b : b + 64, :] = (jnp.concatenate(turned, 0) * scale).astype(BF)

    @pl.when(j < D // PT)
    def _():
        rotated(LOG2E * HEAD_DIM ** (-0.5))

    @pl.when((j >= D // PT) & (j < 2 * D // PT))
    def _():
        rotated(1.0)

    @pl.when(j >= 2 * D // PT)
    def _():
        out_ref[...] = r.astype(BF)

    @pl.when(j == 0)
    def _():
        place(wo_s, wo, ids, 0)
        dout_ref[...] = mm(wo_s[...], d_ref[...], NT).astype(BF)


def proj(ids, n, dy, cos, sin, weights, pieces):
    wargs = [weights, *pieces]
    return pl.pallas_call(
        functools.partial(proj_kernel, len(wargs)),
        grid_spec=pltpu.PrefetchScalarGridSpec(
            num_scalar_prefetch=1,
            grid=(3 * D // PT,),
            in_specs=[
                once((T, D)),
                once((T, D)),
                once((16, T)),
                once((16, T)),
                *[pl.BlockSpec((w.shape[0], PT), lambda j, *_: (0, j)) for w in wargs],
                *[
                    pl.BlockSpec((w.shape[0], D), lambda j, *_: (0, 3), pipeline_mode=pl.Buffered(1))
                    for w in wargs
                ],
            ],
            out_specs=[
                pl.BlockSpec((PT, T), lambda j, *_: (j, 0)),
                once((D, T)),
            ],
            scratch_shapes=[pltpu.VMEM((D, PT), BF), pltpu.VMEM((D, D), BF)],
        ),
        out_shape=[
            jax.ShapeDtypeStruct((3 * D, T), BF),
            jax.ShapeDtypeStruct((D, T), BF),
        ],
        compiler_params=params(),
        cost_estimate=cost(20),
    )(ids, n, dy, cos, sin, *wargs, *wargs)


QB = 512
HPS = 2


def attn_kernel(n_alias, len_ref, q_ref, k_ref, v_ref, do_ref, cos_ref, sin_ref, *refs):
    o_ref, dq_ref, dk_ref, dv_ref = refs[n_alias:]
    sub = lax.broadcasted_iota(jnp.int32, (HEAD_DIM, T), 0)
    lane = lax.broadcasted_iota(jnp.int32, (HEAD_DIM, T), 1)
    bias = jnp.where((sub == 0) & (lane >= len_ref[0]), -1e30, 0.0)
    ones = jnp.where(sub == 0, 1.0, 0.0).astype(BF)
    none = jnp.zeros((HEAD_DIM, T), F32)
    ki = lax.broadcasted_iota(jnp.int32, (QB, QB), 0)
    qi = lax.broadcasted_iota(jnp.int32, (QB, QB), 1)

    def unrot(val, cs, sn, out, base, cols):
        a = val[0:16, :]
        b = val[16:32, :]
        turned = [a * cs + b * sn, b * cs - a * sn, val[32:64, :]]
        out[base : base + 64, cols] = jnp.concatenate(turned, 0).astype(BF)

    for h in range(HPS):
        b = h * HEAD_DIM
        hs = slice(b, b + HEAD_DIM)
        q = q_ref[hs, :]
        k = k_ref[hs, :]
        v = v_ref[hs, :]
        qa = jnp.concatenate([q, ones], 0)
        ka = jnp.concatenate([k.astype(F32), bias], 0).T.astype(BF)
        vt = jnp.concatenate([v.astype(F32), none], 0).T.astype(BF)
        dk = [jnp.zeros((HEAD_DIM, QB), F32) for _ in range(T // QB)]
        dv = [jnp.zeros((HEAD_DIM, QB), F32) for _ in range(T // QB)]
        for i in range(T // QB):
            qs = slice(i * QB, (i + 1) * QB)
            kk = (i + 1) * QB
            st = mm(ka[:kk, :], qa[:, qs])
            diag = jnp.where(ki <= qi, st[kk - QB :, :], -1e30)
            st = diag if i == 0 else jnp.concatenate([st[: kk - QB, :], diag], 0)
            e = jnp.exp2(st - jnp.max(st, 0, keepdims=True))
            rl = 1.0 / jnp.sum(e, 0, keepdims=True)
            eb = e.astype(BF)
            ot = mm(v[:, :kk], eb) * rl
            o_ref[hs, qs] = ot.astype(BF)
            dn = (do_ref[hs, qs].astype(F32) * rl).astype(BF)
            delta = jnp.sum(dn.astype(F32) * ot, 0, keepdims=True)
            da = jnp.concatenate([dn, none[:, qs].astype(BF)], 0)
            ds = (e * (mm(vt[:kk, :], da) - delta)).astype(BF)
            dq = mm(k[:, :kk], ds) * (HEAD_DIM ** (-0.5))
            unrot(dq, cos_ref[:, qs], sin_ref[:, qs], dq_ref, b, qs)
            dvi = mm(dn, eb, NT)
            dki = mm(q[:, qs], ds, NT)
            for t in range(i + 1):
                ts = slice(t * QB, (t + 1) * QB)
                dv[t] = dv[t] + dvi[:, ts]
                dk[t] = dk[t] + dki[:, ts]
        for t in range(T // QB):
            ts = slice(t * QB, (t + 1) * QB)
            dv_ref[hs, ts] = dv[t].astype(BF)
            unrot(dk[t] * LN2, cos_ref[:, ts], sin_ref[:, ts], dk_ref, b, ts)


def attend(length, qkv, dot_, cos, sin, first, heads, before):
    rows = HPS * HEAD_DIM
    steps = HEADS // HPS
    at = first // HPS
    spec = lambda base: pl.BlockSpec((rows, T), lambda h, *_: (base + at + h, 0))
    shape = jax.ShapeDtypeStruct((D, T), BF)
    alias = [] if before is None else list(before)
    return pl.pallas_call(
        functools.partial(attn_kernel, len(alias)),
        grid_spec=pltpu.PrefetchScalarGridSpec(
            num_scalar_prefetch=1,
            grid=(heads // HPS,),
            in_specs=[
                spec(0),
                spec(steps),
                spec(2 * steps),
                spec(0),
                once((16, T)),
                once((16, T)),
            ]
            + [pl.BlockSpec(memory_space=pl.ANY)] * len(alias),
            out_specs=[spec(0)] * 4,
        ),
        out_shape=[shape] * 4,
        input_output_aliases={7 + i: i for i in range(len(alias))},
        compiler_params=params(),
        cost_estimate=cost(46 * heads / HEADS),
    )(length, qkv, qkv, qkv, dot_, cos, sin, *alias)


def agrad_kernel(hr, blocks, ids, nt_ref, dy_ref, o_ref, dq_ref, dk_ref, dv_ref, gm, g0, g1, gf, g_s):
    j = pl.program_id(0)
    for at, (src, near) in enumerate(((dq_ref, g0), (dk_ref, g0), (dv_ref, g1))):

        @pl.when((j >= 2 * at) & (j < 2 * at + 2))
        def _(src=src, near=near):
            spread(mm(nt_ref[...], src[...], NT).astype(BF), 0, gm, near, gf)

    @pl.when(j >= 6)
    def _():
        g_s[...] = mm(o_ref[...], dy_ref[...]).astype(BF)
        rows = [pl.multiple_of(ids[b], hr) for b in range(2 * blocks)]
        spread(jnp.concatenate([g_s[pl.ds(k, hr), :] for k in rows], 0), 0, gm, g1, gf)


def attn_grads(ids, nt, dy, ot, dq, dk, dv, hr, blocks):
    def grab(at):
        return pl.BlockSpec((TILE, T), lambda j, *_: (jnp.clip(j - 2 * at, 0, 1), 0))

    deep = lambda r: pl.BlockSpec((1, r, TILE), lambda j, *_: (j // 4, 0, j % 4))
    gspecs = [
        deep(D // 2),
        pl.BlockSpec((D // 4, TILE), lambda j, *_: (0, jnp.minimum(j, 3))),
        pl.BlockSpec((D // 4, TILE), lambda j, *_: (0, jnp.maximum(j - 4, 0))),
        deep(D // 4),
    ]
    return pl.pallas_call(
        functools.partial(agrad_kernel, hr, blocks),
        grid_spec=pltpu.PrefetchScalarGridSpec(
            num_scalar_prefetch=1,
            grid=(4 * D // TILE,),
            in_specs=[
                once((D, T)),
                pl.BlockSpec((T, TILE), lambda j, *_: (0, jnp.clip(j - 6, 0, 1))),
                once((D, T)),
                grab(0),
                grab(1),
                grab(2),
            ],
            out_specs=gspecs,
            scratch_shapes=[pltpu.VMEM((D, TILE), BF)],
        ),
        out_shape=grad_shapes(2 * D),
        compiler_params=params(),
        cost_estimate=cost(17),
    )(ids, nt, dy, ot, dq, dk, dv)


def final_kernel(np_, ids, x_ref, dy_ref, g_ref, bo_ref, o_ref, dq_ref, dk_ref, dv_ref, ao_ref, ag_ref, *refs):
    wq = refs[:np_]
    out_ref, gin_ref, v_ref, w_s = refs[np_:]
    i = pl.program_id(0)

    @pl.when(i == 0)
    def _():
        place(w_s, wq, ids, 1)

    x = x_ref[...].astype(F32)
    row = i * FT + lax.broadcasted_iota(jnp.int32, (FT, 1), 0)
    attn = mm(o_ref[...], w_s[:, 3 * D :], TN)
    out = x + attn + ao_ref[...].astype(F32) + bo_ref[...]
    out_ref[...] = jnp.where(row < ids[0], out, 0.0).astype(BF)
    dn = (
        ag_ref[...].astype(F32)
        + mm(w_s[:, :D], dq_ref[...])
        + mm(w_s[:, D : 2 * D], dk_ref[...])
        + mm(w_s[:, 2 * D : 3 * D], dv_ref[...])
    ).T
    mean = jnp.mean(x, -1, keepdims=True)
    xc = x - mean
    inv = lax.rsqrt(jnp.mean(xc * xc, -1, keepdims=True) + NORM_EPS)
    xh = xc * inv
    g = dn * g_ref[...]
    gx = dn * xh
    ln = inv * (
        g - jnp.mean(g, -1, keepdims=True) - xh * jnp.mean(g * xh, -1, keepdims=True)
    )
    gin_ref[...] = (dy_ref[...].astype(F32) + ln).astype(BF)

    @pl.when(i == 0)
    def _():
        v_ref[...] = jnp.zeros_like(v_ref)

    v_ref[0:1, :] += jnp.sum(gx, 0, keepdims=True)
    v_ref[1:2, :] += jnp.sum(dn, 0, keepdims=True)


def final(ids, x, dy, gain, b_out, ot, dq, dk, dv, acc_o, acc_g, weights, pieces):
    row = pl.BlockSpec((FT, D), lambda i, *_: (i, 0))
    col = pl.BlockSpec((D, FT), lambda i, *_: (0, i))
    vec = pl.BlockSpec((1, D), lambda i, *_: (0, 0))
    wargs = [weights, *pieces]
    return pl.pallas_call(
        functools.partial(final_kernel, len(wargs)),
        grid_spec=pltpu.PrefetchScalarGridSpec(
            num_scalar_prefetch=1,
            grid=(T // FT,),
            in_specs=[
                row,
                row,
                vec,
                vec,
                col,
                col,
                col,
                col,
                row,
                col,
                *[once((w.shape[0], 4 * D)) for w in wargs],
            ],
            out_specs=[row, row, pl.BlockSpec((8, D), lambda i, *_: (0, 0))],
            scratch_shapes=[pltpu.VMEM((D, 4 * D), BF)],
        ),
        out_shape=[
            jax.ShapeDtypeStruct((T, D), BF),
            jax.ShapeDtypeStruct((T, D), BF),
            jax.ShapeDtypeStruct((8, D), F32),
        ],
        compiler_params=params(),
        cost_estimate=cost(20),
    )(ids, x, dy, gain, b_out, ot, dq, dk, dv, acc_o, acc_g, *wargs)


C1 = float(1.0 - np.float32(B1) ** np.float32(STEP))
C2 = float(1.0 - np.float32(B2) ** np.float32(STEP))


def adam_math(g, m, v, w, decay):
    nm = B1 * m + (1.0 - B1) * g
    nv = B2 * v + (1.0 - B2) * g * g
    up = -LR * (nm / C1 / (jnp.sqrt(nv / C2) + ADAM_EPS) + decay * w)
    return nm, nv, up


def adam_kernel(n_alias, first, ids, sm, rm, so, ro, m_ref, v_ref, w_ref, *refs):
    wg_ref, nm_ref, nv_ref, up_ref, end_ref = refs[n_alias:]
    end_ref[...] = jnp.zeros_like(end_ref)
    summed = pl.program_id(0) + first == ids[1]
    hr = sm.shape[0]
    mine = jnp.where(summed, sm[...].astype(F32), rm[...].astype(F32))
    other = jnp.where(summed, so[...].astype(F32), ro[...].astype(F32))
    lead = ids[0] == 0
    for h, g in enumerate((jnp.where(lead, mine, other), jnp.where(lead, other, mine))):
        rows = slice(h * hr, (h + 1) * hr)
        nm, nv, up = adam_math(g, m_ref[rows, :], v_ref[rows, :], w_ref[rows, :].astype(F32), DECAY)
        wg_ref[rows, :] = g
        nm_ref[rows, :] = nm
        nv_ref[rows, :] = nv
        up_ref[rows, :] = up


def adam(ids, grads, cols, m, v, w, outs, first=0, count=2):
    rows, width = m.shape
    hr = rows // 2
    n = grads[0].shape[1]
    AC = 1024 if n % 1024 == 0 else 512
    pick = lambda hit: pl.BlockSpec(
        (hr, AC), lambda p, j, ids: (0, jnp.where((p + first == ids[1]) == hit, j, 0))
    )
    b0, b1 = cols[0] // AC, cols[1] // AC
    big = pl.BlockSpec((rows, AC), lambda p, j, ids: (0, jnp.where(p + first == 0, b0, b1) + j))
    alias = [] if outs is None else list(outs)
    return pl.pallas_call(
        functools.partial(adam_kernel, len(alias), first),
        grid_spec=pltpu.PrefetchScalarGridSpec(
            num_scalar_prefetch=1,
            grid=(count, n // AC),
            in_specs=[pick(True), pick(False), pick(True), pick(False), big, big, big]
            + [pl.BlockSpec(memory_space=pl.ANY)] * len(alias),
            out_specs=[big] * 4 + [pl.BlockSpec((8, 128), lambda p, j, ids: (0, 0))],
        ),
        out_shape=[jax.ShapeDtypeStruct((rows, width), F32)] * 4
        + [jax.ShapeDtypeStruct((8, 128), F32)],
        input_output_aliases={8 + i: i for i in range(len(alias))},
        compiler_params=pltpu.CompilerParams(
            dimension_semantics=("arbitrary", "arbitrary"), vmem_limit_bytes=VLIM
        ),
        cost_estimate=cost(6 * count * n / 2048),
    )(ids, *grads, m, v, w, *alias)


def after(values, *waits):
    flat = lax.optimization_barrier((*values, *waits))
    return list(flat[: len(values)])


def on_device(shards, reps, hidden_in, cotangent, lengths, weights, moment_m, moment_v, vectors, vector_m, vector_v):
    s = lax.axis_index("shard")
    rep = lax.axis_index("rep")
    c = rep % 2
    z = rep // 2
    zs = reps // 2
    swap = [(i, i ^ 1) for i in range(reps)]
    rows = weights.shape[0]
    hr = rows // 2
    i32 = jnp.int32
    cube = shards == 4 and zs & (zs - 1) == 0 and zs >= 4
    xn = [(i, i ^ 1) for i in range(shards)]
    yn = [(i, i ^ 2) for i in range(shards)]
    zsteps = [3] + [1 << k for k in range(2, 16) if 1 << k < zs]
    zn = lambda bit: [(i, i ^ (2 * bit)) for i in range(reps)]
    own = ((z ^ (z // 2)) % 2) if cube else jnp.int32(0)

    if cube:
        y_rows = [(s ^ r) * rows for r in (2, 3, 0, 1)]
    else:
        y_rows = [r * rows for r in range(shards)]
    cut = lambda at: [b + c * hr for b in at] + [b + (1 - c) * hr for b in at]
    y_off = cut(y_rows)
    stack = lambda *v: jnp.stack([jnp.asarray(x, i32) for x in v])
    length = lengths.astype(i32)
    gain = vectors[:D].reshape(1, D)
    shift = vectors[D : 2 * D].reshape(1, D)
    b_out = vectors[2 * D : 3 * D].reshape(1, D)
    b_in = vectors[3 * D :].reshape(1, FF)
    half_w = lax.dynamic_slice_in_dim(weights, c * hr, hr, 0)

    n, nt, dy, dyt, db_out = prep(
        stack(length[0], *y_off), hidden_in, cotangent, gain, shift, hr, shards
    )

    def part_of(cols):
        return jnp.concatenate([half_w[:, a:b] for a, b in cols], 1)

    q = hr // 2

    def gather_first(part):
        a, b = part[:q], part[q:]
        return [
            lax.ppermute(p, "shard", way) for p, way in ((a, xn), (b, yn), (b, xn), (a, yn))
        ]

    def gather_second(first):
        return [lax.ppermute(first[0], "shard", yn), lax.ppermute(first[1], "shard", xn)]

    def swapped(mine):
        return mine + [lax.ppermute(p, "rep", swap) for p in mine]

    def gather_whole(part):
        full = lax.all_gather(part, "shard", axis=0, tiled=True)
        other = lax.ppermute(full, "rep", swap)
        return [p[b * hr : (b + 1) * hr] for p in (full, other) for b in range(shards)]

    offsets = [0]
    for size in SIZES:
        offsets.append(offsets[-1] + size)
    apart, fpart = part_of([(0, 4 * D)]), part_of([(4 * D, 4 * D + 2 * FF)])
    if cube:
        base = [(s ^ r) * rows + e * q for r, e in ((1, 0), (2, 1), (1, 1), (2, 0), (3, 0), (3, 1))]
        offs = [b + c * hr for b in base] + [b + (1 - c) * hr for b in base]
        one = gather_first(apart)
        one[:2] = after(one[:2], n)
        one = one + gather_second(one)
        (fpart,) = after([fpart], *one)
        apieces = swapped(one)
        two = gather_first(fpart)
    else:
        offs = cut([b * rows for b in range(shards)])
        apieces = gather_whole(apart)
        two = gather_whole(fpart)
    piece_off = stack(s * rows, *offs)
    len_piece_off = stack(length[0], s * rows, *offs)

    add = lambda *v: sum(x.astype(F32) for x in v).astype(BF)

    class Reduce:
        def __init__(self, grads, split=False):
            self.split = split
            self.mine = grads[0]
            self.got = [lax.ppermute(g, "rep", swap) for g in grads[1:]]
            self.at = 0
            self.sums = None
            self.brought = []

        def settle(self, last):
            if self.brought:
                self.brought = after(self.brought, last)

        def step(self):
            self.at += 1
            k = self.at
            m, far, old = self.mine, self.got[2], self.brought
            if not cube:
                groups = [[2 * j + e for j in range(zs)] for e in range(2)]
                both = add(m, jnp.concatenate([jnp.stack(self.got[:2]), far], 1))
                both = lax.psum_scatter(both, "shard", scatter_dimension=1, tiled=True)
                both = lax.psum(both, "rep", axis_index_groups=groups)
                self.sums = (both[0], both[1])
                return [], []
            if self.split and k <= 3:
                return self.step_split(k)
            if k == 1:
                sent = add(m[:, : 2 * hr], jnp.stack(self.got[:2]))
                way = ("shard", yn)
            elif k == 2:
                self.first = old[0]
                sent = add(m[:, 3 * hr :], far[:, hr:], old[0][:, hr:])
                way = ("shard", xn)
            elif k == 3:
                total = add(m[:, 2 * hr : 3 * hr], far[:, :hr], self.first[:, :hr], old[0])
                lead = own == 0
                sent = jnp.where(lead, total[1], total[0])
                self.keep = jnp.where(lead, total[0], total[1])
                way = ("rep", zn(1))
            else:
                sent = self.keep = add(self.keep, old[0])
                last = k == 4 + len(zsteps)
                way = ("rep", zn(1 if last else zsteps[k - 4]))
            self.brought = [lax.ppermute(sent, *way)]
            if k == 4 + len(zsteps):
                self.sums = (self.keep, self.brought[0])
            return [sent], self.brought

        def step_split(self, k):
            m, old = self.mine, self.brought
            near, far = self.got[:2], self.got[2]
            b = [slice(i * hr, (i + 1) * hr) for i in range(4)]
            if k == 1:
                low = [add(m[0, b[3]], far[0, b[1]]), add(m[0, b[1]], near[0][b[1]])]
                sent = [jnp.concatenate(low, 0), add(m[1, : 2 * hr], near[1])]
                ways = xn, yn
            elif k == 2:
                self.first = old
                sent = [
                    add(m[0, b[0]], near[0][b[0]], old[0][b[1]]),
                    add(m[1, b[3]], far[1, b[1]], old[1][b[1]]),
                ]
                ways = yn, xn
            else:
                total = [
                    add(m[e, b[2]], far[e, b[0]], self.first[e][b[0]], old[e]) for e in range(2)
                ]
                lead = own == 0
                sent = [jnp.where(lead, total[1], total[0])]
                self.keep = jnp.where(lead, total[0], total[1])
                self.brought = [lax.ppermute(sent[0], "rep", zn(1))]
                return sent, self.brought
            self.brought = [lax.ppermute(v, "shard", w) for v, w in zip(sent, ways)]
            return sent, self.brought

        def result(self, *waits):
            while self.sums is None:
                self.step()
            sums = after(list(self.sums), *waits)
            return [*sums, *[lax.ppermute(v, "rep", swap) for v in sums]]

    flight = []

    def turn(values, last, *steps):
        nonlocal flight
        waits = flight
        flight = []
        for red in steps:
            if red.sums is None:
                red.settle(last)
                moved = red.step()
                waits = waits + moved[0]
                flight = flight + moved[1]
        return after(values, *waits) if waits else list(values)

    inv_freq = jnp.power(F32(10000.0), -jnp.arange(0, ROT, 2, dtype=F32) / ROT)
    angles = inv_freq[:, None] * jnp.arange(T, dtype=F32)[None, :]
    cos, sin = jnp.cos(angles), jnp.sin(angles)
    qkv, dot_ = proj(piece_off, n, dy, cos, sin, weights, apieces)
    half = HEADS // 2
    heads = attend(length, qkv, dot_, cos, sin, 0, half, None)
    if cube:
        *two, qkv = after([*two, qkv], heads[0])
        three = gather_second(two)
        across = [lax.ppermute(v, "rep", swap) for v in two[:2]]
    ot, dq, dk, dv = attend(length, qkv, dot_, cos, sin, half, half, heads)
    dyg = dy
    if cube:
        (dyg,) = after([dy], ot, *three, *across)
        rest = after(two[2:] + three, ot)
        across += [lax.ppermute(v, "rep", swap) for v in rest]
        fpieces = two + three + across
    else:
        fpieces = two
    grads = attn_grads(stack(*y_off), nt, dyg, ot, dq, dk, dv, hr, shards)
    if cube:
        grads = after(grads, *across[2:])
    reds = [Reduce(grads, True)]
    places = [(0, 2 * D)]
    acc = None
    dbs = []
    nk = n
    for at, size in zip(offsets, SIZES):
        (nk,) = turn([nk], dbs[-1] if dbs else dv, *reds)
        *grads, db_in, acc_o, acc_g = mlp(
            piece_off, nk, nt, dy, dyt, b_in, weights, fpieces, at, size, acc
        )
        acc = (acc_o, acc_g)
        dbs.append(db_in)
        reds.append(Reduce(grads))
        places.append((4 * D + at, 4 * D + FF + at))

    (ot,) = turn([ot], dbs[-1], *reds)
    (ot,) = after([ot], reds[-1].got[2])
    out, grad_in, vsum = final(
        len_piece_off, hidden_in, dy, gain, b_out, ot, dq, dk, dv, *acc, weights, apieces
    )
    core = stack(c, own)
    def push(last, steps, loose):
        waits = []
        for red in steps + loose:
            if red.sums is None:
                red.settle(last)
                sent = red.step()[0]
                waits = waits + (sent if red in steps else [])
        return after([core], *waits)[0] if waits else core

    args = moment_m, moment_v, weights
    vec = jnp.concatenate([vsum[0], vsum[1], db_out[0], *[d[0] for d in dbs]])
    if cube:
        vec = vec.reshape(-1, 128)
        hops = [("rep", swap), ("shard", xn), ("shard", yn)]
        hops += [("rep", zn(bit)) for bit in [1] + zsteps]
    else:
        vec = lax.psum(vec, ("rep", "shard"))
        hops = []

    def hop(last, count=1):
        nonlocal vec
        for _ in range(count):
            if hops:
                (vec,) = after([vec], last)
                vec = vec + lax.ppermute(vec, *hops.pop(0))

    big, end = None, vsum
    for i, (red, place_) in enumerate(zip(reds, places)):
        hop(end)
        near = i + 2 if i else 3
        ids = push(end, reds[i:near], reds[near:])
        *big, end = adam(ids, red.result(*([] if i else [vsum])), place_, *args, big)
    while hops:
        hop(end)
    vec = vec.reshape(-1)
    vm, vv, vu = adam_math(vec, vector_m, vector_v, vectors, 0.0)
    return (out, grad_in, *big, vec, vm, vv, vu)


def solution(mesh):
    tok = P(("rep", "shard"), None)
    w = P("shard", None)
    return jax.shard_map(
        functools.partial(on_device, mesh.shape["shard"], mesh.shape["rep"]),
        mesh=mesh,
        in_specs=(tok, tok, P(("rep", "shard")), w, w, w, P(), P(), P()),
        out_specs=(tok, tok, w, w, w, w, P(), P(), P(), P()),
        check_vma=False,
    )
```

```python
import functools

import jax
import jax.numpy as jnp
import numpy as np
from jax import lax
from jax.experimental import pallas as pl
from jax.experimental.pallas import tpu as pltpu
from jax.sharding import PartitionSpec as P

D = 1024
HEADS = 16
HEAD_DIM = 64
ROT = 32
FF = 4096
T = 1024
STEP = 10

B1 = 0.9
B2 = 0.95
LR = 0.02
DECAY = 0.1
ADAM_EPS = 1e-08
NORM_EPS = 1e-05
GC = 0.7978845608028654
GA = 0.044715
LOG2E = 1.4426950408889634
LN2 = 0.6931471805599453

BF = jnp.bfloat16
F32 = jnp.float32
VLIM = 58 * 1024 * 1024
NN = (((1,), (0,)), ((), ()))
NT = (((1,), (1,)), ((), ()))
TN = (((0,), (0,)), ((), ()))
TT = (((0,), (1,)), ((), ()))
TILE = 512
SIZES = (1024, 1024, 1024, 1024)
MB = 1024
MT = 1024
TB = 256
PT = 512
FT = 256


def mm(a, b, dims=NN):
    return lax.dot_general(a, b, dims, preferred_element_type=F32)


def params():
    return pltpu.CompilerParams(
        dimension_semantics=("arbitrary",), vmem_limit_bytes=VLIM
    )


def once(shape):
    return pl.BlockSpec(shape, lambda *_: (0,) * len(shape), pipeline_mode=pl.Buffered(1))


def cost(us):
    return pl.CostEstimate(flops=int(us * 1.15e9), bytes_accessed=1024, transcendentals=0)


def prep_kernel(hr, blocks, ids, x_ref, c_ref, g_ref, b_ref, n_ref, nt_ref, d_ref, dt_ref, db_ref, s_ref):
    i = pl.program_id(0)
    x = x_ref[...].astype(F32)
    mean = jnp.mean(x, -1, keepdims=True)
    xc = x - mean
    var = jnp.mean(xc * xc, -1, keepdims=True)
    n = xc * lax.rsqrt(var + NORM_EPS) * g_ref[...] + b_ref[...]
    n_ref[...] = n.astype(BF)
    row = i * TB + lax.broadcasted_iota(jnp.int32, (TB, 1), 0)
    dy = jnp.where(row < ids[0], c_ref[...].astype(F32), 0.0)
    d_ref[...] = dy.astype(BF)

    @pl.when(i == 0)
    def _():
        db_ref[...] = jnp.zeros_like(db_ref)

    db_ref[...] += jnp.sum(dy, 0, keepdims=True)
    for val, out in ((n, nt_ref), (dy, dt_ref)):
        s_ref[...] = val.T.astype(BF)
        for b in range(2 * blocks):
            off = pl.multiple_of(ids[1 + b], hr)
            out[b * hr : (b + 1) * hr, :] = s_ref[pl.ds(off, hr), :]


def prep(ids, x, cot, gain, shift, hr, blocks):
    row = lambda i, *_: (i, 0)
    col = lambda i, *_: (0, i)
    fix = lambda i, *_: (0, 0)
    return pl.pallas_call(
        functools.partial(prep_kernel, hr, blocks),
        grid_spec=pltpu.PrefetchScalarGridSpec(
            num_scalar_prefetch=1,
            grid=(T // TB,),
            in_specs=[
                pl.BlockSpec((TB, D), row),
                pl.BlockSpec((TB, D), row),
                pl.BlockSpec((1, D), fix),
                pl.BlockSpec((1, D), fix),
            ],
            out_specs=[
                pl.BlockSpec((TB, D), row),
                pl.BlockSpec((D, TB), col),
                pl.BlockSpec((TB, D), row),
                pl.BlockSpec((D, TB), col),
                pl.BlockSpec((1, D), fix),
            ],
            scratch_shapes=[pltpu.VMEM((D, TB), BF)],
        ),
        out_shape=[
            jax.ShapeDtypeStruct((T, D), BF),
            jax.ShapeDtypeStruct((D, T), BF),
            jax.ShapeDtypeStruct((T, D), BF),
            jax.ShapeDtypeStruct((D, T), BF),
            jax.ShapeDtypeStruct((1, D), F32),
        ],
        compiler_params=params(),
        cost_estimate=cost(8),
    )(ids, x, cot, gain, shift)


def place(dst, srcs, ids, base):
    for k, src in enumerate(srcs):
        rows = src.shape[0]
        dst[pl.ds(pl.multiple_of(ids[base + k], rows), rows), :] = src[...]


def spread(g, e, mine, near, far):
    a, b = D // 2, 3 * D // 4
    mine[e] = g[:a, :]
    near[...] = g[a:b, :]
    far[e] = g[b:, :]


def grad_shapes(n):
    return [
        jax.ShapeDtypeStruct(v, BF)
        for v in ((2, D // 2, n), (D // 4, n), (D // 4, n), (2, D // 4, n))
    ]


def mlp_kernel(np_, first, ids, n_ref, nt_ref, d_ref, dt_ref, b_ref, *refs):
    win = refs[:np_]
    wout = refs[np_ : 2 * np_]
    refs = refs[2 * np_ :]
    if not first:
        oin, gin = refs[:2]
        refs = refs[2:]
    gm, g0, g1, gf = refs[:4]
    db_ref, o_out, g_out, wi, wo, h_s, p_s, o_ref, g_ref = refs[4:]
    j = pl.program_id(0)
    place(wi, win, ids, 0)
    place(wo, wout, ids, 0)
    bias = b_ref[...]
    wi_v = wi[...]
    wo_v = wo[...]
    db = jnp.zeros((1, MT), F32)
    for t in range(T // MB):
        rows = slice(t * MB, (t + 1) * MB)
        pre = mm(n_ref[rows, :], wi_v) + bias
        dh = mm(d_ref[rows, :], wo_v)
        sq = pre * pre
        th = jnp.tanh(GC * pre * (1.0 + GA * sq))
        half = 0.5 * (1.0 + th)
        h = (pre * half).astype(BF)
        slope = half + 0.5 * pre * (1.0 - th * th) * (GC + (3.0 * GA * GC) * sq)
        dp = (dh * slope).astype(BF)
        h_s[rows, :] = h
        p_s[rows, :] = dp
        db = db + jnp.sum(dp.astype(F32), 0, keepdims=True)
        ov = mm(h, wo_v, NT)
        gv = mm(wi_v, dp, NT)

        if first:

            @pl.when(j == 0)
            def _():
                o_ref[rows, :] = ov
                g_ref[:, rows] = gv

        else:

            @pl.when(j == 0)
            def _():
                o_ref[rows, :] = oin[rows, :].astype(F32) + ov
                g_ref[:, rows] = gin[:, rows].astype(F32) + gv

        @pl.when(j > 0)
        def _():
            o_ref[rows, :] += ov
            g_ref[:, rows] += gv

    @pl.when(j == pl.num_programs(0) - 1)
    def _():
        o_out[...] = o_ref[...].astype(BF)
        g_out[...] = g_ref[...].astype(BF)

    db_ref[...] = db
    hv = h_s[...]
    pv = p_s[...]
    for e, (left, right) in enumerate(((nt_ref, pv), (dt_ref, hv))):
        spread(mm(left[...], right).astype(BF), e, gm, (g0, g1)[e], gf)


def mlp(ids, n, nt, dy, dyt, bias, weights, pieces, offset, size, acc):
    first = acc is None
    nt_cols = size // MT
    tall = lambda cols: pl.BlockSpec((T, cols), lambda j, *_: (0, 0))
    own_rows = weights.shape[0]
    in_base = (4 * D + offset) // MT
    out_base = (4 * D + FF + offset) // MT
    wspecs = []
    for base_own, base in ((in_base, offset // MT), (out_base, (FF + offset) // MT)):
        if own_rows:
            wspecs.append(pl.BlockSpec((own_rows, MT), lambda j, *_, b=base_own: (0, b + j)))
        for p in pieces:
            wspecs.append(pl.BlockSpec((p.shape[0], MT), lambda j, *_, b=base: (0, b + j)))
    wargs = [weights, *pieces]
    bb = offset // MT
    flat = pl.BlockSpec((D // 4, MT), lambda j, *_: (0, j))
    deep = lambda r: pl.BlockSpec((2, r, MT), lambda j, *_: (0, 0, j))
    gspecs = [deep(D // 2), flat, flat, deep(D // 4)]
    return pl.pallas_call(
        functools.partial(mlp_kernel, len(wargs), first),
        grid_spec=pltpu.PrefetchScalarGridSpec(
            num_scalar_prefetch=1,
            grid=(nt_cols,),
            in_specs=[
                once((T, D)),
                once((D, T)),
                once((T, D)),
                once((D, T)),
                pl.BlockSpec((1, MT), lambda j, *_: (0, bb + j)),
                *wspecs,
                *([] if first else [once((T, D)), once((D, T))]),
            ],
            out_specs=[
                *gspecs,
                pl.BlockSpec((1, MT), lambda j, *_: (0, j)),
                once((T, D)),
                once((D, T)),
            ],
            scratch_shapes=[
                pltpu.VMEM((D, MT), BF),
                pltpu.VMEM((D, MT), BF),
                pltpu.VMEM((T, MT), BF),
                pltpu.VMEM((T, MT), BF),
                pltpu.VMEM((T, D), F32),
                pltpu.VMEM((D, T), F32),
            ],
        ),
        out_shape=[
            *grad_shapes(size),
            jax.ShapeDtypeStruct((1, size), F32),
            jax.ShapeDtypeStruct((T, D), BF),
            jax.ShapeDtypeStruct((D, T), BF),
        ],
        compiler_params=params(),
        cost_estimate=cost(41 * size / 2048),
    )(ids, n, nt, dy, dyt, bias, *wargs, *wargs, *([] if first else acc))


def proj_kernel(np_, ids, n_ref, d_ref, cos_ref, sin_ref, *refs):
    wq = refs[:np_]
    wo = refs[np_ : 2 * np_]
    out_ref, dout_ref, w_s, wo_s = refs[2 * np_ :]
    j = pl.program_id(0)
    place(w_s, wq, ids, 0)
    r = mm(w_s[...], n_ref[...], TT)

    def rotated(scale):
        for h in range(PT // HEAD_DIM):
            b = h * HEAD_DIM
            u = r[b : b + 16, :]
            w = r[b + 16 : b + 32, :]
            cs = cos_ref[...]
            sn = sin_ref[...]
            turned = [u * cs - w * sn, w * cs + u * sn, r[b + 32 : b + 64, :]]
            out_ref[b : b + 64, :] = (jnp.concatenate(turned, 0) * scale).astype(BF)

    @pl.when(j < D // PT)
    def _():
        rotated(LOG2E * HEAD_DIM ** (-0.5))

    @pl.when((j >= D // PT) & (j < 2 * D // PT))
    def _():
        rotated(1.0)

    @pl.when(j >= 2 * D // PT)
    def _():
        out_ref[...] = r.astype(BF)

    @pl.when(j == 0)
    def _():
        place(wo_s, wo, ids, 0)
        dout_ref[...] = mm(wo_s[...], d_ref[...], NT).astype(BF)


def proj(ids, n, dy, cos, sin, weights, pieces):
    wargs = [weights, *pieces]
    return pl.pallas_call(
        functools.partial(proj_kernel, len(wargs)),
        grid_spec=pltpu.PrefetchScalarGridSpec(
            num_scalar_prefetch=1,
            grid=(3 * D // PT,),
            in_specs=[
                once((T, D)),
                once((T, D)),
                once((16, T)),
                once((16, T)),
                *[pl.BlockSpec((w.shape[0], PT), lambda j, *_: (0, j)) for w in wargs],
                *[
                    pl.BlockSpec((w.shape[0], D), lambda j, *_: (0, 3), pipeline_mode=pl.Buffered(1))
                    for w in wargs
                ],
            ],
            out_specs=[
                pl.BlockSpec((PT, T), lambda j, *_: (j, 0)),
                once((D, T)),
            ],
            scratch_shapes=[pltpu.VMEM((D, PT), BF), pltpu.VMEM((D, D), BF)],
        ),
        out_shape=[
            jax.ShapeDtypeStruct((3 * D, T), BF),
            jax.ShapeDtypeStruct((D, T), BF),
        ],
        compiler_params=params(),
        cost_estimate=cost(20),
    )(ids, n, dy, cos, sin, *wargs, *wargs)


QB = 512
HPS = 2


def attn_kernel(n_alias, len_ref, q_ref, k_ref, v_ref, do_ref, cos_ref, sin_ref, *refs):
    o_ref, dq_ref, dk_ref, dv_ref = refs[n_alias:]
    sub = lax.broadcasted_iota(jnp.int32, (HEAD_DIM, T), 0)
    lane = lax.broadcasted_iota(jnp.int32, (HEAD_DIM, T), 1)
    bias = jnp.where((sub == 0) & (lane >= len_ref[0]), -1e30, 0.0)
    ones = jnp.where(sub == 0, 1.0, 0.0).astype(BF)
    none = jnp.zeros((HEAD_DIM, T), F32)
    ki = lax.broadcasted_iota(jnp.int32, (QB, QB), 0)
    qi = lax.broadcasted_iota(jnp.int32, (QB, QB), 1)

    def unrot(val, cs, sn, out, base, cols):
        a = val[0:16, :]
        b = val[16:32, :]
        turned = [a * cs + b * sn, b * cs - a * sn, val[32:64, :]]
        out[base : base + 64, cols] = jnp.concatenate(turned, 0).astype(BF)

    for h in range(HPS):
        b = h * HEAD_DIM
        hs = slice(b, b + HEAD_DIM)
        q = q_ref[hs, :]
        k = k_ref[hs, :]
        v = v_ref[hs, :]
        qa = jnp.concatenate([q, ones], 0)
        ka = jnp.concatenate([k.astype(F32), bias], 0).T.astype(BF)
        vt = jnp.concatenate([v.astype(F32), none], 0).T.astype(BF)
        dk = [jnp.zeros((HEAD_DIM, QB), F32) for _ in range(T // QB)]
        dv = [jnp.zeros((HEAD_DIM, QB), F32) for _ in range(T // QB)]
        for i in range(T // QB):
            qs = slice(i * QB, (i + 1) * QB)
            kk = (i + 1) * QB
            st = mm(ka[:kk, :], qa[:, qs])
            diag = jnp.where(ki <= qi, st[kk - QB :, :], -1e30)
            st = diag if i == 0 else jnp.concatenate([st[: kk - QB, :], diag], 0)
            e = jnp.exp2(st - jnp.max(st, 0, keepdims=True))
            rl = 1.0 / jnp.sum(e, 0, keepdims=True)
            eb = e.astype(BF)
            ot = mm(v[:, :kk], eb) * rl
            o_ref[hs, qs] = ot.astype(BF)
            dn = (do_ref[hs, qs].astype(F32) * rl).astype(BF)
            delta = jnp.sum(dn.astype(F32) * ot, 0, keepdims=True)
            da = jnp.concatenate([dn, none[:, qs].astype(BF)], 0)
            ds = (e * (mm(vt[:kk, :], da) - delta)).astype(BF)
            dq = mm(k[:, :kk], ds) * (HEAD_DIM ** (-0.5))
            unrot(dq, cos_ref[:, qs], sin_ref[:, qs], dq_ref, b, qs)
            dvi = mm(dn, eb, NT)
            dki = mm(q[:, qs], ds, NT)
            for t in range(i + 1):
                ts = slice(t * QB, (t + 1) * QB)
                dv[t] = dv[t] + dvi[:, ts]
                dk[t] = dk[t] + dki[:, ts]
        for t in range(T // QB):
            ts = slice(t * QB, (t + 1) * QB)
            dv_ref[hs, ts] = dv[t].astype(BF)
            unrot(dk[t] * LN2, cos_ref[:, ts], sin_ref[:, ts], dk_ref, b, ts)


def attend(length, qkv, dot_, cos, sin, first, heads, before):
    rows = HPS * HEAD_DIM
    steps = HEADS // HPS
    at = first // HPS
    spec = lambda base: pl.BlockSpec((rows, T), lambda h, *_: (base + at + h, 0))
    shape = jax.ShapeDtypeStruct((D, T), BF)
    alias = [] if before is None else list(before)
    return pl.pallas_call(
        functools.partial(attn_kernel, len(alias)),
        grid_spec=pltpu.PrefetchScalarGridSpec(
            num_scalar_prefetch=1,
            grid=(heads // HPS,),
            in_specs=[
                spec(0),
                spec(steps),
                spec(2 * steps),
                spec(0),
                once((16, T)),
                once((16, T)),
            ]
            + [pl.BlockSpec(memory_space=pl.ANY)] * len(alias),
            out_specs=[spec(0)] * 4,
        ),
        out_shape=[shape] * 4,
        input_output_aliases={7 + i: i for i in range(len(alias))},
        compiler_params=params(),
        cost_estimate=cost(46 * heads / HEADS),
    )(length, qkv, qkv, qkv, dot_, cos, sin, *alias)


def agrad_kernel(hr, blocks, ids, nt_ref, dy_ref, o_ref, dq_ref, dk_ref, dv_ref, gm, g0, g1, gf, g_s):
    j = pl.program_id(0)
    for at, (src, near) in enumerate(((dq_ref, g0), (dk_ref, g0), (dv_ref, g1))):

        @pl.when((j >= 2 * at) & (j < 2 * at + 2))
        def _(src=src, near=near):
            spread(mm(nt_ref[...], src[...], NT).astype(BF), 0, gm, near, gf)

    @pl.when(j >= 6)
    def _():
        g_s[...] = mm(o_ref[...], dy_ref[...]).astype(BF)
        rows = [pl.multiple_of(ids[b], hr) for b in range(2 * blocks)]
        spread(jnp.concatenate([g_s[pl.ds(k, hr), :] for k in rows], 0), 0, gm, g1, gf)


def attn_grads(ids, nt, dy, ot, dq, dk, dv, hr, blocks):
    def grab(at):
        return pl.BlockSpec((TILE, T), lambda j, *_: (jnp.clip(j - 2 * at, 0, 1), 0))

    deep = lambda r: pl.BlockSpec((1, r, TILE), lambda j, *_: (j // 4, 0, j % 4))
    gspecs = [
        deep(D // 2),
        pl.BlockSpec((D // 4, TILE), lambda j, *_: (0, jnp.minimum(j, 3))),
        pl.BlockSpec((D // 4, TILE), lambda j, *_: (0, jnp.maximum(j - 4, 0))),
        deep(D // 4),
    ]
    return pl.pallas_call(
        functools.partial(agrad_kernel, hr, blocks),
        grid_spec=pltpu.PrefetchScalarGridSpec(
            num_scalar_prefetch=1,
            grid=(4 * D // TILE,),
            in_specs=[
                once((D, T)),
                pl.BlockSpec((T, TILE), lambda j, *_: (0, jnp.clip(j - 6, 0, 1))),
                once((D, T)),
                grab(0),
                grab(1),
                grab(2),
            ],
            out_specs=gspecs,
            scratch_shapes=[pltpu.VMEM((D, TILE), BF)],
        ),
        out_shape=grad_shapes(2 * D),
        compiler_params=params(),
        cost_estimate=cost(17),
    )(ids, nt, dy, ot, dq, dk, dv)


def final_kernel(np_, ids, x_ref, dy_ref, g_ref, bo_ref, o_ref, dq_ref, dk_ref, dv_ref, ao_ref, ag_ref, *refs):
    wq = refs[:np_]
    out_ref, gin_ref, v_ref, w_s = refs[np_:]
    i = pl.program_id(0)

    @pl.when(i == 0)
    def _():
        place(w_s, wq, ids, 1)

    x = x_ref[...].astype(F32)
    row = i * FT + lax.broadcasted_iota(jnp.int32, (FT, 1), 0)
    attn = mm(o_ref[...], w_s[:, 3 * D :], TN)
    out = x + attn + ao_ref[...].astype(F32) + bo_ref[...]
    out_ref[...] = jnp.where(row < ids[0], out, 0.0).astype(BF)
    dn = (
        ag_ref[...].astype(F32)
        + mm(w_s[:, :D], dq_ref[...])
        + mm(w_s[:, D : 2 * D], dk_ref[...])
        + mm(w_s[:, 2 * D : 3 * D], dv_ref[...])
    ).T
    mean = jnp.mean(x, -1, keepdims=True)
    xc = x - mean
    inv = lax.rsqrt(jnp.mean(xc * xc, -1, keepdims=True) + NORM_EPS)
    xh = xc * inv
    g = dn * g_ref[...]
    gx = dn * xh
    ln = inv * (
        g - jnp.mean(g, -1, keepdims=True) - xh * jnp.mean(g * xh, -1, keepdims=True)
    )
    gin_ref[...] = (dy_ref[...].astype(F32) + ln).astype(BF)

    @pl.when(i == 0)
    def _():
        v_ref[...] = jnp.zeros_like(v_ref)

    v_ref[0:1, :] += jnp.sum(gx, 0, keepdims=True)
    v_ref[1:2, :] += jnp.sum(dn, 0, keepdims=True)


def final(ids, x, dy, gain, b_out, ot, dq, dk, dv, acc_o, acc_g, weights, pieces):
    row = pl.BlockSpec((FT, D), lambda i, *_: (i, 0))
    col = pl.BlockSpec((D, FT), lambda i, *_: (0, i))
    vec = pl.BlockSpec((1, D), lambda i, *_: (0, 0))
    wargs = [weights, *pieces]
    return pl.pallas_call(
        functools.partial(final_kernel, len(wargs)),
        grid_spec=pltpu.PrefetchScalarGridSpec(
            num_scalar_prefetch=1,
            grid=(T // FT,),
            in_specs=[
                row,
                row,
                vec,
                vec,
                col,
                col,
                col,
                col,
                row,
                col,
                *[once((w.shape[0], 4 * D)) for w in wargs],
            ],
            out_specs=[row, row, pl.BlockSpec((8, D), lambda i, *_: (0, 0))],
            scratch_shapes=[pltpu.VMEM((D, 4 * D), BF)],
        ),
        out_shape=[
            jax.ShapeDtypeStruct((T, D), BF),
            jax.ShapeDtypeStruct((T, D), BF),
            jax.ShapeDtypeStruct((8, D), F32),
        ],
        compiler_params=params(),
        cost_estimate=cost(20),
    )(ids, x, dy, gain, b_out, ot, dq, dk, dv, acc_o, acc_g, *wargs)


C1 = float(1.0 - np.float32(B1) ** np.float32(STEP))
C2 = float(1.0 - np.float32(B2) ** np.float32(STEP))


def adam_math(g, m, v, w, decay):
    nm = B1 * m + (1.0 - B1) * g
    nv = B2 * v + (1.0 - B2) * g * g
    up = -LR * (nm / C1 / (jnp.sqrt(nv / C2) + ADAM_EPS) + decay * w)
    return nm, nv, up


def adam_kernel(n_alias, first, ids, sm, rm, so, ro, m_ref, v_ref, w_ref, *refs):
    wg_ref, nm_ref, nv_ref, up_ref, end_ref = refs[n_alias:]
    end_ref[...] = jnp.zeros_like(end_ref)
    summed = pl.program_id(0) + first == ids[1]
    hr = sm.shape[0]
    mine = jnp.where(summed, sm[...].astype(F32), rm[...].astype(F32))
    other = jnp.where(summed, so[...].astype(F32), ro[...].astype(F32))
    lead = ids[0] == 0
    for h, g in enumerate((jnp.where(lead, mine, other), jnp.where(lead, other, mine))):
        rows = slice(h * hr, (h + 1) * hr)
        nm, nv, up = adam_math(g, m_ref[rows, :], v_ref[rows, :], w_ref[rows, :].astype(F32), DECAY)
        wg_ref[rows, :] = g
        nm_ref[rows, :] = nm
        nv_ref[rows, :] = nv
        up_ref[rows, :] = up


def adam(ids, grads, cols, m, v, w, outs, first=0, count=2):
    rows, width = m.shape
    hr = rows // 2
    n = grads[0].shape[1]
    AC = 1024 if n % 1024 == 0 else 512
    pick = lambda hit: pl.BlockSpec(
        (hr, AC), lambda p, j, ids: (0, jnp.where((p + first == ids[1]) == hit, j, 0))
    )
    b0, b1 = cols[0] // AC, cols[1] // AC
    big = pl.BlockSpec((rows, AC), lambda p, j, ids: (0, jnp.where(p + first == 0, b0, b1) + j))
    alias = [] if outs is None else list(outs)
    return pl.pallas_call(
        functools.partial(adam_kernel, len(alias), first),
        grid_spec=pltpu.PrefetchScalarGridSpec(
            num_scalar_prefetch=1,
            grid=(count, n // AC),
            in_specs=[pick(True), pick(False), pick(True), pick(False), big, big, big]
            + [pl.BlockSpec(memory_space=pl.ANY)] * len(alias),
            out_specs=[big] * 4 + [pl.BlockSpec((8, 128), lambda p, j, ids: (0, 0))],
        ),
        out_shape=[jax.ShapeDtypeStruct((rows, width), F32)] * 4
        + [jax.ShapeDtypeStruct((8, 128), F32)],
        input_output_aliases={8 + i: i for i in range(len(alias))},
        compiler_params=pltpu.CompilerParams(
            dimension_semantics=("arbitrary", "arbitrary"), vmem_limit_bytes=VLIM
        ),
        cost_estimate=cost(6 * count * n / 2048),
    )(ids, *grads, m, v, w, *alias)


def after(values, *waits):
    flat = lax.optimization_barrier((*values, *waits))
    return list(flat[: len(values)])


def on_device(shards, reps, hidden_in, cotangent, lengths, weights, moment_m, moment_v, vectors, vector_m, vector_v):
    s = lax.axis_index("shard")
    rep = lax.axis_index("rep")
    c = rep % 2
    z = rep // 2
    zs = reps // 2
    swap = [(i, i ^ 1) for i in range(reps)]
    rows = weights.shape[0]
    hr = rows // 2
    i32 = jnp.int32
    cube = shards == 4 and zs & (zs - 1) == 0 and zs >= 4
    xn = [(i, i ^ 1) for i in range(shards)]
    yn = [(i, i ^ 2) for i in range(shards)]
    zsteps = [3] + [1 << k for k in range(2, 16) if 1 << k < zs]
    zn = lambda bit: [(i, i ^ (2 * bit)) for i in range(reps)]
    own = ((z ^ (z // 2)) % 2) if cube else jnp.int32(0)

    if cube:
        y_rows = [(s ^ r) * rows for r in (2, 3, 0, 1)]
    else:
        y_rows = [r * rows for r in range(shards)]
    cut = lambda at: [b + c * hr for b in at] + [b + (1 - c) * hr for b in at]
    y_off = cut(y_rows)
    stack = lambda *v: jnp.stack([jnp.asarray(x, i32) for x in v])
    length = lengths.astype(i32)
    gain = vectors[:D].reshape(1, D)
    shift = vectors[D : 2 * D].reshape(1, D)
    b_out = vectors[2 * D : 3 * D].reshape(1, D)
    b_in = vectors[3 * D :].reshape(1, FF)
    half_w = lax.dynamic_slice_in_dim(weights, c * hr, hr, 0)

    n, nt, dy, dyt, db_out = prep(
        stack(length[0], *y_off), hidden_in, cotangent, gain, shift, hr, shards
    )

    def part_of(cols):
        return jnp.concatenate([half_w[:, a:b] for a, b in cols], 1)

    q = hr // 2

    def gather_first(part):
        a, b = part[:q], part[q:]
        return [
            lax.ppermute(p, "shard", way) for p, way in ((a, xn), (b, yn), (b, xn), (a, yn))
        ]

    def gather_second(first):
        return [lax.ppermute(first[0], "shard", yn), lax.ppermute(first[1], "shard", xn)]

    def swapped(mine):
        return mine + [lax.ppermute(p, "rep", swap) for p in mine]

    def gather_whole(part):
        full = lax.all_gather(part, "shard", axis=0, tiled=True)
        other = lax.ppermute(full, "rep", swap)
        return [p[b * hr : (b + 1) * hr] for p in (full, other) for b in range(shards)]

    offsets = [0]
    for size in SIZES:
        offsets.append(offsets[-1] + size)
    apart, fpart = part_of([(0, 4 * D)]), part_of([(4 * D, 4 * D + 2 * FF)])
    if cube:
        base = [(s ^ r) * rows + e * q for r, e in ((1, 0), (2, 1), (1, 1), (2, 0), (3, 0), (3, 1))]
        offs = [b + c * hr for b in base] + [b + (1 - c) * hr for b in base]
        one = gather_first(apart)
        one[:2] = after(one[:2], n)
        one = one + gather_second(one)
        (fpart,) = after([fpart], *one)
        apieces = swapped(one)
        two = gather_first(fpart)
    else:
        offs = cut([b * rows for b in range(shards)])
        apieces = gather_whole(apart)
        two = gather_whole(fpart)
    piece_off = stack(s * rows, *offs)
    len_piece_off = stack(length[0], s * rows, *offs)

    add = lambda *v: sum(x.astype(F32) for x in v).astype(BF)

    class Reduce:
        def __init__(self, grads, split=False):
            self.split = split
            self.mine = grads[0]
            self.got = [lax.ppermute(g, "rep", swap) for g in grads[1:]]
            self.at = 0
            self.sums = None
            self.brought = []

        def settle(self, last):
            if self.brought:
                self.brought = after(self.brought, last)

        def step(self):
            self.at += 1
            k = self.at
            m, far, old = self.mine, self.got[2], self.brought
            if not cube:
                groups = [[2 * j + e for j in range(zs)] for e in range(2)]
                both = add(m, jnp.concatenate([jnp.stack(self.got[:2]), far], 1))
                both = lax.psum_scatter(both, "shard", scatter_dimension=1, tiled=True)
                both = lax.psum(both, "rep", axis_index_groups=groups)
                self.sums = (both[0], both[1])
                return [], []
            if self.split and k <= 3:
                return self.step_split(k)
            if k == 1:
                sent = add(m[:, : 2 * hr], jnp.stack(self.got[:2]))
                way = ("shard", yn)
            elif k == 2:
                self.first = old[0]
                sent = add(m[:, 3 * hr :], far[:, hr:], old[0][:, hr:])
                way = ("shard", xn)
            elif k == 3:
                total = add(m[:, 2 * hr : 3 * hr], far[:, :hr], self.first[:, :hr], old[0])
                lead = own == 0
                sent = jnp.where(lead, total[1], total[0])
                self.keep = jnp.where(lead, total[0], total[1])
                way = ("rep", zn(1))
            else:
                sent = self.keep = add(self.keep, old[0])
                last = k == 4 + len(zsteps)
                way = ("rep", zn(1 if last else zsteps[k - 4]))
            self.brought = [lax.ppermute(sent, *way)]
            if k == 4 + len(zsteps):
                self.sums = (self.keep, self.brought[0])
            return [sent], self.brought

        def step_split(self, k):
            m, old = self.mine, self.brought
            near, far = self.got[:2], self.got[2]
            b = [slice(i * hr, (i + 1) * hr) for i in range(4)]
            if k == 1:
                low = [add(m[0, b[3]], far[0, b[1]]), add(m[0, b[1]], near[0][b[1]])]
                sent = [jnp.concatenate(low, 0), add(m[1, : 2 * hr], near[1])]
                ways = xn, yn
            elif k == 2:
                self.first = old
                sent = [
                    add(m[0, b[0]], near[0][b[0]], old[0][b[1]]),
                    add(m[1, b[3]], far[1, b[1]], old[1][b[1]]),
                ]
                ways = yn, xn
            else:
                total = [
                    add(m[e, b[2]], far[e, b[0]], self.first[e][b[0]], old[e]) for e in range(2)
                ]
                lead = own == 0
                sent = [jnp.where(lead, total[1], total[0])]
                self.keep = jnp.where(lead, total[0], total[1])
                self.brought = [lax.ppermute(sent[0], "rep", zn(1))]
                return sent, self.brought
            self.brought = [lax.ppermute(v, "shard", w) for v, w in zip(sent, ways)]
            return sent, self.brought

        def result(self, *waits):
            while self.sums is None:
                self.step()
            sums = after(list(self.sums), *waits)
            return [*sums, *[lax.ppermute(v, "rep", swap) for v in sums]]

    flight = []

    def turn(values, last, *steps):
        nonlocal flight
        waits = flight
        flight = []
        for red in steps:
            if red.sums is None:
                red.settle(last)
                moved = red.step()
                waits = waits + moved[0]
                flight = flight + moved[1]
        return after(values, *waits) if waits else list(values)

    inv_freq = jnp.power(F32(10000.0), -jnp.arange(0, ROT, 2, dtype=F32) / ROT)
    angles = inv_freq[:, None] * jnp.arange(T, dtype=F32)[None, :]
    cos, sin = jnp.cos(angles), jnp.sin(angles)
    qkv, dot_ = proj(piece_off, n, dy, cos, sin, weights, apieces)
    half = HEADS // 2
    heads = attend(length, qkv, dot_, cos, sin, 0, half, None)
    if cube:
        *two, qkv = after([*two, qkv], heads[0])
        three = gather_second(two)
        across = [lax.ppermute(v, "rep", swap) for v in two[:2]]
    ot, dq, dk, dv = attend(length, qkv, dot_, cos, sin, half, half, heads)
    dyg = dy
    if cube:
        (dyg,) = after([dy], ot, *three, *across)
        rest = after(two[2:] + three, ot)
        across += [lax.ppermute(v, "rep", swap) for v in rest]
        fpieces = two + three + across
    else:
        fpieces = two
    grads = attn_grads(stack(*y_off), nt, dyg, ot, dq, dk, dv, hr, shards)
    if cube:
        grads = after(grads, *across[2:])
    reds = [Reduce(grads, True)]
    places = [(0, 2 * D)]
    acc = None
    dbs = []
    nk = n
    for at, size in zip(offsets, SIZES):
        (nk,) = turn([nk], dbs[-1] if dbs else dv, *reds)
        *grads, db_in, acc_o, acc_g = mlp(
            piece_off, nk, nt, dy, dyt, b_in, weights, fpieces, at, size, acc
        )
        acc = (acc_o, acc_g)
        dbs.append(db_in)
        reds.append(Reduce(grads))
        places.append((4 * D + at, 4 * D + FF + at))

    (ot,) = turn([ot], dbs[-1], *reds)
    (ot,) = after([ot], reds[-1].got[2])
    out, grad_in, vsum = final(
        len_piece_off, hidden_in, dy, gain, b_out, ot, dq, dk, dv, *acc, weights, apieces
    )
    core = stack(c, own)
    def push(last, steps, loose):
        waits = []
        for red in steps + loose:
            if red.sums is None:
                red.settle(last)
                sent = red.step()[0]
                waits = waits + (sent if red in steps else [])
        return after([core], *waits)[0] if waits else core

    args = moment_m, moment_v, weights
    vec = jnp.concatenate([vsum[0], vsum[1], db_out[0], *[d[0] for d in dbs]])
    if cube:
        vec = vec.reshape(-1, 128)
        hops = [("rep", swap), ("shard", xn), ("shard", yn)]
        hops += [("rep", zn(bit)) for bit in [1] + zsteps]
    else:
        vec = lax.psum(vec, ("rep", "shard"))
        hops = []

    def hop(last, count=1):
        nonlocal vec
        for _ in range(count):
            if hops:
                (vec,) = after([vec], last)
                vec = vec + lax.ppermute(vec, *hops.pop(0))

    big, end = None, vsum
    for i, (red, place_) in enumerate(zip(reds, places)):
        hop(end)
        near = i + 2
        ids = push(end, reds[i:near], reds[near:])
        *big, end = adam(ids, red.result(*([] if i else [vsum])), place_, *args, big)
    while hops:
        hop(end)
    vec = vec.reshape(-1)
    vm, vv, vu = adam_math(vec, vector_m, vector_v, vectors, 0.0)
    return (out, grad_in, *big, vec, vm, vv, vu)


def solution(mesh):
    tok = P(("rep", "shard"), None)
    w = P("shard", None)
    return jax.shard_map(
        functools.partial(on_device, mesh.shape["shard"], mesh.shape["rep"]),
        mesh=mesh,
        in_specs=(tok, tok, P(("rep", "shard")), w, w, w, P(), P(), P()),
        out_specs=(tok, tok, w, w, w, w, P(), P(), P(), P()),
        check_vma=False,
    )
```
